256 devices in a mesh: dp: 64 (over z, y_hi, x), hist: 4 (over y_lo, core).
Axes of the slice: x: 4, y: 4 (y_hi: 2, y_lo: 2; y = y_hi * 2 + y_lo), z: 8, core: 2. Of those that a mesh axis runs over, the one named last changes fastest.
Arguments:
- tokens: bfloat16 [64, 512, 512], P('dp', 'hist'), may hold values from -6 to 6
- targets: bfloat16 [64, 512, 512], P('dp', 'hist'), may hold values from -6 to 6
- target_ids: int32 [64, 512], P('dp', 'hist'), may hold values from 0 to 4095
- lengths: int32 [64], P('dp'), may hold values from 64 to 512
- negatives: bfloat16 [2048, 512], P('dp'), may hold values from -6 to 6
- negative_ids: int32 [2048], P('dp'), may hold values from 0 to 4095
- negative_counts: int32 [2048], P('dp'), may hold values from 1 to 64
- w_in: bfloat16 [512, 2048], replicated, may hold values from -0.25 to 0.25
- w_out: bfloat16 [512, 512], replicated, may hold values from -0.25 to 0.25
Outputs:
- loss: float32 [], replicated
- d_tokens: bfloat16 [64, 512, 512], P('dp', 'hist')
- d_targets: bfloat16 [64, 512, 512], P('dp', 'hist')
- d_w_in: float32 [512, 2048], P('dp')
- d_w_out: float32 [512, 512], P('dp')
- d_negatives: float32 [2048, 512], P('dp')
The draws below stay inside these ranges and needn't reach their ends.
All inputs are finite; a program needn't handle non-finite values.
Results may differ from the reference program's by a relative error of at most 0.018.
Values may be sent and summed in bfloat16 or wider, within the bound.
A program may use at most 64 MiB of HBM per device.

```python
import jax
import jax.numpy as jnp
from jax import lax

D = 512
HEADS = 8
L = 512
HISTS = 64
TOKENS = 32768
NEG = 2048
ITEM_IDS = 4096


def touch_ends(values, own_key, least, largest):
    index_at = [jax.random.randint(jax.random.fold_in(own_key, axis), (), 0, length) for axis, length in enumerate(values.shape)]
    widest = values.shape.index(max(values.shape))
    neighbour = index_at[:widest] + [(index_at[widest] + 1) % values.shape[widest]] + index_at[widest + 1:]
    return values.at[tuple(index_at)].set(least).at[tuple(neighbour)].set(largest)


def levels(stream_key, extent, pieces, least, largest):
    factor_of, own = 1.0, jax.random.fold_in(stream_key, 6)
    for dim, shards_of in pieces:
        draws = jnp.exp(jax.random.uniform(jax.random.fold_in(own, dim), (shards_of,), jnp.float32, least / len(pieces), largest / len(pieces)))
        factor_of = factor_of * jnp.repeat(draws, extent[dim] // shards_of).reshape([-1 if axis == dim else 1 for axis in range(len(extent))])
    return factor_of


def noise(rng, dims, scale, reach, split=(), held_as=jnp.bfloat16):
    drawn = scale * jax.random.normal(rng, dims, jnp.float32)
    if split:
        drawn = drawn * levels(rng, dims, split, -0.22, 0.18)
    return jnp.clip(drawn, -reach, reach).astype(held_as)


def setup_inputs(seed: int = 0) -> dict:
    key_list = jax.random.split(jax.random.key(seed), 10)
    return {
        "tokens": noise(key_list[0], (HISTS, L, D), 1.0, 6.0, ((0, 64), (1, 4))),
        "targets": noise(key_list[1], (HISTS, L, D), 1.0, 6.0, ((0, 64), (1, 4))),
        "target_ids": touch_ends(jax.random.randint(key_list[2], (HISTS, L), 0, ITEM_IDS), jax.random.fold_in(key_list[2], 1), 0, ITEM_IDS - 1).astype(jnp.int32),
        "lengths": touch_ends(jax.random.randint(key_list[3], (HISTS,), L // 8, L + 1), jax.random.fold_in(key_list[3], 1), L // 8, L).astype(jnp.int32),
        "negatives": noise(key_list[4], (NEG, D), 1.0, 6.0, ((0, 64),)),
        "negative_ids": touch_ends(jax.random.randint(key_list[5], (NEG,), 0, ITEM_IDS), jax.random.fold_in(key_list[5], 1), 0, ITEM_IDS - 1).astype(jnp.int32),
        "negative_counts": touch_ends(jax.random.randint(key_list[6], (NEG,), 1, 65), jax.random.fold_in(key_list[6], 1), 1, 64).astype(jnp.int32),
        "w_in": noise(key_list[7], (D, 4 * D), D ** -0.5, 0.25),
        "w_out": noise(key_list[8], (D, D), D ** -0.5, 0.25),
    }


SOFTMAX_TEMP = 0.05

def layer_norm(values):
    centered = values - lax.optimization_barrier(jnp.mean(values, -1, keepdims=True))
    inverse = lax.rsqrt(lax.optimization_barrier(jnp.mean(centered * centered, -1, keepdims=True)) + 1e-06)
    return (centered * inverse, inverse)

def norm_back(grad, normed, inverse):
    return inverse * (grad - lax.optimization_barrier(jnp.mean(grad, -1, keepdims=True)) - normed * lax.optimization_barrier(jnp.mean(grad * normed, -1, keepdims=True)))

def unit_rows(values):
    inverse = lax.rsqrt(lax.optimization_barrier(jnp.sum(values * values, -1, keepdims=True)) + 1e-06)
    return (values * inverse, inverse)

def unit_back(grad, unit, inverse):
    return inverse * (grad - unit * lax.optimization_barrier(jnp.sum(unit * grad, -1, keepdims=True)))

def silu_slope(values):
    sigma = jax.nn.sigmoid(values)
    return sigma * (1.0 + values * (1.0 - sigma))

def inner_product(left, right):
    return lax.dot_general(left, right, (((1,), (1,)), ((), ())), preferred_element_type=jnp.float32)

def outer_sum(left, right):
    return lax.dot_general(left, right, (((0,), (0,)), ((), ())), preferred_element_type=jnp.float32)

def causal_mask(scores, q_start):
    rows = q_start + lax.broadcasted_iota(jnp.int32, scores.shape, 0)
    cols = lax.broadcasted_iota(jnp.int32, scores.shape, 1)
    return cols <= rows

def head_forward(query, key, value, q_start, span):
    scale = query.shape[1] ** (-0.5)
    scores = inner_product(query, key) * scale
    weights = jnp.where(causal_mask(scores, q_start), jax.nn.silu(scores) / span, 0.0).astype(jnp.bfloat16)
    return jnp.dot(weights, value, preferred_element_type=jnp.float32)

def head_backward(query, key, value, d_attn, q_start, span):
    scale = query.shape[1] ** (-0.5)
    scores = inner_product(query, key) * scale
    causal = causal_mask(scores, q_start)
    weights = jnp.where(causal, jax.nn.silu(scores) / span, 0.0).astype(jnp.bfloat16)
    d_weights = inner_product(d_attn, value)
    d_score = jnp.where(causal, d_weights * silu_slope(scores) * (scale / span), 0.0).astype(jnp.bfloat16)
    d_query = jnp.dot(d_score, key, preferred_element_type=jnp.float32)
    d_key = outer_sum(d_score, query)
    d_value = outer_sum(weights, d_attn)
    return (d_query, d_key, d_value)

def split_heads(values, head_dim):
    return values.reshape(values.shape[0], -1, head_dim).transpose(1, 0, 2)

def join_heads(values):
    return values.transpose(1, 0, 2).reshape(values.shape[1], -1)

def attend(query, key, value, q_start, span, head_dim):
    rows = query.shape[0]
    block = min(rows, 512)
    count = rows // block
    q_heads = split_heads(query, head_dim).reshape(-1, count, block, head_dim)
    k_heads = split_heads(key, head_dim)
    v_heads = split_heads(value, head_dim)
    offsets = q_start + block * jnp.arange(count, dtype=jnp.int32)

    def one_head(items):
        q_blocks, k_one, v_one = items
        return lax.map(lambda pair: head_forward(pair[0], k_one, v_one, pair[1], span), (q_blocks, offsets))
    result = lax.map(one_head, (q_heads, k_heads, v_heads))
    return join_heads(result.reshape(result.shape[0], rows, head_dim))

def attend_back(query, key, value, d_attn, q_start, span, head_dim):
    rows = query.shape[0]
    block = min(rows, 512)
    count = rows // block
    q_heads = split_heads(query, head_dim).reshape(-1, count, block, head_dim)
    d_heads = split_heads(d_attn, head_dim).reshape(-1, count, block, head_dim)
    k_heads = split_heads(key, head_dim)
    v_heads = split_heads(value, head_dim)
    offsets = q_start + block * jnp.arange(count, dtype=jnp.int32)

    def one_head(items):
        q_blocks, k_one, v_one, d_blocks = items

        def step(carry, piece):
            d_query, d_key, d_value = head_backward(piece[0], k_one, v_one, piece[1], piece[2], span)
            return ((carry[0] + d_key, carry[1] + d_value), d_query)
        empty = jnp.zeros(k_one.shape, jnp.float32)
        sums, d_query = lax.scan(step, (empty, empty), (q_blocks, d_blocks, offsets))
        return (d_query, sums[0], sums[1])
    d_query, d_key, d_value = lax.map(one_head, (q_heads, k_heads, v_heads, d_heads))
    return (join_heads(d_query.reshape(d_query.shape[0], rows, head_dim)), join_heads(d_key), join_heads(d_value))

def sampled_softmax(output, targets, target_ids, valid, normalized_negative_batch, neg_ids, log_item_frequency):
    normalized_output, y_inv = unit_rows(output)
    normalized_output_batch = normalized_output.astype(jnp.bfloat16)
    normalized_target, t_inv = unit_rows(targets.astype(jnp.float32))
    positive_logits = lax.optimization_barrier(jnp.sum(normalized_output * normalized_target, -1)) / SOFTMAX_TEMP
    negative_logits = inner_product(normalized_output_batch, normalized_negative_batch) / SOFTMAX_TEMP - log_item_frequency[None, :]
    keep = target_ids[:, None] != neg_ids[None, :]
    positive_exponent = jnp.exp(positive_logits)
    negative_exponent = jnp.where(keep, jnp.exp(negative_logits), 0.0)
    partition_sum = positive_exponent + lax.optimization_barrier(jnp.sum(negative_exponent, -1))
    token_weight = valid.astype(jnp.float32)
    loss_sum = jnp.sum(token_weight * (jnp.log(partition_sum) - positive_logits))
    positive_gradient = token_weight * (positive_exponent / partition_sum - 1.0) / SOFTMAX_TEMP
    negative_gradient = (negative_exponent * (token_weight / (partition_sum * SOFTMAX_TEMP))[:, None]).astype(jnp.bfloat16)
    d_hat = positive_gradient[:, None] * normalized_target + jnp.dot(negative_gradient, normalized_negative_batch, preferred_element_type=jnp.float32)
    d_output = unit_back(d_hat, normalized_output, y_inv)
    d_targets = unit_back(positive_gradient[:, None] * normalized_output, normalized_target, t_inv)
    return (loss_sum, normalized_output_batch, negative_gradient, d_output, d_targets)

def reference(tokens, targets, target_ids, lengths, negatives, negative_ids, negative_counts, w_in, w_out):
    width = D
    head_dim = D // HEADS
    span = float(L)
    n_hat, n_inv = unit_rows(negatives.astype(jnp.float32))
    normalized_negative_batch = n_hat.astype(jnp.bfloat16)
    log_item_frequency = jnp.log(negative_counts.astype(jnp.float32))
    positions = jnp.arange(L, dtype=jnp.int32)

    def one_history(carry, items):
        tok, tgt, ids, length = items
        normed_f, inverse = layer_norm(tok.astype(jnp.float32))
        normed = normed_f.astype(jnp.bfloat16)
        proj = jnp.dot(normed, w_in, preferred_element_type=jnp.float32)
        act = jax.nn.silu(proj).astype(jnp.bfloat16)
        gate_u = act[:, :width]
        value = act[:, width:2 * width]
        query = act[:, 2 * width:3 * width]
        key = act[:, 3 * width:]
        attn = attend(query, key, value, 0, span, head_dim).astype(jnp.bfloat16)
        attn_normed, attn_inv = layer_norm(attn.astype(jnp.float32))
        gate_f = gate_u.astype(jnp.float32)
        mixed = (attn_normed * gate_f).astype(jnp.bfloat16)
        output = tok.astype(jnp.float32) + jnp.dot(mixed, w_out, preferred_element_type=jnp.float32)
        valid = positions < length
        loss_sum, normalized_output_batch, negative_gradient, d_output, d_targets = sampled_softmax(output, tgt, ids, valid, normalized_negative_batch, negative_ids, log_item_frequency)
        d_out_b = d_output.astype(jnp.bfloat16)
        d_mixed = inner_product(d_out_b, w_out)
        d_gate = d_mixed * attn_normed
        d_attn = norm_back(d_mixed * gate_f, attn_normed, attn_inv).astype(jnp.bfloat16)
        d_query, d_key, d_value = attend_back(query, key, value, d_attn, 0, span, head_dim)
        d_act = jnp.concatenate([d_gate, d_value.astype(jnp.bfloat16).astype(jnp.float32), d_query.astype(jnp.bfloat16).astype(jnp.float32), d_key.astype(jnp.bfloat16).astype(jnp.float32)], 1)
        d_proj = (d_act * silu_slope(proj)).astype(jnp.bfloat16)
        d_tokens = (d_output + norm_back(inner_product(d_proj, w_in), normed_f, inverse)).astype(jnp.bfloat16)
        carry = (carry[0] + outer_sum(normed, d_proj), carry[1] + outer_sum(mixed, d_out_b), carry[2] + outer_sum(negative_gradient, normalized_output_batch), carry[3] + loss_sum)
        return (carry, (d_tokens, d_targets.astype(jnp.bfloat16)))
    start = (jnp.zeros((D, 4 * D), jnp.float32), jnp.zeros((D, D), jnp.float32), jnp.zeros((NEG, D), jnp.float32), jnp.zeros((), jnp.float32))
    sums, outs = lax.scan(one_history, start, (tokens, targets, target_ids, lengths))
    partition_sum = float(TOKENS)
    return (sums[3] / partition_sum, outs[0], outs[1], sums[0] / partition_sum, sums[1] / partition_sum, unit_back(sums[2], n_hat, n_inv) / partition_sum)
```

```python
import functools

import jax
import jax.numpy as jnp
from jax import lax
from jax.experimental import pallas as pl
from jax.experimental.pallas import tpu as pltpu
from jax.sharding import PartitionSpec as P

HEADS = 8
L = 512
W = 512
HIST = 4
R = 128
NB = 32
NQ = NB // HIST
TEMP = 0.05
MESH = pl.DeviceIdType.MESH
F32 = jnp.float32
BF16 = jnp.bfloat16


def layer_norm(values):
    centered = values - jnp.mean(values, -1, keepdims=True)
    inverse = lax.rsqrt(jnp.mean(centered * centered, -1, keepdims=True) + 1e-06)
    return (centered * inverse, inverse)


def norm_back(grad, normed, inverse):
    return inverse * (
        grad
        - jnp.mean(grad, -1, keepdims=True)
        - normed * jnp.mean(grad * normed, -1, keepdims=True)
    )


def unit_rows(values):
    inverse = lax.rsqrt(jnp.sum(values * values, -1, keepdims=True) + 1e-06)
    return (values * inverse, inverse)


def unit_back(grad, unit, inverse):
    return inverse * (grad - unit * jnp.sum(unit * grad, -1, keepdims=True))


def sigmoid(values):
    return 0.5 * jnp.tanh(0.5 * values) + 0.5


def silu_slope(values):
    sigma = sigmoid(values)
    return sigma * (1.0 + values * (1.0 - sigma))


def silu(values):
    return values * sigmoid(values)


def inner_product(left, right):
    return lax.dot_general(left, right, (((1,), (1,)), ((), ())), preferred_element_type=F32)


def matmul(left, right):
    return jnp.dot(left, right, preferred_element_type=F32)


def plan(mesh):
    dp = mesh.shape["dp"]
    if dp == 64:
        return 8, 2, 4
    return 2, 1, dp // 2


def kernel(
    sizes,
    count,
    tok_ref,
    tgt_ref,
    tid_ref,
    len_ref,
    neg_ref,
    nid_ref,
    ncnt_ref,
    win_ref,
    wout_ref,
    loss_ref,
    dtok_ref,
    dtgt_ref,
    dwin_ref,
    dwout_ref,
    dneg_ref,
    tok_all,
    nrm_all,
    nrmf,
    proj,
    gate,
    k_all,
    v_all,
    q_all,
    slope,
    attn,
    nall,
    idz,
    idp,
    idb,
    lcb,
    ex,
    ngo,
    ngs,
    nga,
    my_all,
    da_all,
    dps,
    dpa,
    dpo,
    dout,
    rsa_s,
    rsa_r,
    za_s,
    za_r,
    ea,
    rsb_s,
    rsb_r,
    zb_s,
    zb_r,
    eb,
    l1,
    l2,
    l3,
    ssem,
    rsem,
):
    nz, nyh, nx = sizes
    npl = nyh * nx
    dp_size = nz * npl
    rw = W // dp_size
    total_events = float(dp_size * L)
    d = lax.axis_index("dp")
    h = lax.axis_index("hist")
    z = lax.div(d, npl)
    p = lax.rem(d, npl)
    yh = lax.div(p, nx)
    x = lax.rem(p, nx)
    core = lax.rem(h, 2)
    sib = h + 1 - 2 * core

    def hist_to(o):
        return lax.rem(h + o, HIST)

    def hist_from(o):
        return lax.rem(h + HIST - o, HIST)

    def z_to(o):
        return lax.rem(z + o, nz)

    def z_from(o):
        return lax.rem(z + nz - o, nz)

    offsets = [(a, b) for a in range(nyh) for b in range(nx) if (a, b) != (0, 0)]

    def p_to(ab):
        return lax.rem(yh + ab[0], nyh) * nx + lax.rem(x + ab[1], nx)

    def p_from(ab):
        return lax.rem(yh + nyh - ab[0], nyh) * nx + lax.rem(x + nx - ab[1], nx)

    def hist_dev(index):
        return {"dp": d, "hist": index}

    def z_dev(index):
        return {"dp": index * npl + p, "hist": h}

    def p_dev(index):
        return {"dp": z * npl + index, "hist": h}

    sends = []
    taken = [0]

    def slots(number):
        base = taken[0]
        taken[0] += number
        assert taken[0] <= count
        return base

    def send(src, dst, slot, device):
        copy = pltpu.make_async_remote_copy(
            src_ref=src,
            dst_ref=dst,
            send_sem=ssem.at[slot],
            recv_sem=rsem.at[slot],
            device_id=device,
            device_id_type=MESH,
        )
        copy.start()
        sends.append(copy)

    def recv(dst, slot):
        pltpu.make_async_remote_copy(
            src_ref=dst,
            dst_ref=dst,
            send_sem=ssem.at[slot],
            recv_sem=rsem.at[slot],
            device_id=hist_dev(sib),
            device_id_type=MESH,
        ).wait_recv()

    barrier = pltpu.get_barrier_semaphore()
    peers = (
        [hist_dev(hist_to(o)) for o in range(1, HIST)]
        + [p_dev(p_to(ab)) for ab in offsets]
        + [z_dev(z_to(o)) for o in range(1, nz)]
    )
    for device in peers:
        pl.semaphore_signal(barrier, inc=1, device_id=device, device_id_type=MESH)

    n_hat, n_inv = unit_rows(neg_ref[...].astype(F32))
    n_hat_b = n_hat.astype(BF16)
    nall[core, p, z] = jnp.where(core == 0, n_hat_b[:, :256], n_hat_b[:, 256:])
    row_at = lax.broadcasted_iota(jnp.int32, (8, 128), 0)
    lane_at = lax.broadcasted_iota(jnp.int32, (8, 128), 1)
    own_place = (row_at == z) & (lane_at >= x * NB) & (lane_at < x * NB + NB)
    for kind, ref in enumerate((nid_ref, ncnt_ref)):
        wide = jnp.concatenate([ref[...]] * (128 // NB), axis=1)
        idz[z, kind * 8 : kind * 8 + 8] = jnp.where(own_place, wide, 0)

    pl.semaphore_wait(barrier, len(peers))

    s_tok = slots(HIST)
    for o in range(1, HIST):
        send(tok_ref, tok_all.at[h], s_tok + o, hist_dev(hist_to(o)))
    s_nz = slots(nz)
    s_iz = slots(nz)
    for o in range(1, nz):
        send(nall.at[core, p, z], nall.at[core, p, z], s_nz + o, z_dev(z_to(o)))
        send(idz.at[z], idz.at[z], s_iz + o, z_dev(z_to(o)))

    tokf = tok_ref[...].astype(F32)
    normed_f, inverse = layer_norm(tokf)
    nrmf[...] = normed_f
    normed = normed_f.astype(BF16)
    nrm_all[h] = normed
    for blk, ref in enumerate((gate, v_all.at[h], q_all.at[h], k_all.at[h])):
        cols = slice(blk * W, (blk + 1) * W)
        part = matmul(normed, win_ref[:, cols])
        proj[:, cols] = part
        ref[...] = silu(part).astype(BF16)

    for o in range(1, nz):
        recv(nall.at[core, p, z_from(o)], s_nz + o)
        recv(idz.at[z_from(o)], s_iz + o)
    tile = idz[0]
    for k in range(1, nz):
        tile = tile + idz[k]
    idp[p] = tile
    s_np = slots(npl)
    s_ip = slots(npl)
    for k, ab in enumerate(offsets):
        send(nall.at[core, p], nall.at[core, p], s_np + k, p_dev(p_to(ab)))
        send(idp.at[p], idp.at[p], s_ip + k, p_dev(p_to(ab)))
    s_sib = slots(npl)
    send(nall.at[core, p], nall.at[core, p], s_sib + npl - 1, hist_dev(sib))

    for o in range(1, HIST):
        b = hist_from(o)
        recv(tok_all.at[b], s_tok + o)
        other = layer_norm(tok_all[b].astype(F32))[0].astype(BF16)
        nrm_all[b] = other
        v_all[b] = silu(matmul(other, win_ref[:, W : 2 * W])).astype(BF16)
        k_all[b] = silu(matmul(other, win_ref[:, 3 * W :])).astype(BF16)

    lane = lax.broadcasted_iota(jnp.int32, (1, 128), 1)
    low = lane < 64
    half_mask = [jnp.where(low, 1.0, 0.0).astype(BF16), jnp.where(low, 0.0, 1.0).astype(BF16)]
    causal = lax.broadcasted_iota(jnp.int32, (R, L), 1) <= h * R + lax.broadcasted_iota(
        jnp.int32, (R, L), 0
    )
    scale = 0.125

    def forward_pair(n, carry):
        cols = pl.ds(pl.multiple_of(n * 128, 128), 128)
        q = q_all[h, :, cols]
        k = k_all[:, :, cols].reshape(L, 128)
        v = v_all[:, :, cols].reshape(L, 128)
        halves = []
        for e in range(2):
            s = inner_product(q * half_mask[e], k) * scale
            sigma = sigmoid(s)
            w = jnp.where(causal, s * sigma * (1.0 / L), 0.0).astype(BF16)
            slope[2 * n + e] = jnp.where(
                causal, sigma * (1.0 + s * (1.0 - sigma)) * (scale / L), 0.0
            )
            halves.append(matmul(w, v))
        attn[:, cols] = jnp.where(low, halves[0], halves[1]).astype(BF16)
        return carry

    lax.fori_loop(0, HEADS // 2, forward_pair, 0)

    attn_normed, attn_inv = layer_norm(attn[...].astype(F32))
    gate_f = gate[...].astype(F32)
    mixed = (attn_normed * gate_f).astype(BF16)
    my_all[h, :, :W] = mixed
    output = tok_ref[...].astype(F32) + matmul(mixed, wout_ref[...])
    y_hat, y_inv = unit_rows(output)
    y_hat_b = y_hat.astype(BF16)
    my_all[h, :, W:] = y_hat_b
    s_my = slots(HIST)
    for o in range(1, HIST):
        send(my_all.at[h], my_all.at[h], s_my + o, hist_dev(hist_to(o)))
    t_hat, t_inv = unit_rows(tgt_ref[...].astype(F32))
    pos_col = jnp.sum(y_hat * t_hat, -1, keepdims=True) / TEMP
    pos_row = jnp.broadcast_to(pos_col, (R, 128)).T[0:1, :]

    for k, ab in enumerate(offsets):
        src = p_from(ab)
        recv(nall.at[core, src], s_np + k)
        recv(idp.at[src], s_ip + k)
        send(nall.at[core, src], nall.at[core, src], s_sib + k, hist_dev(sib))
    for a in range(nyh):
        both = idp[a * nx]
        for b in range(1, nx):
            both = both + idp[a * nx + b]
        ids = both[:8].astype(F32)
        logs = jnp.log(jnp.maximum(both[8:].astype(F32), 1.0))
        turned = jnp.concatenate([ids, logs, jnp.zeros((112, 128), F32)], axis=0).T
        for b in range(nx):
            rows = turned[b * NB : (b + 1) * NB]
            for k in range(nz):
                at = pl.ds(k * NB, NB)
                idb[a * nx + b, at] = jnp.broadcast_to(rows[:, k : k + 1], (NB, 128))
                lcb[a * nx + b, at] = jnp.broadcast_to(rows[:, 8 + k : 9 + k], (NB, 128))
    other_core = 1 - core
    recv(nall.at[other_core, p], s_sib + npl - 1)
    for k, ab in enumerate(offsets):
        recv(nall.at[other_core, p_from(ab)], s_sib + k)

    tid_row = tid_ref[...].astype(F32)

    def logits_chunk(c, acc):
        lg = inner_product(nall[0, c].reshape(nz * NB, 256), y_hat_b[:, :256]) + inner_product(
            nall[1, c].reshape(nz * NB, 256), y_hat_b[:, 256:]
        )
        lg = lg * (1.0 / TEMP) - lcb[c]
        value = jnp.where(idb[c] != tid_row, jnp.exp(lg), 0.0)
        ex[c] = value
        return acc + jnp.sum(value.reshape(nz * NB // 8, 8, 128), 0)

    acc = lax.fori_loop(0, npl, logits_chunk, jnp.zeros((8, 128), F32))
    total = jnp.exp(pos_row) + jnp.sum(acc, 0, keepdims=True)
    position = h * R + lax.broadcasted_iota(jnp.int32, (1, 128), 1)
    valid = jnp.where(position < len_ref[...], 1.0, 0.0)
    loss = jnp.sum(valid * (jnp.log(total) - pos_row), -1, keepdims=True)
    l1[p] = jnp.broadcast_to(loss, (8, 128))
    s_l1 = slots(npl)
    for k, ab in enumerate(offsets):
        send(l1.at[p], l1.at[p], s_l1 + k, p_dev(p_to(ab)))
    pg_row = valid * (jnp.exp(pos_row) / total - 1.0) / TEMP
    pg = jnp.broadcast_to(pg_row, (128, 128)).T[:, 0:1]
    scale_row = valid / (total * TEMP)

    def grad_chunk(c, carry):
        g = ex[c] * scale_row
        ngo[c] = g.astype(BF16)
        g4 = g.reshape(nz, HIST, NQ, 128)
        for q in range(HIST):
            ngs[q, c] = g4[:, q].reshape(nz * NQ, 128).astype(BF16)
        return carry

    lax.fori_loop(0, npl, grad_chunk, 0)
    ng = ngo[...].reshape(dp_size * NB, 128).T
    d_hat = pg * t_hat + jnp.concatenate(
        [matmul(ng, nall[c].reshape(dp_size * NB, 256)) for c in range(2)], axis=1
    )
    d_out = unit_back(d_hat, y_hat, y_inv)
    dout[...] = d_out
    dtgt_ref[...] = unit_back(pg * y_hat, t_hat, t_inv).astype(BF16)
    d_out_b = d_out.astype(BF16)
    d_mixed = inner_product(d_out_b, wout_ref[...])
    da_all[h] = norm_back(d_mixed * gate_f, attn_normed, attn_inv).astype(BF16)
    s_da = slots(HIST)
    for o in range(1, HIST):
        send(da_all.at[h], da_all.at[h], s_da + o, hist_dev(hist_to(o)))
    d_gate = (d_mixed * attn_normed * silu_slope(proj[:, :W])).astype(BF16)
    dpo[:, :W] = d_gate
    for n in range(HIST):
        cols = slice(n * 128, (n + 1) * 128)
        dps[n, :, 0:128] = d_out_b[:, cols]
        dps[n, :, 128:256] = d_gate[:, cols]
    s_dg = slots(HIST)
    s_ng = slots(HIST)
    for o in range(1, HIST):
        to = hist_to(o)
        send(dps.at[to, :, pl.ds(0, 256)], dpa.at[h, :, pl.ds(0, 256)], s_dg + o, hist_dev(to))
    for o in range(1, HIST):
        to = hist_to(o)
        send(ngs.at[to], nga.at[h], s_ng + o, hist_dev(to))
    nga[h] = ngs[h]

    for k, ab in enumerate(offsets):
        recv(l1.at[p_from(ab)], s_l1 + k)
    part = l1[0]
    for k in range(1, npl):
        part = part + l1[k]
    l2[z] = part
    s_l2 = slots(nz)
    for o in range(1, nz):
        send(l2.at[z], l2.at[z], s_l2 + o, z_dev(z_to(o)))

    def query_pair(n, carry):
        cols = pl.ds(pl.multiple_of(n * 128, 128), 128)
        da = da_all[h, :, cols]
        k = k_all[:, :, cols].reshape(L, 128)
        v = v_all[:, :, cols].reshape(L, 128)
        halves = []
        for e in range(2):
            dw = inner_product(da * half_mask[e], v)
            halves.append(matmul((dw * slope[2 * n + e]).astype(BF16), k))
        dq = jnp.where(low, halves[0], halves[1]).astype(BF16).astype(F32)
        at = pl.ds(pl.multiple_of(2 * W + n * 128, 128), 128)
        piece = (dq * silu_slope(proj[:, at])).astype(BF16)
        dpo[:, at] = piece
        dps[n, :, 384:512] = piece
        return carry

    lax.fori_loop(0, HEADS // 2, query_pair, 0)
    for o in range(1, HIST):
        b = hist_from(o)
        q_all[b] = silu(matmul(nrm_all[b], win_ref[:, 2 * W : 3 * W])).astype(BF16)
    for o in range(1, HIST):
        recv(da_all.at[hist_from(o)], s_da + o)

    causal_t = lax.broadcasted_iota(jnp.int32, (R, L), 1) >= h * R + lax.broadcasted_iota(
        jnp.int32, (R, L), 0
    )

    def key_pair(n):
        cols = pl.ds(pl.multiple_of(n * 128, 128), 128)
        k = k_all[h, :, cols]
        v = v_all[h, :, cols]
        q = q_all[:, :, cols].reshape(L, 128)
        da = da_all[:, :, cols].reshape(L, 128)
        dks, dvs = [], []
        for e in range(2):
            s = inner_product(k * half_mask[e], q) * scale
            sigma = sigmoid(s)
            w = jnp.where(causal_t, s * sigma * (1.0 / L), 0.0).astype(BF16)
            dw = inner_product(v * half_mask[e], da)
            ds = jnp.where(
                causal_t, dw * (sigma * (1.0 + s * (1.0 - sigma))) * (scale / L), 0.0
            ).astype(BF16)
            dks.append(matmul(ds, q))
            dvs.append(matmul(w, da))
        for at, parts, place in ((W, dvs, 256), (3 * W, dks, 512)):
            grad = jnp.where(low, parts[0], parts[1]).astype(BF16).astype(F32)
            at = pl.ds(pl.multiple_of(at + n * 128, 128), 128)
            piece = (grad * silu_slope(proj[:, at])).astype(BF16)
            dpo[:, at] = piece
            dps[n, :, place : place + 128] = piece

    s_dp = slots(HIST)
    for o in range(1, HIST + 1):
        n = hist_to(o)
        key_pair(n)
        if o < HIST:
            send(dps.at[n, :, pl.ds(256, 384)], dpa.at[h, :, pl.ds(256, 384)], s_dp + o, hist_dev(n))
    dpa[h] = dps[h]

    for o in range(1, HIST):
        recv(my_all.at[hist_from(o)], s_my + o)
        recv(nga.at[hist_from(o)], s_ng + o)

    def neg_chunk(c, carry):
        left = jnp.concatenate([nga[k, c] for k in range(HIST)], axis=1)
        rsa_s[c] = matmul(left, my_all[:, :, W:].reshape(L, W)).astype(BF16)
        return carry

    lax.fori_loop(0, npl, neg_chunk, 0)
    s_ra = slots(npl)
    for k, ab in enumerate(offsets):
        to = p_to(ab)
        send(rsa_s.at[to], rsa_r.at[k], s_ra + k, p_dev(to))

    for o in range(1, HIST):
        recv(dpa.at[hist_from(o), :, pl.ds(0, 256)], s_dg + o)
        recv(dpa.at[hist_from(o), :, pl.ds(256, 384)], s_dp + o)

    def spread(result, c0, width):
        parts = result.reshape(nz, npl, rw, width)
        for c in range(npl):
            rsb_s[c, :, c0 : c0 + width] = parts[:, c].reshape(nz * rw, width).astype(BF16)

    mixed_t = my_all[:, :, :W].reshape(L, W).T
    spread(matmul(mixed_t, dpa[:, :, 0:128].reshape(L, 128)), 0, 128)
    normed_t = nrm_all[...].reshape(L, W).T
    for c0 in (128, 384):
        spread(matmul(normed_t, dpa[:, :, c0 : c0 + 256].reshape(L, 256)), c0, 256)
    s_rb = slots(npl)
    for k, ab in enumerate(offsets):
        to = p_to(ab)
        send(rsb_s.at[to], rsb_r.at[k], s_rb + k, p_dev(to))

    for o in range(1, nz):
        recv(l2.at[z_from(o)], s_l2 + o)
    part = l2[0]
    for k in range(1, nz):
        part = part + l2[k]
    l3[h] = part
    s_l3 = slots(HIST)
    for o in range(1, HIST):
        send(l3.at[h], l3.at[h], s_l3 + o, hist_dev(hist_to(o)))

    grad = inner_product(dpo[...], win_ref[...])
    dtok_ref[...] = (dout[...] + norm_back(grad, nrmf[...], inverse)).astype(BF16)

    def over_plane(src, arrived, base, out):
        total = src[p].astype(F32)
        for k in range(len(offsets)):
            recv(arrived.at[k], base + k)
            total = total + arrived[k].astype(F32)
        out[...] = total.reshape(out.shape)
        slot = slots(nz)
        return slot

    def over_z(out, arrived, slot):
        for o in range(1, nz):
            to = z_to(o)
            send(out.at[to], arrived.at[o], slot + o, z_dev(to))

    def sum_z(out, arrived, slot):
        total = out[z]
        for o in range(1, nz):
            recv(arrived.at[o], slot + o)
            total = total + arrived[o]
        return total

    s_za = over_plane(rsa_s, rsa_r, s_ra, za_s)
    over_z(za_s, za_r, s_za)
    s_zb = over_plane(rsb_s, rsb_r, s_rb, zb_s)
    over_z(zb_s, zb_r, s_zb)
    s_ea = slots(HIST)
    s_eb = slots(HIST)
    ea[h] = sum_z(za_s, za_r, s_za)
    for o in range(1, HIST):
        send(ea.at[h], ea.at[h], s_ea + o, hist_dev(hist_to(o)))
    eb[h] = sum_z(zb_s, zb_r, s_zb)
    for o in range(1, HIST):
        send(eb.at[h], eb.at[h], s_eb + o, hist_dev(hist_to(o)))

    for o in range(1, HIST):
        recv(l3.at[hist_from(o)], s_l3 + o)
    part = l3[0]
    for k in range(1, HIST):
        part = part + l3[k]
    loss_ref[...] = part / total_events
    for o in range(1, HIST):
        recv(ea.at[hist_from(o)], s_ea + o)
    d_nhat = ea[...].reshape(NB, W)
    dneg_ref[...] = unit_back(d_nhat, n_hat, n_inv) / total_events
    for o in range(1, HIST):
        recv(eb.at[hist_from(o)], s_eb + o)
    for k in range(HIST):
        dwout_ref[:, k * 128 : (k + 1) * 128] = eb[k, :, 0:128] / total_events
        for blk in range(4):
            dwin_ref[:, blk * W + k * 128 : blk * W + (k + 1) * 128] = (
                eb[k, :, (blk + 1) * 128 : (blk + 2) * 128] / total_events
            )
    for copy in sends:
        copy.wait_send()


def local(sizes, *args):
    tokens, targets, target_ids, lengths, negatives, negative_ids, counts, w_in, w_out = args
    nz, nyh, nx = sizes
    npl = nyh * nx
    dp_size = nz * npl
    rw = W // dp_size
    vmem = pltpu.VMEM
    count = 256
    scratch = [
        vmem((HIST, R, W), BF16),
        vmem((HIST, R, W), BF16),
        vmem((R, W), F32),
        vmem((R, 4 * W), F32),
        vmem((R, W), BF16),
        vmem((HIST, R, W), BF16),
        vmem((HIST, R, W), BF16),
        vmem((HIST, R, W), BF16),
        vmem((HEADS, R, L), F32),
        vmem((R, W), BF16),
        vmem((2, npl, nz, NB, 256), BF16),
        vmem((nz, 16, 128), jnp.int32),
        vmem((npl, 16, 128), jnp.int32),
        vmem((npl, nz * NB, 128), F32),
        vmem((npl, nz * NB, 128), F32),
        vmem((npl, nz * NB, 128), F32),
        vmem((npl, nz * NB, 128), BF16),
        vmem((HIST, npl, nz * NQ, 128), BF16),
        vmem((HIST, npl, nz * NQ, 128), BF16),
        vmem((HIST, R, 2 * W), BF16),
        vmem((HIST, R, W), BF16),
        vmem((HIST, R, 640), BF16),
        vmem((HIST, R, 640), BF16),
        vmem((R, 4 * W), BF16),
        vmem((R, W), F32),
        vmem((npl, nz * NQ, W), BF16),
        vmem((npl, nz * NQ, W), BF16),
        vmem((nz, NQ, W), F32),
        vmem((nz, NQ, W), F32),
        vmem((HIST, NQ, W), F32),
        vmem((npl, nz * rw, 640), BF16),
        vmem((npl, nz * rw, 640), BF16),
        vmem((nz, rw, 640), F32),
        vmem((nz, rw, 640), F32),
        vmem((HIST, rw, 640), F32),
        vmem((npl, 8, 128), F32),
        vmem((nz, 8, 128), F32),
        vmem((HIST, 8, 128), F32),
        pltpu.SemaphoreType.DMA((count,)),
        pltpu.SemaphoreType.DMA((count,)),
    ]
    shape = jax.ShapeDtypeStruct
    outs = pl.pallas_call(
        functools.partial(kernel, sizes, count),
        out_shape=[
            shape((8, 128), F32),
            shape((R, W), BF16),
            shape((R, W), BF16),
            shape((rw, 4 * W), F32),
            shape((rw, W), F32),
            shape((NB, W), F32),
        ],
        in_specs=[pl.BlockSpec(memory_space=pltpu.VMEM)] * 9,
        out_specs=[pl.BlockSpec(memory_space=pltpu.VMEM)] * 6,
        scratch_shapes=scratch,
        compiler_params=pltpu.CompilerParams(
            collective_id=0, has_side_effects=True, vmem_limit_bytes=48 * 1024 * 1024
        ),
    )(
        tokens.reshape(R, W),
        targets.reshape(R, W),
        target_ids,
        lengths.reshape(1, 1),
        negatives,
        negative_ids.reshape(1, NB),
        counts.reshape(1, NB),
        w_in,
        w_out,
    )
    return (
        outs[0][0, 0],
        outs[1].reshape(1, R, W),
        outs[2].reshape(1, R, W),
        outs[3],
        outs[4],
        outs[5],
    )


def solution(mesh):
    in_specs = (
        P("dp", "hist", None),
        P("dp", "hist", None),
        P("dp", "hist"),
        P("dp"),
        P("dp", None),
        P("dp"),
        P("dp"),
        P(),
        P(),
    )
    out_specs = (
        P(),
        P("dp", "hist", None),
        P("dp", "hist", None),
        P("dp", None),
        P("dp", None),
        P("dp", None),
    )
    return jax.shard_map(
        functools.partial(local, plan(mesh)),
        mesh=mesh,
        in_specs=in_specs,
        out_specs=out_specs,
        check_vma=False,
    )
```

```python
import functools

import jax
import jax.numpy as jnp
from jax import lax
from jax.experimental import pallas as pl
from jax.experimental.pallas import tpu as pltpu
from jax.sharding import PartitionSpec as P

HEADS = 8
L = 512
W = 512
HIST = 4
R = 128
NB = 32
NQ = NB // HIST
NH = NB // 2
TEMP = 0.05
MESH = pl.DeviceIdType.MESH
F32 = jnp.float32
BF16 = jnp.bfloat16


def layer_norm(values):
    centered = values - jnp.mean(values, -1, keepdims=True)
    inverse = lax.rsqrt(jnp.mean(centered * centered, -1, keepdims=True) + 1e-06)
    return (centered * inverse, inverse)


def norm_back(grad, normed, inverse):
    return inverse * (
        grad
        - jnp.mean(grad, -1, keepdims=True)
        - normed * jnp.mean(grad * normed, -1, keepdims=True)
    )


def unit_rows(values):
    inverse = lax.rsqrt(jnp.sum(values * values, -1, keepdims=True) + 1e-06)
    return (values * inverse, inverse)


def unit_back(grad, unit, inverse):
    return inverse * (grad - unit * jnp.sum(unit * grad, -1, keepdims=True))


def sigmoid(values):
    return 0.5 * jnp.tanh(0.5 * values) + 0.5


def silu_slope(values):
    sigma = sigmoid(values)
    return sigma * (1.0 + values * (1.0 - sigma))


def silu(values):
    return values * sigmoid(values)


def inner_product(left, right):
    return lax.dot_general(left, right, (((1,), (1,)), ((), ())), preferred_element_type=F32)


def matmul(left, right):
    return jnp.dot(left, right, preferred_element_type=F32)


def plan(mesh):
    dp = mesh.shape["dp"]
    if dp == 64:
        return 8, 2, 4
    return dp // 2, 1, 2


def kernel(
    sizes,
    count,
    tok_hbm,
    tgt_hbm,
    tid_hbm,
    len_hbm,
    neg_hbm,
    nid_hbm,
    ncnt_hbm,
    win_hbm,
    wout_hbm,
    loss_ref,
    dtok_ref,
    dtgt_ref,
    dwin_ref,
    dwout_ref,
    dneg_ref,
    tok_ref,
    tgt_ref,
    tid_ref,
    len_ref,
    neg_ref,
    nid_ref,
    ncnt_ref,
    win_ref,
    wout_ref,
    tok_all,
    nrm_all,
    nrmf,
    proj,
    gate,
    k_all,
    v_all,
    q_all,
    slope,
    attn,
    nall,
    idz,
    idx,
    idy,
    idb,
    lcb,
    ex,
    ngo,
    ngs,
    nga,
    my_own,
    my_sib,
    da_all,
    dpq,
    dpq_r,
    dpk,
    dpk_r,
    dpo,
    dout,
    g1,
    g2,
    g3,
    l1,
    l2,
    l3,
    l4,
    lsem,
    ssem,
    rsem,
):
    nz, nyh, nx = sizes
    npl = nyh * nx
    ring = nx
    chunks = 2 * ring
    zh = nz // 2
    dp_size = nz * npl
    rw = W // dp_size
    total_events = float(dp_size * L)
    d = lax.axis_index("dp")
    h = lax.axis_index("hist")
    z = lax.div(d, npl)
    p = lax.rem(d, npl)
    yh = lax.div(p, nx)
    x = lax.rem(p, nx)
    yl = lax.div(h, 2)
    y = yh * 2 + yl
    core = lax.rem(h, 2)
    other = 1 - core
    sib = yl * 2 + other

    def hist_to(o):
        return lax.rem(h + o, HIST)

    def hist_from(o):
        return lax.rem(h + HIST - o, HIST)

    def z_to(o):
        return lax.rem(z + o, nz)

    def z_from(o):
        return lax.rem(z + nz - o, nz)

    def x_to(o):
        return lax.rem(x + o, ring)

    def x_from(o):
        return lax.rem(x + ring - o, ring)

    def y_to(o):
        return lax.rem(y + o, ring)

    def y_from(o):
        return lax.rem(y + ring - o, ring)

    def hist_dev(index):
        return {"dp": d, "hist": index}

    def z_dev(index):
        return {"dp": index * npl + p, "hist": h}

    def x_dev(index):
        return {"dp": z * npl + yh * nx + index, "hist": h}

    def y_dev(index):
        return {
            "dp": z * npl + lax.div(index, 2) * nx + x,
            "hist": lax.rem(index, 2) * 2 + core,
        }

    sends = []
    taken = [0]

    def slots(number):
        base = taken[0]
        taken[0] += number
        assert taken[0] <= count
        return base

    def send(src, dst, slot, device):
        copy = pltpu.make_async_remote_copy(
            src_ref=src,
            dst_ref=dst,
            send_sem=ssem.at[slot],
            recv_sem=rsem.at[slot],
            device_id=device,
            device_id_type=MESH,
        )
        copy.start()
        sends.append(copy)

    def recv(dst, slot):
        pltpu.make_async_remote_copy(
            src_ref=dst,
            dst_ref=dst,
            send_sem=ssem.at[slot],
            recv_sem=rsem.at[slot],
            device_id=hist_dev(sib),
            device_id_type=MESH,
        ).wait_recv()

    barrier = pltpu.get_barrier_semaphore()
    peers = (
        [hist_dev(hist_to(o)) for o in range(1, HIST)]
        + [x_dev(x_to(o)) for o in range(1, ring)]
        + [z_dev(z_to(o)) for o in range(1, nz)]
    )
    if nyh > 1:
        peers += [y_dev(lax.rem(yh + 1, nyh) * 2 + k) for k in range(2)]
    for device in peers:
        pl.semaphore_signal(barrier, inc=1, device_id=device, device_id_type=MESH)

    loads = []
    for k, (src, dst) in enumerate(
        (
            (neg_hbm, neg_ref),
            (nid_hbm, nid_ref),
            (ncnt_hbm, ncnt_ref),
            (tok_hbm, tok_ref),
            (win_hbm, win_ref),
            (wout_hbm, wout_ref),
            (tgt_hbm, tgt_ref),
            (tid_hbm, tid_ref),
            (len_hbm, len_ref),
        )
    ):
        copy = pltpu.make_async_copy(src, dst, lsem.at[k])
        copy.start()
        loads.append(copy)

    for k in range(3):
        loads[k].wait()
    n_hat, n_inv = unit_rows(neg_ref[...].astype(F32))
    rows16 = jnp.where(yl == 0, n_hat[:NH], n_hat[NH:])
    own16 = jnp.where(core == 0, rows16[:, :256], rows16[:, 256:]).astype(BF16)
    lane_at = lax.broadcasted_iota(jnp.int32, (1, 128), 1)
    own_lanes = (lane_at >= x * NB) & (lane_at < x * NB + NB)
    wide = [
        jnp.where(own_lanes, jnp.concatenate([ref[...]] * (128 // NB), axis=1), 0)
        for ref in (nid_ref, ncnt_ref)
    ]
    idz[z] = jnp.concatenate(wide + [jnp.zeros((6, 128), jnp.int32)], axis=0)

    pl.semaphore_wait(barrier, len(peers))

    s_tok = slots(HIST)
    for o in range(1, HIST):
        send(tok_hbm, tok_all.at[h], s_tok + o, hist_dev(hist_to(o)))
    upper = lax.div(z, zh)
    own_chunk = y + upper * (ring + x - y)
    own_place = x + upper * (y - x)
    own_z = lax.rem(z, zh)
    nall[core, own_chunk, own_place, own_z] = own16
    s_nz = slots(nz)
    s_iz = slots(nz)
    own_slot = nall.at[core, own_chunk, own_place, own_z]
    for o in range(1, nz):
        send(own_slot, own_slot, s_nz + o, z_dev(z_to(o)))
        send(idz.at[z], idz.at[z], s_iz + o, z_dev(z_to(o)))

    loads[3].wait()
    loads[4].wait()
    tokf = tok_ref[...].astype(F32)
    normed_f, inverse = layer_norm(tokf)
    nrmf[...] = normed_f
    normed = normed_f.astype(BF16)
    nrm_all[h] = normed
    for blk, ref in enumerate((gate, v_all.at[h], q_all.at[h], k_all.at[h])):
        cols = slice(blk * W, (blk + 1) * W)
        part = matmul(normed, win_ref[:, cols])
        proj[:, cols] = part
        ref[...] = silu(part).astype(BF16)

    for o in range(1, nz):
        src = z_from(o)
        src_upper = lax.div(src, zh)
        recv(
            nall.at[core, y + src_upper * (ring + x - y), x + src_upper * (y - x), lax.rem(src, zh)],
            s_nz + o,
        )
        recv(idz.at[src], s_iz + o)
    idx[x] = jnp.concatenate(
        [idz[k, 0:1] for k in range(nz)]
        + [jnp.zeros((8 - nz, 128), jnp.int32)] * (nz < 8)
        + [idz[k, 1:2] for k in range(nz)]
        + [jnp.zeros((8 - nz, 128), jnp.int32)] * (nz < 8),
        axis=0,
    )
    s_n2x = slots(ring)
    s_n2y = slots(ring)
    s_ix = slots(ring)
    for o in range(1, ring):
        low_half = nall.at[core, y, x]
        high_half = nall.at[core, ring + x, y]
        send(low_half, low_half, s_n2x + o, x_dev(x_to(o)))
        send(high_half, high_half, s_n2y + o, y_dev(y_to(o)))
        send(idx.at[x], idx.at[x], s_ix + o, x_dev(x_to(o)))

    for o in (1, 3, 2):
        b = hist_from(o)
        recv(tok_all.at[b], s_tok + o)
        normed_b = layer_norm(tok_all[b].astype(F32))[0].astype(BF16)
        nrm_all[b] = normed_b
        v_all[b] = silu(matmul(normed_b, win_ref[:, W : 2 * W])).astype(BF16)
        k_all[b] = silu(matmul(normed_b, win_ref[:, 3 * W :])).astype(BF16)

    for o in range(1, ring):
        recv(nall.at[core, y, x_from(o)], s_n2x + o)
        recv(nall.at[core, ring + x, y_from(o)], s_n2y + o)
        recv(idx.at[x_from(o)], s_ix + o)
    tile = idx[0]
    for k in range(1, ring):
        tile = tile + idx[k]
    idy[yh] = tile
    s_n3y = slots(ring)
    s_n3x = slots(ring)
    s_iy = slots(1)
    for o in range(1, ring):
        send(nall.at[core, y], nall.at[core, y], s_n3y + o, y_dev(y_to(o)))
        send(nall.at[core, ring + x], nall.at[core, ring + x], s_n3x + o, x_dev(x_to(o)))
    if nyh > 1:
        send(idy.at[yh], idy.at[yh], s_iy, y_dev(lax.rem(yh + 1, nyh) * 2 + yl))
    s_sib = slots(2 * ring)
    for k, own in enumerate((y, ring + x)):
        send(nall.at[core, own], nall.at[core, own], s_sib + k * ring, hist_dev(sib))

    lane = lax.broadcasted_iota(jnp.int32, (1, 128), 1)
    low = lane < 64
    half_mask = [jnp.where(low, 1.0, 0.0).astype(BF16), jnp.where(low, 0.0, 1.0).astype(BF16)]
    causal = lax.broadcasted_iota(jnp.int32, (R, L), 1) <= h * R + lax.broadcasted_iota(
        jnp.int32, (R, L), 0
    )
    scale = 0.125

    def forward_pair(n, carry):
        cols = pl.ds(pl.multiple_of(n * 128, 128), 128)
        q = q_all[h, :, cols]
        k = k_all[:, :, cols].reshape(L, 128)
        v = v_all[:, :, cols].reshape(L, 128)
        halves = []
        for e in range(2):
            s = inner_product(q * half_mask[e], k) * scale
            sigma = sigmoid(s)
            w = jnp.where(causal, s * sigma * (1.0 / L), 0.0).astype(BF16)
            slope[2 * n + e] = jnp.where(
                causal, sigma * (1.0 + s * (1.0 - sigma)) * (scale / L), 0.0
            )
            halves.append(matmul(w, v))
        attn[:, cols] = jnp.where(low, halves[0], halves[1]).astype(BF16)
        return carry

    lax.fori_loop(0, HEADS // 2, forward_pair, 0)

    for k in range(5, 9):
        loads[k].wait()
    attn_normed, attn_inv = layer_norm(attn[...].astype(F32))
    gate_f = gate[...].astype(F32)
    mixed = (attn_normed * gate_f).astype(BF16)
    my_own[:, :W] = mixed
    output = tok_ref[...].astype(F32) + matmul(mixed, wout_ref[...])
    y_hat, y_inv = unit_rows(output)
    y_hat_b = y_hat.astype(BF16)
    my_own[:, W:] = y_hat_b
    t_hat, t_inv = unit_rows(tgt_ref[...].astype(F32))
    pos_col = jnp.sum(y_hat * t_hat, -1, keepdims=True) / TEMP
    pos_row = jnp.broadcast_to(pos_col, (R, 128)).T[0:1, :]

    for o in range(1, ring):
        for k, (src, base) in enumerate(((y_from(o), s_n3y), (ring + x_from(o), s_n3x))):
            recv(nall.at[core, src], base + o)
            send(nall.at[core, src], nall.at[core, src], s_sib + k * ring + o, hist_dev(sib))
    s_my = slots(1)
    send(my_own, my_sib, s_my, hist_dev(sib))
    if nyh > 1:
        recv(idy.at[lax.rem(yh + 1, nyh)], s_iy)
    for a in range(nyh):
        ids = idy[a, :8].astype(F32)
        logs = jnp.log(jnp.maximum(idy[a, 8:].astype(F32), 1.0))
        turned = jnp.concatenate([ids, logs, jnp.zeros((112, 128), F32)], axis=0).T
        for b in range(nx):
            for c in range(2):
                rows = turned[b * NB + c * NH : b * NB + (c + 1) * NH]
                for k in range(nz):
                    if k < zh:
                        chunk, place = 2 * a + c, b
                    else:
                        chunk, place = ring + b, 2 * a + c
                    at = pl.ds((place * zh + k % zh) * NH, NH)
                    idb[chunk, at] = jnp.broadcast_to(rows[:, k : k + 1], (NH, 128))
                    lcb[chunk, at] = jnp.broadcast_to(rows[:, 8 + k : 9 + k], (NH, 128))
    for o in range(ring):
        recv(nall.at[other, y_from(o)], s_sib + o)
        recv(nall.at[other, ring + x_from(o)], s_sib + ring + o)

    span = ring * zh * NH
    tid_row = tid_ref[...].astype(F32)

    def logits_chunk(c, acc):
        lg = inner_product(nall[0, c].reshape(span, 256), y_hat_b[:, :256]) + inner_product(
            nall[1, c].reshape(span, 256), y_hat_b[:, 256:]
        )
        lg = lg * (1.0 / TEMP) - lcb[c]
        value = jnp.where(idb[c] != tid_row, jnp.exp(lg), 0.0)
        ex[c] = value
        return acc + jnp.sum(value.reshape(span // 8, 8, 128), 0)

    acc = lax.fori_loop(0, chunks, logits_chunk, jnp.zeros((8, 128), F32))
    total = jnp.exp(pos_row) + jnp.sum(acc, 0, keepdims=True)
    position = h * R + lax.broadcasted_iota(jnp.int32, (1, 128), 1)
    valid = jnp.where(position < len_ref[...], 1.0, 0.0)
    pg_row = valid * (jnp.exp(pos_row) / total - 1.0) / TEMP
    pg = jnp.broadcast_to(pg_row, (128, 128)).T[:, 0:1]
    scale_row = valid / (total * TEMP)

    def grad_chunk(c, carry):
        g = ex[c] * scale_row
        ngo[c] = g.astype(BF16)
        g4 = g.reshape(span // NH, 2, NQ, 128)
        for q in range(2):
            ngs[q, c] = g4[:, q].reshape(span // 2, 128).astype(BF16)
        return carry

    lax.fori_loop(0, chunks, grad_chunk, 0)
    ng = ngo[...].reshape(dp_size * NB, 128).T
    d_hat = pg * t_hat + jnp.concatenate(
        [matmul(ng, nall[c].reshape(dp_size * NB, 256)) for c in range(2)], axis=1
    )
    d_out = unit_back(d_hat, y_hat, y_inv)
    d_out_b = d_out.astype(BF16)
    d_mixed = inner_product(d_out_b, wout_ref[...])
    da_all[h] = norm_back(d_mixed * gate_f, attn_normed, attn_inv).astype(BF16)
    s_da = slots(HIST)
    for o in range(1, HIST):
        send(da_all.at[h], da_all.at[h], s_da + o, hist_dev(hist_to(o)))
    s_ng = slots(1)
    send(ngs.at[other], nga, s_ng, hist_dev(sib))
    dout[...] = d_out
    dtgt_ref[...] = unit_back(pg * y_hat, t_hat, t_inv).astype(BF16)
    d_gate = (d_mixed * attn_normed * silu_slope(proj[:, :W])).astype(BF16)
    dpo[:, :W] = d_gate
    for n in range(HIST):
        cols = slice(n * 128, (n + 1) * 128)
        dpq[n % 2, n // 2, :, 0:128] = d_out_b[:, cols]
        dpq[n % 2, n // 2, :, 128:256] = d_gate[:, cols]

    loss = jnp.sum(valid * (jnp.log(total) - pos_row), -1, keepdims=True)
    l1[x] = jnp.broadcast_to(loss, (8, 128))
    s_l1 = slots(ring)
    for o in range(1, ring):
        send(l1.at[x], l1.at[x], s_l1 + o, x_dev(x_to(o)))

    def query_pair(n, carry):
        cols = pl.ds(pl.multiple_of(n * 128, 128), 128)
        da = da_all[h, :, cols]
        k = k_all[:, :, cols].reshape(L, 128)
        v = v_all[:, :, cols].reshape(L, 128)
        halves = []
        for e in range(2):
            dw = inner_product(da * half_mask[e], v)
            halves.append(matmul((dw * slope[2 * n + e]).astype(BF16), k))
        dq = jnp.where(low, halves[0], halves[1]).astype(BF16).astype(F32)
        at = pl.ds(pl.multiple_of(2 * W + n * 128, 128), 128)
        piece = (dq * silu_slope(proj[:, at])).astype(BF16)
        dpo[:, at] = piece
        dpq[lax.rem(n, 2), lax.div(n, 2), :, 256:384] = piece
        return carry

    lax.fori_loop(0, HEADS // 2, query_pair, 0)
    s_dq = slots(1)
    send(dpq.at[other], dpq_r, s_dq, hist_dev(sib))

    def leg1(group):
        src, arrived = group[0], group[1]
        base = slots(2 * ring)
        for o in range(1, ring):
            send(src.at[y_to(o)], arrived.at[0, o], base + o, y_dev(y_to(o)))
            send(src.at[ring + x_to(o)], arrived.at[1, o], base + ring + o, x_dev(x_to(o)))
        return base

    def leg2(group, base):
        src, arrived, mid, arrived2 = group[:4]
        out = slots(2 * ring)
        for part, own in enumerate((y, ring + x)):
            total = src[own].astype(F32)
            for o in range(1, ring):
                recv(arrived.at[part, o], base + part * ring + o)
                total = total + arrived[part, o].astype(F32)
            mid[part] = total.astype(BF16).reshape(mid.shape[1:])
            for o in range(1, ring):
                to, device = (x_to(o), x_dev(x_to(o))) if part == 0 else (y_to(o), y_dev(y_to(o)))
                send(mid.at[part, to], arrived2.at[part, o], out + part * ring + o, device)
        return out

    def leg3(group, base):
        mid, arrived2, zs, zr = group[2:6]
        for part, own in enumerate((x, y)):
            total = mid[part, own].astype(F32)
            for o in range(1, ring):
                recv(arrived2.at[part, o], base + part * ring + o)
                total = total + arrived2[part, o].astype(F32)
            zs[part * zh : (part + 1) * zh] = total.reshape((zh,) + zs.shape[1:])
        out = slots(nz)
        for o in range(1, nz):
            send(zs.at[z_to(o)], zr.at[o], out + o, z_dev(z_to(o)))
        return out

    def leg4(group, base):
        zs, zr, eh = group[4:]
        total = zs[z]
        for o in range(1, nz):
            recv(zr.at[o], base + o)
            total = total + zr[o]
        eh[h] = total
        out = slots(HIST)
        for o in range(1, HIST):
            send(eh.at[h], eh.at[h], out + o, hist_dev(hist_to(o)))
        return out

    def arrive(group, base):
        for o in range(1, HIST):
            recv(group[6].at[hist_from(o)], base + o)

    def spread(result, k, group, c0):
        width = result.shape[1]
        for a in range(nyh):
            for b in range(nx):
                for half in range(2):
                    block = jnp.concatenate(
                        [
                            result[((half * zh + j) * npl + a * nx + b) * rw :][:rw]
                            for j in range(zh)
                        ],
                        axis=0,
                    ).astype(BF16)
                    chunk, place = (2 * a + k, b) if half == 0 else (ring + b, 2 * a + k)
                    group[0][chunk, place * zh * rw : (place + 1) * zh * rw, c0 : c0 + width] = block

    recv(my_sib, s_my)
    recv(nga, s_ng)

    def neg_chunk(c, carry):
        left = jnp.concatenate([ngs[core, c], nga[c]], axis=1)
        right = jnp.concatenate([my_own[:, W:], my_sib[:, W:]], axis=0)
        g1[0][c] = matmul(left, right).astype(BF16)
        return carry

    lax.fori_loop(0, chunks, neg_chunk, 0)
    t1 = leg1(g1)

    mixed_t = jnp.concatenate([my_own[:, :W], my_sib[:, :W]], axis=0).T
    normed_t = jnp.concatenate([nrm_all[h], nrm_all[sib]], axis=0).T
    recv(dpq_r, s_dq)
    for k in range(2):
        right = jnp.concatenate([dpq[core, k], dpq_r[k]], axis=0)
        spread(matmul(mixed_t, right[:, :128]), k, g2, 0)
        spread(matmul(normed_t, right[:, 128:]), k, g2, 128)
    t2 = leg1(g2)

    for o in range(1, HIST):
        b = hist_from(o)
        q_all[b] = silu(matmul(nrm_all[b], win_ref[:, 2 * W : 3 * W])).astype(BF16)

    for o in range(1, ring):
        recv(l1.at[x_from(o)], s_l1 + o)
    part = l1[0]
    for k in range(1, ring):
        part = part + l1[k]
    l2[y] = part
    s_l2 = slots(ring)
    for o in range(1, ring):
        send(l2.at[y], l2.at[y], s_l2 + o, y_dev(y_to(o)))

    for o in range(1, HIST):
        recv(da_all.at[hist_from(o)], s_da + o)
    causal_t = lax.broadcasted_iota(jnp.int32, (R, L), 1) >= h * R + lax.broadcasted_iota(
        jnp.int32, (R, L), 0
    )

    def key_pair(n, carry):
        cols = pl.ds(pl.multiple_of(n * 128, 128), 128)
        k = k_all[h, :, cols]
        v = v_all[h, :, cols]
        q = q_all[:, :, cols].reshape(L, 128)
        da = da_all[:, :, cols].reshape(L, 128)
        dks, dvs = [], []
        for e in range(2):
            s = inner_product(k * half_mask[e], q) * scale
            sigma = sigmoid(s)
            w = jnp.where(causal_t, s * sigma * (1.0 / L), 0.0).astype(BF16)
            dw = inner_product(v * half_mask[e], da)
            ds = jnp.where(
                causal_t, dw * (sigma * (1.0 + s * (1.0 - sigma))) * (scale / L), 0.0
            ).astype(BF16)
            dks.append(matmul(ds, q))
            dvs.append(matmul(w, da))
        for at, parts, place in ((W, dvs, 0), (3 * W, dks, 128)):
            grad = jnp.where(low, parts[0], parts[1]).astype(BF16).astype(F32)
            at = pl.ds(pl.multiple_of(at + n * 128, 128), 128)
            piece = (grad * silu_slope(proj[:, at])).astype(BF16)
            dpo[:, at] = piece
            dpk[lax.rem(n, 2), lax.div(n, 2), :, place : place + 128] = piece
        return carry

    lax.fori_loop(0, HEADS // 2, key_pair, 0)
    s_dk = slots(1)
    send(dpk.at[other], dpk_r, s_dk, hist_dev(sib))

    t1 = leg2(g1, t1)
    recv(dpk_r, s_dk)
    for k in range(2):
        right = jnp.concatenate([dpk[core, k], dpk_r[k]], axis=0)
        spread(matmul(normed_t, right), k, g3, 0)
    t3 = leg1(g3)
    t2 = leg2(g2, t2)

    for o in range(1, ring):
        recv(l2.at[y_from(o)], s_l2 + o)
    part = l2[0]
    for k in range(1, ring):
        part = part + l2[k]
    l3[z] = part
    s_l3 = slots(nz)
    for o in range(1, nz):
        send(l3.at[z], l3.at[z], s_l3 + o, z_dev(z_to(o)))

    grad = inner_product(dpo[...], win_ref[...])
    dtok_ref[...] = (dout[...] + norm_back(grad, nrmf[...], inverse)).astype(BF16)

    t1 = leg3(g1, t1)
    t3 = leg2(g3, t3)
    t2 = leg3(g2, t2)
    t1 = leg4(g1, t1)
    t3 = leg3(g3, t3)
    for o in range(1, nz):
        recv(l3.at[z_from(o)], s_l3 + o)
    part = l3[0]
    for k in range(1, nz):
        part = part + l3[k]
    l4[core] = part
    s_l4 = slots(1)
    send(l4.at[core], l4.at[core], s_l4, hist_dev(sib))
    t2 = leg4(g2, t2)
    arrive(g1, t1)
    d_nhat = g1[6][...].reshape(NB, W)
    dneg_ref[...] = unit_back(d_nhat, n_hat, n_inv) / total_events
    t3 = leg4(g3, t3)
    recv(l4.at[other], s_l4)
    loss_ref[...] = (l4[0] + l4[1]) / total_events
    arrive(g2, t2)
    for k in range(HIST):
        cols = slice(k * 128, (k + 1) * 128)
        dwout_ref[:, cols] = g2[6][k, :, 0:128] / total_events
        dwin_ref[:, cols] = g2[6][k, :, 128:256] / total_events
        dwin_ref[:, 2 * W + k * 128 : 2 * W + (k + 1) * 128] = g2[6][k, :, 256:384] / total_events
    arrive(g3, t3)
    for k in range(HIST):
        dwin_ref[:, W + k * 128 : W + (k + 1) * 128] = g3[6][k, :, 0:128] / total_events
        dwin_ref[:, 3 * W + k * 128 : 3 * W + (k + 1) * 128] = g3[6][k, :, 128:256] / total_events
    for copy in sends:
        copy.wait_send()


def local(sizes, *args):
    tokens, targets, target_ids, lengths, negatives, negative_ids, counts, w_in, w_out = args
    nz, nyh, nx = sizes
    npl = nyh * nx
    dp_size = nz * npl
    rw = W // dp_size
    ring = nx
    assert ring == 2 * nyh
    zh = nz // 2
    chunks = 2 * ring
    span = ring * zh * NH
    vmem = pltpu.VMEM
    count = 256

    def group(rows, width):
        block = ring * zh * rows
        return (
            vmem((chunks, block, width), BF16),
            vmem((2, ring, block, width), BF16),
            vmem((2, ring, zh * rows, width), BF16),
            vmem((2, ring, zh * rows, width), BF16),
            vmem((nz, rows, width), F32),
            vmem((nz, rows, width), F32),
            vmem((HIST, rows, width), F32),
        )

    scratch = [
        vmem((R, W), BF16),
        vmem((R, W), BF16),
        vmem((1, R), jnp.int32),
        vmem((1, 1), jnp.int32),
        vmem((NB, W), BF16),
        vmem((1, NB), jnp.int32),
        vmem((1, NB), jnp.int32),
        vmem((W, 4 * W), BF16),
        vmem((W, W), BF16),
        vmem((HIST, R, W), BF16),
        vmem((HIST, R, W), BF16),
        vmem((R, W), F32),
        vmem((R, 4 * W), F32),
        vmem((R, W), BF16),
        vmem((HIST, R, W), BF16),
        vmem((HIST, R, W), BF16),
        vmem((HIST, R, W), BF16),
        vmem((HEADS, R, L), F32),
        vmem((R, W), BF16),
        vmem((2, chunks, ring, zh, NH, 256), BF16),
        vmem((nz, 8, 128), jnp.int32),
        vmem((ring, 16, 128), jnp.int32),
        vmem((nyh, 16, 128), jnp.int32),
        vmem((chunks, span, 128), F32),
        vmem((chunks, span, 128), F32),
        vmem((chunks, span, 128), F32),
        vmem((chunks, span, 128), BF16),
        vmem((2, chunks, span // 2, 128), BF16),
        vmem((chunks, span // 2, 128), BF16),
        vmem((R, 2 * W), BF16),
        vmem((R, 2 * W), BF16),
        vmem((HIST, R, W), BF16),
        vmem((2, 2, R, 384), BF16),
        vmem((2, R, 384), BF16),
        vmem((2, 2, R, 256), BF16),
        vmem((2, R, 256), BF16),
        vmem((R, 4 * W), BF16),
        vmem((R, W), F32),
        group(NQ, W),
        group(rw, 384),
        group(rw, 256),
        vmem((ring, 8, 128), F32),
        vmem((ring, 8, 128), F32),
        vmem((nz, 8, 128), F32),
        vmem((2, 8, 128), F32),
        pltpu.SemaphoreType.DMA((9,)),
        pltpu.SemaphoreType.DMA((count,)),
        pltpu.SemaphoreType.DMA((count,)),
    ]
    shape = jax.ShapeDtypeStruct
    outs = pl.pallas_call(
        functools.partial(kernel, sizes, count),
        out_shape=[
            shape((8, 128), F32),
            shape((R, W), BF16),
            shape((R, W), BF16),
            shape((rw, 4 * W), F32),
            shape((rw, W), F32),
            shape((NB, W), F32),
        ],
        in_specs=[pl.BlockSpec(memory_space=pltpu.HBM)] * 9,
        out_specs=[pl.BlockSpec(memory_space=pltpu.VMEM)] * 6,
        scratch_shapes=scratch,
        compiler_params=pltpu.CompilerParams(
            collective_id=0, has_side_effects=True, vmem_limit_bytes=48 * 1024 * 1024
        ),
    )(
        tokens.reshape(R, W),
        targets.reshape(R, W),
        target_ids,
        lengths.reshape(1, 1),
        negatives,
        negative_ids.reshape(1, NB),
        counts.reshape(1, NB),
        w_in,
        w_out,
    )
    return (
        outs[0][0, 0],
        outs[1].reshape(1, R, W),
        outs[2].reshape(1, R, W),
        outs[3],
        outs[4],
        outs[5],
    )


def solution(mesh):
    in_specs = (
        P("dp", "hist", None),
        P("dp", "hist", None),
        P("dp", "hist"),
        P("dp"),
        P("dp", None),
        P("dp"),
        P("dp"),
        P(),
        P(),
    )
    out_specs = (
        P(),
        P("dp", "hist", None),
        P("dp", "hist", None),
        P("dp", None),
        P("dp", None),
        P("dp", None),
    )
    return jax.shard_map(
        functools.partial(local, plan(mesh)),
        mesh=mesh,
        in_specs=in_specs,
        out_specs=out_specs,
        check_vma=False,
    )
```

```python
import functools

import jax
import jax.numpy as jnp
from jax import lax
from jax.experimental import pallas as pl
from jax.experimental.pallas import tpu as pltpu
from jax.sharding import PartitionSpec as P

HEADS = 8
L = 512
W = 512
HIST = 4
R = 128
NB = 32
NQ = NB // HIST
NH = NB // 2
TEMP = 0.05
MESH = pl.DeviceIdType.MESH
VMEM_LIMIT = 64 * 1024 * 1024
F32 = jnp.float32
BF16 = jnp.bfloat16


def layer_norm(values):
    centered = values - jnp.mean(values, -1, keepdims=True)
    inverse = lax.rsqrt(jnp.mean(centered * centered, -1, keepdims=True) + 1e-06)
    return (centered * inverse, inverse)


def norm_back(grad, normed, inverse):
    return inverse * (
        grad
        - jnp.mean(grad, -1, keepdims=True)
        - normed * jnp.mean(grad * normed, -1, keepdims=True)
    )


def unit_rows(values):
    inverse = lax.rsqrt(jnp.sum(values * values, -1, keepdims=True) + 1e-06)
    return (values * inverse, inverse)


def unit_back(grad, unit, inverse):
    return inverse * (grad - unit * jnp.sum(unit * grad, -1, keepdims=True))


def sigmoid(values):
    return 0.5 * jnp.tanh(0.5 * values) + 0.5


def silu_slope(values):
    sigma = sigmoid(values)
    return sigma * (1.0 + values * (1.0 - sigma))


def silu(values):
    return values * sigmoid(values)


def inner_product(left, right):
    return lax.dot_general(left, right, (((1,), (1,)), ((), ())), preferred_element_type=F32)


def matmul(left, right):
    return jnp.dot(left, right, preferred_element_type=F32)


def plan(mesh):
    dp = mesh.shape["dp"]
    if dp == 64:
        return 8, 2, 4
    return dp // 2, 1, 2


def kernel(
    sizes,
    count,
    tok_hbm,
    tgt_hbm,
    tid_hbm,
    len_hbm,
    neg_hbm,
    nid_hbm,
    ncnt_hbm,
    win_hbm,
    wout_hbm,
    loss_hbm,
    dtok_hbm,
    dtgt_hbm,
    dwin_hbm,
    dwout_hbm,
    dneg_hbm,
    loss_ref,
    dtok_ref,
    dtgt_ref,
    dwin_ref,
    dwout_ref,
    dneg_ref,
    tok_ref,
    tgt_ref,
    tid_ref,
    len_ref,
    neg_ref,
    nid_ref,
    ncnt_ref,
    win_ref,
    wout_ref,
    tok_all,
    nrm_all,
    nrmf,
    proj,
    gate,
    k_all,
    v_all,
    q_all,
    slope,
    attn,
    nall,
    idz,
    idx,
    idy,
    idb,
    lcb,
    ex,
    ngo,
    ngs,
    nga,
    my_own,
    my_sib,
    da_all,
    dpq,
    dpq_r,
    dpk,
    dpk_r,
    dpo,
    dout,
    g1,
    g2,
    g3,
    l1,
    l2,
    l3,
    l4,
    lsem,
    osem,
    ssem,
    rsem,
):
    nz, nyh, nx = sizes
    npl = nyh * nx
    ring = nx
    chunks = 2 * ring
    zh = nz // 2
    dp_size = nz * npl
    rw = W // dp_size
    total_events = float(dp_size * L)
    d = lax.axis_index("dp")
    h = lax.axis_index("hist")
    z = lax.div(d, npl)
    p = lax.rem(d, npl)
    yh = lax.div(p, nx)
    x = lax.rem(p, nx)
    yl = lax.div(h, 2)
    y = yh * 2 + yl
    core = lax.rem(h, 2)
    other = 1 - core
    sib = yl * 2 + other

    def hist_to(o):
        return lax.rem(h + o, HIST)

    def hist_from(o):
        return lax.rem(h + HIST - o, HIST)

    def z_to(o):
        return lax.rem(z + o, nz)

    def z_from(o):
        return lax.rem(z + nz - o, nz)

    def x_to(o):
        return lax.rem(x + o, ring)

    def x_from(o):
        return lax.rem(x + ring - o, ring)

    def y_to(o):
        return lax.rem(y + o, ring)

    def y_from(o):
        return lax.rem(y + ring - o, ring)

    def hist_dev(index):
        return {"dp": d, "hist": index}

    def z_dev(index):
        return {"dp": index * npl + p, "hist": h}

    def x_dev(index):
        return {"dp": z * npl + yh * nx + index, "hist": h}

    def y_dev(index):
        return {
            "dp": z * npl + lax.div(index, 2) * nx + x,
            "hist": lax.rem(index, 2) * 2 + core,
        }

    sends = []
    taken = [0]

    def slots(number):
        base = taken[0]
        taken[0] += number
        assert taken[0] <= count
        return base

    def send(src, dst, slot, device):
        copy = pltpu.make_async_remote_copy(
            src_ref=src,
            dst_ref=dst,
            send_sem=ssem.at[slot],
            recv_sem=rsem.at[slot],
            device_id=device,
            device_id_type=MESH,
        )
        copy.start()
        sends.append(copy)

    def recv(dst, slot):
        pltpu.make_async_remote_copy(
            src_ref=dst,
            dst_ref=dst,
            send_sem=ssem.at[slot],
            recv_sem=rsem.at[slot],
            device_id=hist_dev(sib),
            device_id_type=MESH,
        ).wait_recv()

    stores = []

    def store(src, dst):
        copy = pltpu.make_async_copy(src, dst, osem.at[len(stores)])
        copy.start()
        stores.append(copy)

    barrier = pltpu.get_barrier_semaphore()
    peers = (
        [hist_dev(hist_to(o)) for o in range(1, HIST)]
        + [x_dev(x_to(o)) for o in range(1, ring)]
        + [z_dev(z_to(o)) for o in range(1, nz)]
    )
    if nyh > 1:
        peers += [y_dev(lax.rem(yh + 1, nyh) * 2 + k) for k in range(2)]
    for device in peers:
        pl.semaphore_signal(barrier, inc=1, device_id=device, device_id_type=MESH)

    loads = []
    for k, (src, dst) in enumerate(
        (
            (neg_hbm, neg_ref),
            (nid_hbm, nid_ref),
            (ncnt_hbm, ncnt_ref),
            (tok_hbm, tok_ref),
            (win_hbm, win_ref),
            (wout_hbm, wout_ref),
            (tgt_hbm, tgt_ref),
            (tid_hbm, tid_ref),
            (len_hbm, len_ref),
        )
    ):
        copy = pltpu.make_async_copy(src, dst, lsem.at[k])
        copy.start()
        loads.append(copy)

    for k in range(3):
        loads[k].wait()
    n_hat, n_inv = unit_rows(neg_ref[...].astype(F32))
    rows16 = jnp.where(yl == 0, n_hat[:NH], n_hat[NH:])
    own16 = jnp.where(core == 0, rows16[:, :256], rows16[:, 256:]).astype(BF16)
    lane_at = lax.broadcasted_iota(jnp.int32, (1, 128), 1)
    own_lanes = (lane_at >= x * NB) & (lane_at < x * NB + NB)
    wide = [
        jnp.where(own_lanes, jnp.concatenate([ref[...]] * (128 // NB), axis=1), 0)
        for ref in (nid_ref, ncnt_ref)
    ]
    idz[z] = jnp.concatenate(wide + [jnp.zeros((6, 128), jnp.int32)], axis=0)

    pl.semaphore_wait(barrier, len(peers))

    s_tok = slots(HIST)
    for o in range(1, HIST):
        send(tok_hbm, tok_all.at[h], s_tok + o, hist_dev(hist_to(o)))
    upper = lax.div(z, zh)
    own_chunk = y + upper * (ring + x - y)
    own_place = x + upper * (y - x)
    own_z = lax.rem(z, zh)
    nall[core, own_chunk, own_place, own_z] = own16
    s_nz = slots(nz)
    s_iz = slots(nz)
    own_slot = nall.at[core, own_chunk, own_place, own_z]
    for o in range(1, nz):
        send(own_slot, own_slot, s_nz + o, z_dev(z_to(o)))
        send(idz.at[z], idz.at[z], s_iz + o, z_dev(z_to(o)))

    loads[3].wait()
    loads[4].wait()
    tokf = tok_ref[...].astype(F32)
    normed_f, inverse = layer_norm(tokf)
    nrmf[...] = normed_f
    normed = normed_f.astype(BF16)
    nrm_all[h] = normed
    for blk, ref in enumerate((gate, v_all.at[h], q_all.at[h], k_all.at[h])):
        cols = slice(blk * W, (blk + 1) * W)
        part = matmul(normed, win_ref[:, cols])
        proj[:, cols] = part
        ref[...] = silu(part).astype(BF16)

    for o in range(1, nz):
        src = z_from(o)
        src_upper = lax.div(src, zh)
        recv(
            nall.at[core, y + src_upper * (ring + x - y), x + src_upper * (y - x), lax.rem(src, zh)],
            s_nz + o,
        )
        recv(idz.at[src], s_iz + o)
    idx[x] = jnp.concatenate(
        [idz[k, 0:1] for k in range(nz)]
        + [jnp.zeros((8 - nz, 128), jnp.int32)] * (nz < 8)
        + [idz[k, 1:2] for k in range(nz)]
        + [jnp.zeros((8 - nz, 128), jnp.int32)] * (nz < 8),
        axis=0,
    )
    s_n2x = slots(ring)
    s_n2y = slots(ring)
    s_ix = slots(ring)
    for o in range(1, ring):
        low_half = nall.at[core, y, x]
        high_half = nall.at[core, ring + x, y]
        send(low_half, low_half, s_n2x + o, x_dev(x_to(o)))
        send(high_half, high_half, s_n2y + o, y_dev(y_to(o)))
        send(idx.at[x], idx.at[x], s_ix + o, x_dev(x_to(o)))

    for o in (1, 3, 2):
        b = hist_from(o)
        recv(tok_all.at[b], s_tok + o)
        normed_b = layer_norm(tok_all[b].astype(F32))[0].astype(BF16)
        nrm_all[b] = normed_b
        v_all[b] = silu(matmul(normed_b, win_ref[:, W : 2 * W])).astype(BF16)
        k_all[b] = silu(matmul(normed_b, win_ref[:, 3 * W :])).astype(BF16)

    for o in range(1, ring):
        recv(nall.at[core, y, x_from(o)], s_n2x + o)
        recv(nall.at[core, ring + x, y_from(o)], s_n2y + o)
        recv(idx.at[x_from(o)], s_ix + o)
    tile = idx[0]
    for k in range(1, ring):
        tile = tile + idx[k]
    idy[yh] = tile
    s_n3y = slots(ring)
    s_n3x = slots(ring)
    s_iy = slots(1)
    for o in range(1, ring):
        send(nall.at[core, y], nall.at[core, y], s_n3y + o, y_dev(y_to(o)))
        send(nall.at[core, ring + x], nall.at[core, ring + x], s_n3x + o, x_dev(x_to(o)))
    if nyh > 1:
        send(idy.at[yh], idy.at[yh], s_iy, y_dev(lax.rem(yh + 1, nyh) * 2 + yl))
    s_sib = slots(2 * ring)
    for k, own in enumerate((y, ring + x)):
        send(nall.at[core, own], nall.at[core, own], s_sib + k * ring, hist_dev(sib))

    lane = lax.broadcasted_iota(jnp.int32, (1, 128), 1)
    low = lane < 64
    half_mask = [jnp.where(low, 1.0, 0.0).astype(BF16), jnp.where(low, 0.0, 1.0).astype(BF16)]
    causal = lax.broadcasted_iota(jnp.int32, (R, L), 1) <= h * R + lax.broadcasted_iota(
        jnp.int32, (R, L), 0
    )
    scale = 0.125

    def forward_pair(n, carry):
        cols = pl.ds(pl.multiple_of(n * 128, 128), 128)
        q = q_all[h, :, cols]
        k = k_all[:, :, cols].reshape(L, 128)
        v = v_all[:, :, cols].reshape(L, 128)
        halves = []
        for e in range(2):
            s = inner_product(q * half_mask[e], k) * scale
            sigma = sigmoid(s)
            w = jnp.where(causal, s * sigma * (1.0 / L), 0.0).astype(BF16)
            slope[2 * n + e] = jnp.where(
                causal, sigma * (1.0 + s * (1.0 - sigma)) * (scale / L), 0.0
            )
            halves.append(matmul(w, v))
        attn[:, cols] = jnp.where(low, halves[0], halves[1]).astype(BF16)
        return carry

    lax.fori_loop(0, HEADS // 2, forward_pair, 0)

    for k in range(5, 9):
        loads[k].wait()
    attn_normed, attn_inv = layer_norm(attn[...].astype(F32))
    gate_f = gate[...].astype(F32)
    mixed = (attn_normed * gate_f).astype(BF16)
    my_own[:, :W] = mixed
    output = tok_ref[...].astype(F32) + matmul(mixed, wout_ref[...])
    y_hat, y_inv = unit_rows(output)
    y_hat_b = y_hat.astype(BF16)
    my_own[:, W:] = y_hat_b
    t_hat, t_inv = unit_rows(tgt_ref[...].astype(F32))
    pos_col = jnp.sum(y_hat * t_hat, -1, keepdims=True) / TEMP
    pos_row = jnp.broadcast_to(pos_col, (R, 128)).T[0:1, :]

    for o in range(1, ring):
        for k, (src, base) in enumerate(((y_from(o), s_n3y), (ring + x_from(o), s_n3x))):
            recv(nall.at[core, src], base + o)
            send(nall.at[core, src], nall.at[core, src], s_sib + k * ring + o, hist_dev(sib))
    s_my = slots(1)
    send(my_own, my_sib, s_my, hist_dev(sib))
    if nyh > 1:
        recv(idy.at[lax.rem(yh + 1, nyh)], s_iy)
    for a in range(nyh):
        ids = idy[a, :8].astype(F32)
        logs = jnp.log(jnp.maximum(idy[a, 8:].astype(F32), 1.0))
        turned = jnp.concatenate([ids, logs, jnp.zeros((112, 128), F32)], axis=0).T
        for b in range(nx):
            for c in range(2):
                rows = turned[b * NB + c * NH : b * NB + (c + 1) * NH]
                for k in range(nz):
                    if k < zh:
                        chunk, place = 2 * a + c, b
                    else:
                        chunk, place = ring + b, 2 * a + c
                    at = pl.ds((place * zh + k % zh) * NH, NH)
                    idb[chunk, at] = jnp.broadcast_to(rows[:, k : k + 1], (NH, 128))
                    lcb[chunk, at] = jnp.broadcast_to(rows[:, 8 + k : 9 + k], (NH, 128))
    for o in range(ring):
        recv(nall.at[other, y_from(o)], s_sib + o)
        recv(nall.at[other, ring + x_from(o)], s_sib + ring + o)

    span = ring * zh * NH
    tid_row = tid_ref[...].astype(F32)

    def logits_chunk(c, acc):
        lg = inner_product(nall[0, c].reshape(span, 256), y_hat_b[:, :256]) + inner_product(
            nall[1, c].reshape(span, 256), y_hat_b[:, 256:]
        )
        lg = lg * (1.0 / TEMP) - lcb[c]
        value = jnp.where(idb[c] != tid_row, jnp.exp(lg), 0.0)
        ex[c] = value
        return acc + jnp.sum(value.reshape(span // 8, 8, 128), 0)

    acc = lax.fori_loop(0, chunks, logits_chunk, jnp.zeros((8, 128), F32))
    total = jnp.exp(pos_row) + jnp.sum(acc, 0, keepdims=True)
    position = h * R + lax.broadcasted_iota(jnp.int32, (1, 128), 1)
    valid = jnp.where(position < len_ref[0], 1.0, 0.0)
    pg_row = valid * (jnp.exp(pos_row) / total - 1.0) / TEMP
    pg = jnp.broadcast_to(pg_row, (128, 128)).T[:, 0:1]
    scale_row = valid / (total * TEMP)

    def grad_chunk(c, carry):
        g = ex[c] * scale_row
        ngo[c] = g.astype(BF16)
        g4 = g.reshape(span // NH, 2, NQ, 128)
        for q in range(2):
            ngs[q, c] = g4[:, q].reshape(span // 2, 128).astype(BF16)
        return carry

    lax.fori_loop(0, chunks, grad_chunk, 0)
    ng = ngo[...].reshape(dp_size * NB, 128).T
    d_hat = pg * t_hat + jnp.concatenate(
        [matmul(ng, nall[c].reshape(dp_size * NB, 256)) for c in range(2)], axis=1
    )
    d_out = unit_back(d_hat, y_hat, y_inv)
    d_out_b = d_out.astype(BF16)
    d_mixed = inner_product(d_out_b, wout_ref[...])
    da_all[h] = norm_back(d_mixed * gate_f, attn_normed, attn_inv).astype(BF16)
    s_da = slots(HIST)
    for o in range(1, HIST):
        send(da_all.at[h], da_all.at[h], s_da + o, hist_dev(hist_to(o)))
    s_ng = slots(1)
    send(ngs.at[other], nga, s_ng, hist_dev(sib))
    dout[...] = d_out
    dtgt_ref[...] = unit_back(pg * y_hat, t_hat, t_inv).astype(BF16)
    store(dtgt_ref, dtgt_hbm)
    d_gate = (d_mixed * attn_normed * silu_slope(proj[:, :W])).astype(BF16)
    dpo[:, :W] = d_gate
    for n in range(HIST):
        cols = slice(n * 128, (n + 1) * 128)
        dpq[n % 2, n // 2, :, 0:128] = d_out_b[:, cols]
        dpq[n % 2, n // 2, :, 128:256] = d_gate[:, cols]

    loss = jnp.sum(valid * (jnp.log(total) - pos_row), -1, keepdims=True)
    l1[x] = jnp.broadcast_to(loss, (8, 128))
    s_l1 = slots(ring)
    for o in range(1, ring):
        send(l1.at[x], l1.at[x], s_l1 + o, x_dev(x_to(o)))

    def query_pair(n, carry):
        cols = pl.ds(pl.multiple_of(n * 128, 128), 128)
        da = da_all[h, :, cols]
        k = k_all[:, :, cols].reshape(L, 128)
        v = v_all[:, :, cols].reshape(L, 128)
        halves = []
        for e in range(2):
            dw = inner_product(da * half_mask[e], v)
            halves.append(matmul((dw * slope[2 * n + e]).astype(BF16), k))
        dq = jnp.where(low, halves[0], halves[1]).astype(BF16).astype(F32)
        at = pl.ds(pl.multiple_of(2 * W + n * 128, 128), 128)
        piece = (dq * silu_slope(proj[:, at])).astype(BF16)
        dpo[:, at] = piece
        dpq[lax.rem(n, 2), lax.div(n, 2), :, 256:384] = piece
        return carry

    lax.fori_loop(0, HEADS // 2, query_pair, 0)
    s_dq = slots(1)
    send(dpq.at[other], dpq_r, s_dq, hist_dev(sib))

    def leg1(group):
        src, arrived = group[0], group[1]
        base = slots(2 * ring)
        for o in range(1, ring):
            send(src.at[y_to(o)], arrived.at[0, o], base + o, y_dev(y_to(o)))
            send(src.at[ring + x_to(o)], arrived.at[1, o], base + ring + o, x_dev(x_to(o)))
        return base

    def leg2(group, base):
        src, arrived, mid, arrived2 = group[:4]
        out = slots(2 * ring)
        for part, own in enumerate((y, ring + x)):
            total = src[own].astype(F32)
            for o in range(1, ring):
                recv(arrived.at[part, o], base + part * ring + o)
                total = total + arrived[part, o].astype(F32)
            mid[part] = total.astype(BF16).reshape(mid.shape[1:])
            for o in range(1, ring):
                to, device = (x_to(o), x_dev(x_to(o))) if part == 0 else (y_to(o), y_dev(y_to(o)))
                send(mid.at[part, to], arrived2.at[part, o], out + part * ring + o, device)
        return out

    def leg3(group, base):
        mid, arrived2, zs, zr = group[2:6]
        for part, own in enumerate((x, y)):
            total = mid[part, own].astype(F32)
            for o in range(1, ring):
                recv(arrived2.at[part, o], base + part * ring + o)
                total = total + arrived2[part, o].astype(F32)
            zs[part * zh : (part + 1) * zh] = total.reshape((zh,) + zs.shape[1:])
        out = slots(nz)
        for o in range(1, nz):
            send(zs.at[z_to(o)], zr.at[o], out + o, z_dev(z_to(o)))
        return out

    def leg4(group, base):
        zs, zr, eh = group[4:]
        total = zs[z]
        for o in range(1, nz):
            recv(zr.at[o], base + o)
            total = total + zr[o]
        eh[h] = total
        out = slots(HIST)
        for o in range(1, HIST):
            send(eh.at[h], eh.at[h], out + o, hist_dev(hist_to(o)))
        return out

    def arrive(group, base):
        for o in range(1, HIST):
            recv(group[6].at[hist_from(o)], base + o)

    def spread(result, k, group, c0):
        width = result.shape[1]
        for a in range(nyh):
            for b in range(nx):
                for half in range(2):
                    block = jnp.concatenate(
                        [
                            result[((half * zh + j) * npl + a * nx + b) * rw :][:rw]
                            for j in range(zh)
                        ],
                        axis=0,
                    ).astype(BF16)
                    chunk, place = (2 * a + k, b) if half == 0 else (ring + b, 2 * a + k)
                    group[0][chunk, place * zh * rw : (place + 1) * zh * rw, c0 : c0 + width] = block

    recv(my_sib, s_my)
    recv(nga, s_ng)

    def neg_chunk(c, carry):
        left = jnp.concatenate([ngs[core, c], nga[c]], axis=1)
        right = jnp.concatenate([my_own[:, W:], my_sib[:, W:]], axis=0)
        g1[0][c] = matmul(left, right).astype(BF16)
        return carry

    lax.fori_loop(0, chunks, neg_chunk, 0)
    t1 = leg1(g1)

    mixed_t = jnp.concatenate([my_own[:, :W], my_sib[:, :W]], axis=0).T
    normed_t = jnp.concatenate([nrm_all[h], nrm_all[sib]], axis=0).T
    recv(dpq_r, s_dq)
    for k in range(2):
        right = jnp.concatenate([dpq[core, k], dpq_r[k]], axis=0)
        spread(matmul(mixed_t, right[:, :128]), k, g2, 0)
        spread(matmul(normed_t, right[:, 128:]), k, g2, 128)
    t2 = leg1(g2)

    for o in range(1, HIST):
        b = hist_from(o)
        q_all[b] = silu(matmul(nrm_all[b], win_ref[:, 2 * W : 3 * W])).astype(BF16)

    for o in range(1, ring):
        recv(l1.at[x_from(o)], s_l1 + o)
    part = l1[0]
    for k in range(1, ring):
        part = part + l1[k]
    l2[y] = part
    s_l2 = slots(ring)
    for o in range(1, ring):
        send(l2.at[y], l2.at[y], s_l2 + o, y_dev(y_to(o)))

    for o in range(1, HIST):
        recv(da_all.at[hist_from(o)], s_da + o)
    causal_t = lax.broadcasted_iota(jnp.int32, (R, L), 1) >= h * R + lax.broadcasted_iota(
        jnp.int32, (R, L), 0
    )

    def key_pair(n, carry):
        cols = pl.ds(pl.multiple_of(n * 128, 128), 128)
        k = k_all[h, :, cols]
        v = v_all[h, :, cols]
        q = q_all[:, :, cols].reshape(L, 128)
        da = da_all[:, :, cols].reshape(L, 128)
        dks, dvs = [], []
        for e in range(2):
            s = inner_product(k * half_mask[e], q) * scale
            sigma = sigmoid(s)
            w = jnp.where(causal_t, s * sigma * (1.0 / L), 0.0).astype(BF16)
            dw = inner_product(v * half_mask[e], da)
            ds = jnp.where(
                causal_t, dw * (sigma * (1.0 + s * (1.0 - sigma))) * (scale / L), 0.0
            ).astype(BF16)
            dks.append(matmul(ds, q))
            dvs.append(matmul(w, da))
        for at, parts, place in ((W, dvs, 0), (3 * W, dks, 128)):
            grad = jnp.where(low, parts[0], parts[1]).astype(BF16).astype(F32)
            at = pl.ds(pl.multiple_of(at + n * 128, 128), 128)
            piece = (grad * silu_slope(proj[:, at])).astype(BF16)
            dpo[:, at] = piece
            dpk[lax.rem(n, 2), lax.div(n, 2), :, place : place + 128] = piece
        return carry

    lax.fori_loop(0, HEADS // 2, key_pair, 0)
    s_dk = slots(1)
    send(dpk.at[other], dpk_r, s_dk, hist_dev(sib))

    t1 = leg2(g1, t1)
    recv(dpk_r, s_dk)
    for k in range(2):
        right = jnp.concatenate([dpk[core, k], dpk_r[k]], axis=0)
        spread(matmul(normed_t, right), k, g3, 0)
    t3 = leg1(g3)
    t2 = leg2(g2, t2)

    for o in range(1, ring):
        recv(l2.at[y_from(o)], s_l2 + o)
    part = l2[0]
    for k in range(1, ring):
        part = part + l2[k]
    l3[z] = part
    s_l3 = slots(nz)
    for o in range(1, nz):
        send(l3.at[z], l3.at[z], s_l3 + o, z_dev(z_to(o)))

    grad = inner_product(dpo[...], win_ref[...])
    dtok_ref[...] = (dout[...] + norm_back(grad, nrmf[...], inverse)).astype(BF16)
    store(dtok_ref, dtok_hbm)

    t1 = leg3(g1, t1)
    t3 = leg2(g3, t3)
    t2 = leg3(g2, t2)
    t1 = leg4(g1, t1)
    t3 = leg3(g3, t3)
    for o in range(1, nz):
        recv(l3.at[z_from(o)], s_l3 + o)
    part = l3[0]
    for k in range(1, nz):
        part = part + l3[k]
    l4[core] = part
    s_l4 = slots(1)
    send(l4.at[core], l4.at[core], s_l4, hist_dev(sib))
    t2 = leg4(g2, t2)
    arrive(g1, t1)
    d_nhat = g1[6][...].reshape(NB, W)
    dneg_ref[...] = unit_back(d_nhat, n_hat, n_inv) / total_events
    store(dneg_ref, dneg_hbm)
    t3 = leg4(g3, t3)
    recv(l4.at[other], s_l4)
    loss_ref[...] = (l4[0] + l4[1])[0:1, 0:1] / total_events
    store(loss_ref, loss_hbm)
    arrive(g2, t2)
    for k in range(HIST):
        cols = slice(k * 128, (k + 1) * 128)
        dwout_ref[:, cols] = g2[6][k, :, 0:128] / total_events
        dwin_ref[:, cols] = g2[6][k, :, 128:256] / total_events
        dwin_ref[:, 2 * W + k * 128 : 2 * W + (k + 1) * 128] = g2[6][k, :, 256:384] / total_events
    store(dwout_ref, dwout_hbm)
    arrive(g3, t3)
    for k in range(HIST):
        dwin_ref[:, W + k * 128 : W + (k + 1) * 128] = g3[6][k, :, 0:128] / total_events
        dwin_ref[:, 3 * W + k * 128 : 3 * W + (k + 1) * 128] = g3[6][k, :, 128:256] / total_events
    store(dwin_ref, dwin_hbm)
    for copy in sends:
        copy.wait_send()
    for copy in stores:
        copy.wait()


def hand_over(*refs):
    sources, results, staged, sems = refs[:6], refs[6:12], refs[12:18], refs[18]
    loads = [pltpu.make_async_copy(sources[k], staged[k], sems.at[k]) for k in range(6)]
    stores = [pltpu.make_async_copy(staged[k], results[k], sems.at[6 + k]) for k in range(6)]
    for copy in loads:
        copy.start()
    for load, copy in zip(loads, stores):
        load.wait()
        copy.start()
    for copy in stores:
        copy.wait()


def local(sizes, *args):
    tokens, targets, target_ids, lengths, negatives, negative_ids, counts, w_in, w_out = args
    nz, nyh, nx = sizes
    npl = nyh * nx
    dp_size = nz * npl
    rw = W // dp_size
    ring = nx
    assert ring == 2 * nyh
    zh = nz // 2
    chunks = 2 * ring
    span = ring * zh * NH
    vmem = pltpu.VMEM
    count = 256

    def group(rows, width):
        block = ring * zh * rows
        return (
            vmem((chunks, block, width), BF16),
            vmem((2, ring, block, width), BF16),
            vmem((2, ring, zh * rows, width), BF16),
            vmem((2, ring, zh * rows, width), BF16),
            vmem((nz, rows, width), F32),
            vmem((nz, rows, width), F32),
            vmem((HIST, rows, width), F32),
        )

    scratch = [
        vmem((1, 1), F32),
        vmem((R, W), BF16),
        vmem((R, W), BF16),
        vmem((rw, 4 * W), F32),
        vmem((rw, W), F32),
        vmem((NB, W), F32),
        vmem((R, W), BF16),
        vmem((R, W), BF16),
        vmem((1, R), jnp.int32),
        pltpu.SMEM((1,), jnp.int32),
        vmem((NB, W), BF16),
        vmem((1, NB), jnp.int32),
        vmem((1, NB), jnp.int32),
        vmem((W, 4 * W), BF16),
        vmem((W, W), BF16),
        vmem((HIST, R, W), BF16),
        vmem((HIST, R, W), BF16),
        vmem((R, W), F32),
        vmem((R, 4 * W), F32),
        vmem((R, W), BF16),
        vmem((HIST, R, W), BF16),
        vmem((HIST, R, W), BF16),
        vmem((HIST, R, W), BF16),
        vmem((HEADS, R, L), F32),
        vmem((R, W), BF16),
        vmem((2, chunks, ring, zh, NH, 256), BF16),
        vmem((nz, 8, 128), jnp.int32),
        vmem((ring, 16, 128), jnp.int32),
        vmem((nyh, 16, 128), jnp.int32),
        vmem((chunks, span, 128), F32),
        vmem((chunks, span, 128), F32),
        vmem((chunks, span, 128), F32),
        vmem((chunks, span, 128), BF16),
        vmem((2, chunks, span // 2, 128), BF16),
        vmem((chunks, span // 2, 128), BF16),
        vmem((R, 2 * W), BF16),
        vmem((R, 2 * W), BF16),
        vmem((HIST, R, W), BF16),
        vmem((2, 2, R, 384), BF16),
        vmem((2, R, 384), BF16),
        vmem((2, 2, R, 256), BF16),
        vmem((2, R, 256), BF16),
        vmem((R, 4 * W), BF16),
        vmem((R, W), F32),
        group(NQ, W),
        group(rw, 384),
        group(rw, 256),
        vmem((ring, 8, 128), F32),
        vmem((ring, 8, 128), F32),
        vmem((nz, 8, 128), F32),
        vmem((2, 8, 128), F32),
        pltpu.SemaphoreType.DMA((9,)),
        pltpu.SemaphoreType.DMA((6,)),
        pltpu.SemaphoreType.DMA((count,)),
        pltpu.SemaphoreType.DMA((count,)),
    ]
    shape = jax.ShapeDtypeStruct
    shapes = [
        shape((1, 1), F32),
        shape((R, W), BF16),
        shape((R, W), BF16),
        shape((rw, 4 * W), F32),
        shape((rw, W), F32),
        shape((NB, W), F32),
    ]
    outs = pl.pallas_call(
        functools.partial(kernel, sizes, count),
        out_shape=shapes,
        in_specs=[pl.BlockSpec(memory_space=pltpu.HBM)] * 9,
        out_specs=[pl.BlockSpec(memory_space=pltpu.HBM)] * 6,
        scratch_shapes=scratch,
        compiler_params=pltpu.CompilerParams(
            collective_id=0, has_side_effects=True, vmem_limit_bytes=VMEM_LIMIT
        ),
    )(
        tokens.reshape(R, W),
        targets.reshape(R, W),
        target_ids,
        lengths,
        negatives,
        negative_ids.reshape(1, NB),
        counts.reshape(1, NB),
        w_in,
        w_out,
    )
    outs = pl.pallas_call(
        hand_over,
        out_shape=shapes,
        in_specs=[pl.BlockSpec(memory_space=pl.ANY)] * 6,
        out_specs=[pl.BlockSpec(memory_space=pl.ANY)] * 6,
        scratch_shapes=[vmem(item.shape, item.dtype) for item in shapes]
        + [pltpu.SemaphoreType.DMA((12,))],
        compiler_params=pltpu.CompilerParams(vmem_limit_bytes=VMEM_LIMIT),
    )(*outs)
    return (
        outs[0].reshape(()),
        outs[1].reshape(1, R, W),
        outs[2].reshape(1, R, W),
        outs[3],
        outs[4],
        outs[5],
    )


def solution(mesh):
    in_specs = (
        P("dp", "hist", None),
        P("dp", "hist", None),
        P("dp", "hist"),
        P("dp"),
        P("dp", None),
        P("dp"),
        P("dp"),
        P(),
        P(),
    )
    out_specs = (
        P(),
        P("dp", "hist", None),
        P("dp", "hist", None),
        P("dp", None),
        P("dp", None),
        P("dp", None),
    )
    return jax.shard_map(
        functools.partial(local, plan(mesh)),
        mesh=mesh,
        in_specs=in_specs,
        out_specs=out_specs,
        check_vma=False,
    )
```

```python
import functools

import jax
import jax.numpy as jnp
from jax import lax
from jax.experimental import pallas as pl
from jax.experimental.pallas import tpu as pltpu
from jax.sharding import PartitionSpec as P

HEADS = 8
L = 512
W = 512
HIST = 4
R = 128
NB = 32
NQ = NB // HIST
NH = NB // 2
TEMP = 0.05
MESH = pl.DeviceIdType.MESH
VMEM_LIMIT = 64 * 1024 * 1024
F32 = jnp.float32
BF16 = jnp.bfloat16


def layer_norm(values):
    centered = values - jnp.mean(values, -1, keepdims=True)
    inverse = lax.rsqrt(jnp.mean(centered * centered, -1, keepdims=True) + 1e-06)
    return (centered * inverse, inverse)


def norm_back(grad, normed, inverse):
    return inverse * (
        grad
        - jnp.mean(grad, -1, keepdims=True)
        - normed * jnp.mean(grad * normed, -1, keepdims=True)
    )


def unit_rows(values):
    inverse = lax.rsqrt(jnp.sum(values * values, -1, keepdims=True) + 1e-06)
    return (values * inverse, inverse)


def unit_back(grad, unit, inverse):
    return inverse * (grad - unit * jnp.sum(unit * grad, -1, keepdims=True))


def sigmoid(values):
    return 0.5 * jnp.tanh(0.5 * values) + 0.5


def silu_slope(values):
    sigma = sigmoid(values)
    return sigma * (1.0 + values * (1.0 - sigma))


def silu(values):
    return values * sigmoid(values)


def inner_product(left, right):
    return lax.dot_general(left, right, (((1,), (1,)), ((), ())), preferred_element_type=F32)


def matmul(left, right):
    return jnp.dot(left, right, preferred_element_type=F32)


def plan(mesh):
    dp = mesh.shape["dp"]
    if dp == 64:
        return 8, 2, 4
    return dp // 2, 1, 2


def kernel(
    sizes,
    count,
    tok_hbm,
    tgt_hbm,
    tid_hbm,
    len_hbm,
    neg_hbm,
    nid_hbm,
    ncnt_hbm,
    win_hbm,
    wout_hbm,
    loss_hbm,
    dtok_hbm,
    dtgt_hbm,
    dwin_hbm,
    dwout_hbm,
    dneg_hbm,
    loss_ref,
    dtok_ref,
    dtgt_ref,
    dwin_ref,
    dwout_ref,
    dneg_ref,
    tok_ref,
    tgt_ref,
    tid_ref,
    len_ref,
    neg_ref,
    nid_ref,
    ncnt_ref,
    win_ref,
    wout_ref,
    tok_all,
    nrm_all,
    nrmf,
    proj,
    gate,
    k_all,
    v_all,
    q_all,
    slope,
    slope_t,
    weights_t,
    attn,
    nall,
    idz,
    idx,
    idy,
    idb,
    lcb,
    ex,
    ngo,
    ngs,
    nga,
    my_own,
    my_sib,
    da_all,
    dpq,
    dpq_r,
    dpk,
    dpk_r,
    dpo,
    dout,
    g1,
    g2,
    g3,
    l1,
    l2,
    l3,
    l4,
    lsem,
    osem,
    ssem,
    rsem,
):
    nz, nyh, nx = sizes
    npl = nyh * nx
    ring = nx
    chunks = 2 * ring
    zh = nz // 2
    dp_size = nz * npl
    rw = W // dp_size
    total_events = float(dp_size * L)
    d = lax.axis_index("dp")
    h = lax.axis_index("hist")
    z = lax.div(d, npl)
    p = lax.rem(d, npl)
    yh = lax.div(p, nx)
    x = lax.rem(p, nx)
    yl = lax.div(h, 2)
    y = yh * 2 + yl
    core = lax.rem(h, 2)
    other = 1 - core
    sib = yl * 2 + other
    partner = (1 - yl) * 2 + core
    cross = (1 - yl) * 2 + other

    def hist_to(o):
        return lax.rem(h + o, HIST)

    def hist_from(o):
        return lax.rem(h + HIST - o, HIST)

    def z_to(o):
        return lax.rem(z + o, nz)

    def z_from(o):
        return lax.rem(z + nz - o, nz)

    def x_to(o):
        return lax.rem(x + o, ring)

    def x_from(o):
        return lax.rem(x + ring - o, ring)

    def y_to(o):
        return lax.rem(y + o, ring)

    def y_from(o):
        return lax.rem(y + ring - o, ring)

    def hist_dev(index):
        return {"dp": d, "hist": index}

    def z_dev(index):
        return {"dp": index * npl + p, "hist": h}

    def x_dev(index):
        return {"dp": z * npl + yh * nx + index, "hist": h}

    def y_dev(index):
        return {
            "dp": z * npl + lax.div(index, 2) * nx + x,
            "hist": lax.rem(index, 2) * 2 + core,
        }

    sends = []
    taken = [0]

    def slots(number):
        base = taken[0]
        taken[0] += number
        assert taken[0] <= count
        return base

    def send(src, dst, slot, device):
        copy = pltpu.make_async_remote_copy(
            src_ref=src,
            dst_ref=dst,
            send_sem=ssem.at[slot],
            recv_sem=rsem.at[slot],
            device_id=device,
            device_id_type=MESH,
        )
        copy.start()
        sends.append(copy)

    def recv(dst, slot):
        pltpu.make_async_remote_copy(
            src_ref=dst,
            dst_ref=dst,
            send_sem=ssem.at[slot],
            recv_sem=rsem.at[slot],
            device_id=hist_dev(sib),
            device_id_type=MESH,
        ).wait_recv()

    stores = []

    def store(src, dst):
        copy = pltpu.make_async_copy(src, dst, osem.at[len(stores)])
        copy.start()
        stores.append(copy)

    barrier = pltpu.get_barrier_semaphore()
    peers = (
        [hist_dev(hist_to(o)) for o in range(1, HIST)]
        + [x_dev(x_to(o)) for o in range(1, ring)]
        + [z_dev(z_to(o)) for o in range(1, nz)]
    )
    if nyh > 1:
        peers += [y_dev(lax.rem(yh + 1, nyh) * 2 + k) for k in range(2)]
    for device in peers:
        pl.semaphore_signal(barrier, inc=1, device_id=device, device_id_type=MESH)

    loads = []
    for k, (src, dst) in enumerate(
        (
            (neg_hbm, neg_ref),
            (nid_hbm, nid_ref),
            (ncnt_hbm, ncnt_ref),
            (tok_hbm, tok_ref),
            (win_hbm, win_ref),
            (wout_hbm, wout_ref),
            (tgt_hbm, tgt_ref),
            (tid_hbm, tid_ref),
            (len_hbm, len_ref),
        )
    ):
        copy = pltpu.make_async_copy(src, dst, lsem.at[k])
        copy.start()
        loads.append(copy)

    for k in range(3):
        loads[k].wait()
    n_hat, n_inv = unit_rows(neg_ref[...].astype(F32))
    rows16 = jnp.where(yl == 0, n_hat[:NH], n_hat[NH:])
    own16 = jnp.where(core == 0, rows16[:, :256], rows16[:, 256:]).astype(BF16)
    lane_at = lax.broadcasted_iota(jnp.int32, (1, 128), 1)
    own_lanes = (lane_at >= x * NB) & (lane_at < x * NB + NB)
    wide = [
        jnp.where(own_lanes, jnp.concatenate([ref[...]] * (128 // NB), axis=1), 0)
        for ref in (nid_ref, ncnt_ref)
    ]
    idz[z] = jnp.concatenate(wide + [jnp.zeros((6, 128), jnp.int32)], axis=0)

    pl.semaphore_wait(barrier, len(peers))

    upper = lax.div(z, zh)
    own_chunk = y + upper * (ring + x - y)
    own_place = x + upper * (y - x)
    own_z = lax.rem(z, zh)
    nall[core, own_chunk, own_place, own_z] = own16
    s_nz = slots(nz)
    s_iz = slots(nz)
    own_slot = nall.at[core, own_chunk, own_place, own_z]
    for o in range(1, nz):
        send(own_slot, own_slot, s_nz + o, z_dev(z_to(o)))
        send(idz.at[z], idz.at[z], s_iz + o, z_dev(z_to(o)))
    s_tok = slots(3)
    send(tok_hbm, tok_all.at[h], s_tok, hist_dev(partner))
    send(tok_hbm, tok_all.at[h], s_tok + 1, hist_dev(sib))

    loads[3].wait()
    loads[4].wait()
    tokf = tok_ref[...].astype(F32)
    normed_f, inverse = layer_norm(tokf)
    nrmf[...] = normed_f
    normed = normed_f.astype(BF16)
    nrm_all[h] = normed
    for blk, ref in enumerate((gate, v_all.at[h], q_all.at[h], k_all.at[h])):
        cols = slice(blk * W, (blk + 1) * W)
        part = matmul(normed, win_ref[:, cols])
        proj[:, cols] = part
        ref[...] = silu(part).astype(BF16)

    for o in range(1, nz):
        src = z_from(o)
        src_upper = lax.div(src, zh)
        recv(
            nall.at[core, y + src_upper * (ring + x - y), x + src_upper * (y - x), lax.rem(src, zh)],
            s_nz + o,
        )
        recv(idz.at[src], s_iz + o)
    idx[x] = jnp.concatenate(
        [idz[k, 0:1] for k in range(nz)]
        + [jnp.zeros((8 - nz, 128), jnp.int32)] * (nz < 8)
        + [idz[k, 1:2] for k in range(nz)]
        + [jnp.zeros((8 - nz, 128), jnp.int32)] * (nz < 8),
        axis=0,
    )
    s_n2x = slots(ring)
    s_n2y = slots(ring)
    s_ix = slots(ring)
    for o in range(1, ring):
        low_half = nall.at[core, y, x]
        high_half = nall.at[core, ring + x, y]
        send(low_half, low_half, s_n2x + o, x_dev(x_to(o)))
        send(high_half, high_half, s_n2y + o, y_dev(y_to(o)))
        send(idx.at[x], idx.at[x], s_ix + o, x_dev(x_to(o)))

    def keys_values(b):
        normed_b = layer_norm(tok_all[b].astype(F32))[0].astype(BF16)
        nrm_all[b] = normed_b
        v_all[b] = silu(matmul(normed_b, win_ref[:, W : 2 * W])).astype(BF16)
        k_all[b] = silu(matmul(normed_b, win_ref[:, 3 * W :])).astype(BF16)

    recv(tok_all.at[partner], s_tok)
    send(tok_all.at[partner], tok_all.at[partner], s_tok + 2, hist_dev(sib))
    recv(tok_all.at[sib], s_tok + 1)
    keys_values(sib)
    keys_values(partner)

    for o in range(1, ring):
        recv(nall.at[core, y, x_from(o)], s_n2x + o)
        recv(nall.at[core, ring + x, y_from(o)], s_n2y + o)
        recv(idx.at[x_from(o)], s_ix + o)
    tile = idx[0]
    for k in range(1, ring):
        tile = tile + idx[k]
    idy[yh] = tile
    s_n3y = slots(ring)
    s_n3x = slots(ring)
    s_iy = slots(1)

    def third_leg(o):
        send(nall.at[core, y], nall.at[core, y], s_n3y + o, y_dev(y_to(o)))
        send(nall.at[core, ring + x], nall.at[core, ring + x], s_n3x + o, x_dev(x_to(o)))

    for o in (1, ring - 1)[: ring - 1]:
        third_leg(o)
    if nyh > 1:
        send(idy.at[yh], idy.at[yh], s_iy, y_dev(lax.rem(yh + 1, nyh) * 2 + yl))
    s_sib = slots(2 * ring)
    for k, own in enumerate((y, ring + x)):
        send(nall.at[core, own], nall.at[core, own], s_sib + k * ring, hist_dev(sib))

    recv(tok_all.at[cross], s_tok + 2)
    keys_values(cross)

    lane = lax.broadcasted_iota(jnp.int32, (1, 128), 1)
    low = lane < 64
    half_mask = [jnp.where(low, 1.0, 0.0).astype(BF16), jnp.where(low, 0.0, 1.0).astype(BF16)]
    causal = lax.broadcasted_iota(jnp.int32, (R, L), 1) <= h * R + lax.broadcasted_iota(
        jnp.int32, (R, L), 0
    )
    scale = 0.125

    def forward_pair(n, carry):
        cols = pl.ds(pl.multiple_of(n * 128, 128), 128)
        q = q_all[h, :, cols]
        k = k_all[:, :, cols].reshape(L, 128)
        v = v_all[:, :, cols].reshape(L, 128)
        halves = []
        for e in range(2):
            s = inner_product(q * half_mask[e], k) * scale
            sigma = sigmoid(s)
            w = jnp.where(causal, s * sigma * (1.0 / L), 0.0).astype(BF16)
            slope[2 * n + e] = jnp.where(
                causal, sigma * (1.0 + s * (1.0 - sigma)) * (scale / L), 0.0
            )
            halves.append(matmul(w, v))
        attn[:, cols] = jnp.where(low, halves[0], halves[1]).astype(BF16)
        return carry

    lax.fori_loop(0, 1, forward_pair, 0)
    for o in range(2, ring - 1):
        third_leg(o)
    lax.fori_loop(1, HEADS // 2, forward_pair, 0)

    for k in range(5, 9):
        loads[k].wait()
    attn_normed, attn_inv = layer_norm(attn[...].astype(F32))
    gate_f = gate[...].astype(F32)
    mixed = (attn_normed * gate_f).astype(BF16)
    my_own[:, :W] = mixed
    output = tok_ref[...].astype(F32) + matmul(mixed, wout_ref[...])
    y_hat, y_inv = unit_rows(output)
    y_hat_b = y_hat.astype(BF16)
    my_own[:, W:] = y_hat_b
    t_hat, t_inv = unit_rows(tgt_ref[...].astype(F32))
    pos_col = jnp.sum(y_hat * t_hat, -1, keepdims=True) / TEMP
    pos_row = jnp.broadcast_to(pos_col, (R, 128)).T[0:1, :]

    if nyh > 1:
        recv(idy.at[lax.rem(yh + 1, nyh)], s_iy)
    for a in range(nyh):
        ids = idy[a, :8].astype(F32)
        logs = jnp.log(jnp.maximum(idy[a, 8:].astype(F32), 1.0))
        turned = jnp.concatenate([ids, logs, jnp.zeros((112, 128), F32)], axis=0).T
        for b in range(nx):
            for c in range(2):
                rows = turned[b * NB + c * NH : b * NB + (c + 1) * NH]
                for k in range(nz):
                    if k < zh:
                        chunk, place = 2 * a + c, b
                    else:
                        chunk, place = ring + b, 2 * a + c
                    at = pl.ds((place * zh + k % zh) * NH, NH)
                    idb[chunk, at] = jnp.broadcast_to(rows[:, k : k + 1], (NH, 128))
                    lcb[chunk, at] = jnp.broadcast_to(rows[:, 8 + k : 9 + k], (NH, 128))

    span = ring * zh * NH
    tid_row = tid_ref[...].astype(F32)

    def hand_on(o):
        for k, (src, base) in enumerate(((y_from(o), s_n3y), (ring + x_from(o), s_n3x))):
            recv(nall.at[core, src], base + o)
            send(nall.at[core, src], nall.at[core, src], s_sib + k * ring + o, hist_dev(sib))

    def logits(o, acc):
        for k, c in enumerate((y_from(o), ring + x_from(o))):
            recv(nall.at[other, c], s_sib + k * ring + o)
            lg = inner_product(nall[0, c].reshape(span, 256), y_hat_b[:, :256]) + inner_product(
                nall[1, c].reshape(span, 256), y_hat_b[:, 256:]
            )
            lg = lg * (1.0 / TEMP) - lcb[c]
            value = jnp.where(idb[c] != tid_row, jnp.exp(lg), 0.0)
            ex[c] = value
            acc = acc + jnp.sum(value.reshape(span // 8, 8, 128), 0)
        return acc

    order = [0, 1, 3, 2] if ring == 4 else list(range(ring))
    acc = jnp.zeros((8, 128), F32)
    for k in range(1, ring):
        hand_on(order[k])
        acc = logits(order[k - 1], acc)
    s_my = slots(1)
    send(my_own, my_sib, s_my, hist_dev(sib))
    acc = logits(order[-1], acc)
    total = jnp.exp(pos_row) + jnp.sum(acc, 0, keepdims=True)
    position = h * R + lax.broadcasted_iota(jnp.int32, (1, 128), 1)
    valid = jnp.where(position < len_ref[0], 1.0, 0.0)
    pg_row = valid * (jnp.exp(pos_row) / total - 1.0) / TEMP
    pg = jnp.broadcast_to(pg_row, (128, 128)).T[:, 0:1]
    scale_row = valid / (total * TEMP)

    def grad_chunk(c, carry):
        g = ex[c] * scale_row
        ngo[c] = g.astype(BF16)
        g4 = g.reshape(span // NH, 2, NQ, 128)
        for q in range(2):
            ngs[q, c] = g4[:, q].reshape(span // 2, 128).astype(BF16)
        return carry

    lax.fori_loop(0, chunks, grad_chunk, 0)
    s_ng = slots(1)
    send(ngs.at[other], nga, s_ng, hist_dev(sib))
    ng = ngo[...].reshape(dp_size * NB, 128).T
    d_hat = pg * t_hat + jnp.concatenate(
        [matmul(ng, nall[c].reshape(dp_size * NB, 256)) for c in range(2)], axis=1
    )
    d_out = unit_back(d_hat, y_hat, y_inv)
    d_out_b = d_out.astype(BF16)
    d_mixed = inner_product(d_out_b, wout_ref[...])
    da_all[h] = norm_back(d_mixed * gate_f, attn_normed, attn_inv).astype(BF16)
    s_da = slots(3)
    send(da_all.at[h], da_all.at[h], s_da, hist_dev(partner))
    send(da_all.at[h], da_all.at[h], s_da + 1, hist_dev(sib))

    def leg1(group):
        src, arrived = group[0], group[1]
        base = slots(2 * ring)
        for o in range(1, ring):
            send(src.at[y_to(o)], arrived.at[0, o], base + o, y_dev(y_to(o)))
            send(src.at[ring + x_to(o)], arrived.at[1, o], base + ring + o, x_dev(x_to(o)))
        return base

    def leg2(group, base):
        src, arrived, mid, arrived2 = group[:4]
        out = slots(2 * ring)
        for part, own in enumerate((y, ring + x)):
            total = src[own].astype(F32)
            for o in range(1, ring):
                recv(arrived.at[part, o], base + part * ring + o)
                total = total + arrived[part, o].astype(F32)
            mid[part] = total.astype(BF16).reshape(mid.shape[1:])
            for o in range(1, ring):
                to, device = (x_to(o), x_dev(x_to(o))) if part == 0 else (y_to(o), y_dev(y_to(o)))
                send(mid.at[part, to], arrived2.at[part, o], out + part * ring + o, device)
        return out

    def leg3(group, base):
        mid, arrived2, zs, zr = group[2:6]
        for part, own in enumerate((x, y)):
            total = mid[part, own].astype(F32)
            for o in range(1, ring):
                recv(arrived2.at[part, o], base + part * ring + o)
                total = total + arrived2[part, o].astype(F32)
            total = total.reshape((zh, total.shape[0] // zh, total.shape[1]))
            if zs.dtype == BF16:
                half = total.shape[2] // 2
                total = jnp.concatenate([total[:, :, :half], total[:, :, half:]], axis=1).astype(BF16)
            zs[part * zh : (part + 1) * zh] = total
        out = slots(nz)
        for o in range(1, nz):
            send(zs.at[z_to(o)], zr.at[o], out + o, z_dev(z_to(o)))
        return out

    def leg4(group, base):
        zs, zr, eh = group[4:]
        total = zs[z].astype(F32)
        for o in range(1, nz):
            recv(zr.at[o], base + o)
            total = total + zr[o].astype(F32)
        if zs.dtype == BF16:
            rows = total.shape[0] // 2
            total = jnp.concatenate([total[:rows], total[rows:]], axis=1)
        eh[h] = total
        out = slots(HIST)
        for o in range(1, HIST):
            send(eh.at[h], eh.at[h], out + o, hist_dev(hist_to(o)))
        return out

    def arrive(group, base):
        for o in range(1, HIST):
            recv(group[6].at[hist_from(o)], base + o)

    def spread(result, k, group, c0):
        width = result.shape[1]
        for a in range(nyh):
            for b in range(nx):
                for half in range(2):
                    block = jnp.concatenate(
                        [
                            result[((half * zh + j) * npl + a * nx + b) * rw :][:rw]
                            for j in range(zh)
                        ],
                        axis=0,
                    ).astype(BF16)
                    chunk, place = (2 * a + k, b) if half == 0 else (ring + b, 2 * a + k)
                    group[0][chunk, place * zh * rw : (place + 1) * zh * rw, c0 : c0 + width] = block

    for o in range(1, HIST):
        b = hist_from(o)
        q_all[b] = silu(matmul(nrm_all[b], win_ref[:, 2 * W : 3 * W])).astype(BF16)

    recv(my_sib, s_my)
    recv(nga, s_ng)

    def neg_chunk(c, carry):
        left = jnp.concatenate([ngs[core, c], nga[c]], axis=1)
        right = jnp.concatenate([my_own[:, W:], my_sib[:, W:]], axis=0)
        g1[0][c] = matmul(left, right).astype(BF16)
        return carry

    lax.fori_loop(0, chunks, neg_chunk, 0)
    t1 = leg1(g1)

    dout[...] = d_out
    dtgt_ref[...] = unit_back(pg * y_hat, t_hat, t_inv).astype(BF16)
    store(dtgt_ref, dtgt_hbm)
    d_gate = (d_mixed * attn_normed * silu_slope(proj[:, :W])).astype(BF16)
    dpo[:, :W] = d_gate
    for n in range(HIST):
        cols = slice(n * 128, (n + 1) * 128)
        dpq[n % 2, n // 2, :, 0:128] = d_out_b[:, cols]
        dpq[n % 2, n // 2, :, 128:256] = d_gate[:, cols]

    loss = jnp.sum(valid * (jnp.log(total) - pos_row), -1, keepdims=True)
    l1[x] = jnp.broadcast_to(loss, (8, 128))
    s_l1 = slots(ring)
    for o in range(1, ring):
        send(l1.at[x], l1.at[x], s_l1 + o, x_dev(x_to(o)))

    def query_pair(n, carry):
        cols = pl.ds(pl.multiple_of(n * 128, 128), 128)
        da = da_all[h, :, cols]
        k = k_all[:, :, cols].reshape(L, 128)
        v = v_all[:, :, cols].reshape(L, 128)
        halves = []
        for e in range(2):
            dw = inner_product(da * half_mask[e], v)
            halves.append(matmul((dw * slope[2 * n + e]).astype(BF16), k))
        dq = jnp.where(low, halves[0], halves[1]).astype(BF16).astype(F32)
        at = pl.ds(pl.multiple_of(2 * W + n * 128, 128), 128)
        piece = (dq * silu_slope(proj[:, at])).astype(BF16)
        dpo[:, at] = piece
        dpq[lax.rem(n, 2), lax.div(n, 2), :, 256:384] = piece
        return carry

    lax.fori_loop(0, HEADS // 2, query_pair, 0)
    s_dq = slots(1)
    send(dpq.at[other], dpq_r, s_dq, hist_dev(sib))

    mixed_t = jnp.concatenate([my_own[:, :W], my_sib[:, :W]], axis=0).T
    normed_t = jnp.concatenate([nrm_all[h], nrm_all[sib]], axis=0).T
    causal_t = lax.broadcasted_iota(jnp.int32, (R, L), 1) >= h * R + lax.broadcasted_iota(
        jnp.int32, (R, L), 0
    )

    def key_prepare(n, carry):
        cols = pl.ds(pl.multiple_of(n * 128, 128), 128)
        k = k_all[h, :, cols]
        q = q_all[:, :, cols].reshape(L, 128)
        for e in range(2):
            s = inner_product(k * half_mask[e], q) * scale
            sigma = sigmoid(s)
            weights_t[2 * n + e] = jnp.where(causal_t, s * sigma * (1.0 / L), 0.0).astype(BF16)
            slope_t[2 * n + e] = jnp.where(
                causal_t, sigma * (1.0 + s * (1.0 - sigma)) * (scale / L), 0.0
            )
        for first in (W, 3 * W):
            at = pl.ds(pl.multiple_of(first + n * 128, 128), 128)
            proj[:, at] = silu_slope(proj[:, at])
        return carry

    lax.fori_loop(0, HEADS // 2, key_prepare, 0)
    recv(da_all.at[partner], s_da)
    send(da_all.at[partner], da_all.at[partner], s_da + 2, hist_dev(sib))
    recv(dpq_r, s_dq)
    for k in range(2):
        right = jnp.concatenate([dpq[core, k], dpq_r[k]], axis=0)
        spread(matmul(mixed_t, right[:, :128]), k, g2, 0)
        spread(matmul(normed_t, right[:, 128:]), k, g2, 128)
    t2 = leg1(g2)


    for o in range(1, ring):
        recv(l1.at[x_from(o)], s_l1 + o)
    part = l1[0]
    for k in range(1, ring):
        part = part + l1[k]
    l2[y] = part
    s_l2 = slots(ring)
    for o in range(1, ring):
        send(l2.at[y], l2.at[y], s_l2 + o, y_dev(y_to(o)))

    recv(da_all.at[sib], s_da + 1)
    recv(da_all.at[cross], s_da + 2)
    def key_pair(n, carry):
        cols = pl.ds(pl.multiple_of(n * 128, 128), 128)
        v = v_all[h, :, cols]
        q = q_all[:, :, cols].reshape(L, 128)
        da = da_all[:, :, cols].reshape(L, 128)
        dks, dvs = [], []
        for e in range(2):
            dw = inner_product(v * half_mask[e], da)
            dks.append(matmul((dw * slope_t[2 * n + e]).astype(BF16), q))
            dvs.append(matmul(weights_t[2 * n + e], da))
        for at, parts, place in ((W, dvs, 0), (3 * W, dks, 128)):
            grad = jnp.where(low, parts[0], parts[1]).astype(BF16).astype(F32)
            at = pl.ds(pl.multiple_of(at + n * 128, 128), 128)
            piece = (grad * proj[:, at]).astype(BF16)
            dpo[:, at] = piece
            dpk[lax.rem(n, 2), lax.div(n, 2), :, place : place + 128] = piece
        return carry

    lax.fori_loop(0, HEADS // 2, key_pair, 0)
    s_dk = slots(1)
    send(dpk.at[other], dpk_r, s_dk, hist_dev(sib))

    t1 = leg2(g1, t1)
    recv(dpk_r, s_dk)
    for k in range(2):
        right = jnp.concatenate([dpk[core, k], dpk_r[k]], axis=0)
        spread(matmul(normed_t, right), k, g3, 0)
    t3 = leg1(g3)
    t2 = leg2(g2, t2)
    t1 = leg3(g1, t1)

    for o in range(1, ring):
        recv(l2.at[y_from(o)], s_l2 + o)
    part = l2[0]
    for k in range(1, ring):
        part = part + l2[k]
    l3[z] = part
    s_l3 = slots(nz)
    for o in range(1, nz):
        send(l3.at[z], l3.at[z], s_l3 + o, z_dev(z_to(o)))

    grad = inner_product(dpo[...], win_ref[...])
    dtok_ref[...] = (dout[...] + norm_back(grad, nrmf[...], inverse)).astype(BF16)
    store(dtok_ref, dtok_hbm)

    t3 = leg2(g3, t3)
    t2 = leg3(g2, t2)
    t1 = leg4(g1, t1)
    t3 = leg3(g3, t3)
    for o in range(1, nz):
        recv(l3.at[z_from(o)], s_l3 + o)
    part = l3[0]
    for k in range(1, nz):
        part = part + l3[k]
    l4[core] = part
    s_l4 = slots(1)
    send(l4.at[core], l4.at[core], s_l4, hist_dev(sib))
    t2 = leg4(g2, t2)
    arrive(g1, t1)
    d_nhat = g1[6][...].reshape(NB, W)
    dneg_ref[...] = unit_back(d_nhat, n_hat, n_inv) / total_events
    store(dneg_ref, dneg_hbm)
    t3 = leg4(g3, t3)
    recv(l4.at[other], s_l4)
    loss_ref[...] = (l4[0] + l4[1])[0:1, 0:1] / total_events
    store(loss_ref, loss_hbm)
    arrive(g2, t2)
    for k in range(HIST):
        cols = slice(k * 128, (k + 1) * 128)
        dwout_ref[:, cols] = g2[6][k, :, 0:128] / total_events
        dwin_ref[:, cols] = g2[6][k, :, 128:256] / total_events
        dwin_ref[:, 2 * W + k * 128 : 2 * W + (k + 1) * 128] = g2[6][k, :, 256:384] / total_events
    store(dwout_ref, dwout_hbm)
    arrive(g3, t3)
    for k in range(HIST):
        dwin_ref[:, W + k * 128 : W + (k + 1) * 128] = g3[6][k, :, 0:128] / total_events
        dwin_ref[:, 3 * W + k * 128 : 3 * W + (k + 1) * 128] = g3[6][k, :, 128:256] / total_events
    store(dwin_ref, dwin_hbm)
    for copy in sends:
        copy.wait_send()
    for copy in stores:
        copy.wait()


def hand_over(*refs):
    sources, results, staged, sems = refs[:6], refs[6:12], refs[12:18], refs[18]
    loads = [pltpu.make_async_copy(sources[k], staged[k], sems.at[k]) for k in range(6)]
    stores = [pltpu.make_async_copy(staged[k], results[k], sems.at[6 + k]) for k in range(6)]
    for copy in loads:
        copy.start()
    for load, copy in zip(loads, stores):
        load.wait()
        copy.start()
    for copy in stores:
        copy.wait()


def local(sizes, *args):
    tokens, targets, target_ids, lengths, negatives, negative_ids, counts, w_in, w_out = args
    nz, nyh, nx = sizes
    npl = nyh * nx
    dp_size = nz * npl
    rw = W // dp_size
    ring = nx
    assert ring == 2 * nyh
    zh = nz // 2
    chunks = 2 * ring
    span = ring * zh * NH
    vmem = pltpu.VMEM
    count = 256

    def group(rows, width, narrow):
        block = ring * zh * rows
        over_z = vmem((nz, 2 * rows, width // 2), BF16) if narrow else vmem((nz, rows, width), F32)
        return (
            vmem((chunks, block, width), BF16),
            vmem((2, ring, block, width), BF16),
            vmem((2, ring, zh * rows, width), BF16),
            vmem((2, ring, zh * rows, width), BF16),
            over_z,
            over_z,
            vmem((HIST, rows, width), F32),
        )

    scratch = [
        vmem((1, 1), F32),
        vmem((R, W), BF16),
        vmem((R, W), BF16),
        vmem((rw, 4 * W), F32),
        vmem((rw, W), F32),
        vmem((NB, W), F32),
        vmem((R, W), BF16),
        vmem((R, W), BF16),
        vmem((1, R), jnp.int32),
        pltpu.SMEM((1,), jnp.int32),
        vmem((NB, W), BF16),
        vmem((1, NB), jnp.int32),
        vmem((1, NB), jnp.int32),
        vmem((W, 4 * W), BF16),
        vmem((W, W), BF16),
        vmem((HIST, R, W), BF16),
        vmem((HIST, R, W), BF16),
        vmem((R, W), F32),
        vmem((R, 4 * W), F32),
        vmem((R, W), BF16),
        vmem((HIST, R, W), BF16),
        vmem((HIST, R, W), BF16),
        vmem((HIST, R, W), BF16),
        vmem((HEADS, R, L), F32),
        vmem((HEADS, R, L), F32),
        vmem((HEADS, R, L), BF16),
        vmem((R, W), BF16),
        vmem((2, chunks, ring, zh, NH, 256), BF16),
        vmem((nz, 8, 128), jnp.int32),
        vmem((ring, 16, 128), jnp.int32),
        vmem((nyh, 16, 128), jnp.int32),
        vmem((chunks, span, 128), F32),
        vmem((chunks, span, 128), F32),
        vmem((chunks, span, 128), F32),
        vmem((chunks, span, 128), BF16),
        vmem((2, chunks, span // 2, 128), BF16),
        vmem((chunks, span // 2, 128), BF16),
        vmem((R, 2 * W), BF16),
        vmem((R, 2 * W), BF16),
        vmem((HIST, R, W), BF16),
        vmem((2, 2, R, 384), BF16),
        vmem((2, R, 384), BF16),
        vmem((2, 2, R, 256), BF16),
        vmem((2, R, 256), BF16),
        vmem((R, 4 * W), BF16),
        vmem((R, W), F32),
        group(NQ, W, True),
        group(rw, 384, False),
        group(rw, 256, True),
        vmem((ring, 8, 128), F32),
        vmem((ring, 8, 128), F32),
        vmem((nz, 8, 128), F32),
        vmem((2, 8, 128), F32),
        pltpu.SemaphoreType.DMA((9,)),
        pltpu.SemaphoreType.DMA((6,)),
        pltpu.SemaphoreType.DMA((count,)),
        pltpu.SemaphoreType.DMA((count,)),
    ]
    shape = jax.ShapeDtypeStruct
    shapes = [
        shape((1, 1), F32),
        shape((R, W), BF16),
        shape((R, W), BF16),
        shape((rw, 4 * W), F32),
        shape((rw, W), F32),
        shape((NB, W), F32),
    ]
    outs = pl.pallas_call(
        functools.partial(kernel, sizes, count),
        out_shape=shapes,
        in_specs=[pl.BlockSpec(memory_space=pltpu.HBM)] * 9,
        out_specs=[pl.BlockSpec(memory_space=pltpu.HBM)] * 6,
        scratch_shapes=scratch,
        compiler_params=pltpu.CompilerParams(
            collective_id=0, has_side_effects=True, vmem_limit_bytes=VMEM_LIMIT
        ),
    )(
        tokens.reshape(R, W),
        targets.reshape(R, W),
        target_ids,
        lengths,
        negatives,
        negative_ids.reshape(1, NB),
        counts.reshape(1, NB),
        w_in,
        w_out,
    )
    outs = pl.pallas_call(
        hand_over,
        out_shape=shapes,
        in_specs=[pl.BlockSpec(memory_space=pl.ANY)] * 6,
        out_specs=[pl.BlockSpec(memory_space=pl.ANY)] * 6,
        scratch_shapes=[vmem(item.shape, item.dtype) for item in shapes]
        + [pltpu.SemaphoreType.DMA((12,))],
        compiler_params=pltpu.CompilerParams(vmem_limit_bytes=VMEM_LIMIT),
    )(*outs)
    return (
        outs[0].reshape(()),
        outs[1].reshape(1, R, W),
        outs[2].reshape(1, R, W),
        outs[3],
        outs[4],
        outs[5],
    )


def solution(mesh):
    in_specs = (
        P("dp", "hist", None),
        P("dp", "hist", None),
        P("dp", "hist"),
        P("dp"),
        P("dp", None),
        P("dp"),
        P("dp"),
        P(),
        P(),
    )
    out_specs = (
        P(),
        P("dp", "hist", None),
        P("dp", "hist", None),
        P("dp", None),
        P("dp", None),
        P("dp", None),
    )
    return jax.shard_map(
        functools.partial(local, plan(mesh)),
        mesh=mesh,
        in_specs=in_specs,
        out_specs=out_specs,
        check_vma=False,
    )
```

```python
import functools

import jax
import jax.numpy as jnp
from jax import lax
from jax.experimental import pallas as pl
from jax.experimental.pallas import tpu as pltpu
from jax.sharding import PartitionSpec as P

HEADS = 8
L = 512
W = 512
HIST = 4
R = 128
NB = 32
NQ = NB // HIST
NH = NB // 2
TEMP = 0.05
MESH = pl.DeviceIdType.MESH
VMEM_LIMIT = 64 * 1024 * 1024
F32 = jnp.float32
BF16 = jnp.bfloat16


def layer_norm(values):
    centered = values - jnp.mean(values, -1, keepdims=True)
    inverse = lax.rsqrt(jnp.mean(centered * centered, -1, keepdims=True) + 1e-06)
    return (centered * inverse, inverse)


def norm_back(grad, normed, inverse):
    return inverse * (
        grad
        - jnp.mean(grad, -1, keepdims=True)
        - normed * jnp.mean(grad * normed, -1, keepdims=True)
    )


def unit_rows(values):
    inverse = lax.rsqrt(jnp.sum(values * values, -1, keepdims=True) + 1e-06)
    return (values * inverse, inverse)


def unit_back(grad, unit, inverse):
    return inverse * (grad - unit * jnp.sum(unit * grad, -1, keepdims=True))


def sigmoid(values):
    return 0.5 * jnp.tanh(0.5 * values) + 0.5


def silu_slope(values):
    sigma = sigmoid(values)
    return sigma * (1.0 + values * (1.0 - sigma))


def silu(values):
    return values * sigmoid(values)


def inner_product(left, right):
    return lax.dot_general(left, right, (((1,), (1,)), ((), ())), preferred_element_type=F32)


def matmul(left, right):
    return jnp.dot(left, right, preferred_element_type=F32)


def plan(mesh):
    dp = mesh.shape["dp"]
    if dp == 64:
        return 8, 2, 4
    return dp // 2, 1, 2


def kernel(
    sizes,
    count,
    tok_hbm,
    tgt_hbm,
    tid_hbm,
    len_hbm,
    neg_hbm,
    nid_hbm,
    ncnt_hbm,
    win_hbm,
    wout_hbm,
    loss_hbm,
    dtok_hbm,
    dtgt_hbm,
    dwin_hbm,
    dwout_hbm,
    dneg_hbm,
    loss_ref,
    dtok_ref,
    dtgt_ref,
    dwin_ref,
    dwout_ref,
    dneg_ref,
    tok_ref,
    tgt_ref,
    tid_ref,
    len_ref,
    neg_ref,
    nid_ref,
    ncnt_ref,
    win_ref,
    wout_ref,
    tok_all,
    nrm_all,
    nrmf,
    proj,
    gate,
    k_all,
    v_all,
    q_all,
    slope,
    slope_t,
    weights_t,
    attn,
    nall,
    idz,
    idx,
    idy,
    idb,
    lcb,
    ex,
    ngo,
    ngs,
    nga,
    my_own,
    my_sib,
    da_all,
    dpq,
    dpq_r,
    dpk,
    dpk_r,
    dpo,
    dout,
    g1,
    gz,
    g2,
    g3,
    l1,
    l2,
    l3,
    l4,
    lsem,
    osem,
    ssem,
    rsem,
):
    nz, nyh, nx = sizes
    npl = nyh * nx
    ring = nx
    chunks = 2 * ring
    zh = nz // 2
    dp_size = nz * npl
    rw = W // dp_size
    total_events = float(dp_size * L)
    d = lax.axis_index("dp")
    h = lax.axis_index("hist")
    z = lax.div(d, npl)
    p = lax.rem(d, npl)
    yh = lax.div(p, nx)
    x = lax.rem(p, nx)
    yl = lax.div(h, 2)
    y = yh * 2 + yl
    core = lax.rem(h, 2)
    other = 1 - core
    sib = yl * 2 + other
    partner = (1 - yl) * 2 + core
    cross = (1 - yl) * 2 + other

    def hist_to(o):
        return lax.rem(h + o, HIST)

    def hist_from(o):
        return lax.rem(h + HIST - o, HIST)

    def z_to(o):
        return lax.rem(z + o, nz)

    def z_from(o):
        return lax.rem(z + nz - o, nz)

    def x_to(o):
        return lax.rem(x + o, ring)

    def x_from(o):
        return lax.rem(x + ring - o, ring)

    def y_to(o):
        return lax.rem(y + o, ring)

    def y_from(o):
        return lax.rem(y + ring - o, ring)

    def hist_dev(index):
        return {"dp": d, "hist": index}

    def z_dev(index):
        return {"dp": index * npl + p, "hist": h}

    def x_dev(index):
        return {"dp": z * npl + yh * nx + index, "hist": h}

    def y_dev(index):
        return {
            "dp": z * npl + lax.div(index, 2) * nx + x,
            "hist": lax.rem(index, 2) * 2 + core,
        }

    sends = []
    taken = [0]

    def slots(number):
        base = taken[0]
        taken[0] += number
        assert taken[0] <= count
        return base

    def send(src, dst, slot, device):
        copy = pltpu.make_async_remote_copy(
            src_ref=src,
            dst_ref=dst,
            send_sem=ssem.at[slot],
            recv_sem=rsem.at[slot],
            device_id=device,
            device_id_type=MESH,
        )
        copy.start()
        sends.append(copy)

    def recv(dst, slot):
        pltpu.make_async_remote_copy(
            src_ref=dst,
            dst_ref=dst,
            send_sem=ssem.at[slot],
            recv_sem=rsem.at[slot],
            device_id=hist_dev(sib),
            device_id_type=MESH,
        ).wait_recv()

    stores = []

    def store(src, dst):
        copy = pltpu.make_async_copy(src, dst, osem.at[len(stores)])
        copy.start()
        stores.append(copy)

    barrier = pltpu.get_barrier_semaphore()
    peers = (
        [hist_dev(hist_to(o)) for o in range(1, HIST)]
        + [x_dev(x_to(o)) for o in range(1, ring)]
        + [z_dev(z_to(o)) for o in range(1, nz)]
    )
    if nyh > 1:
        peers += [y_dev(lax.rem(yh + 1, nyh) * 2 + k) for k in range(2)]
    for device in peers:
        pl.semaphore_signal(barrier, inc=1, device_id=device, device_id_type=MESH)

    loads = []
    for k, (src, dst) in enumerate(
        (
            (neg_hbm, neg_ref),
            (nid_hbm, nid_ref),
            (ncnt_hbm, ncnt_ref),
            (tok_hbm, tok_ref),
            (win_hbm, win_ref),
            (wout_hbm, wout_ref),
            (tgt_hbm, tgt_ref),
            (tid_hbm, tid_ref),
            (len_hbm, len_ref),
        )
    ):
        copy = pltpu.make_async_copy(src, dst, lsem.at[k])
        copy.start()
        loads.append(copy)

    for k in range(3):
        loads[k].wait()
    n_hat, n_inv = unit_rows(neg_ref[...].astype(F32))
    rows16 = jnp.where(yl == 0, n_hat[:NH], n_hat[NH:])
    own16 = jnp.where(core == 0, rows16[:, :256], rows16[:, 256:]).astype(BF16)
    lane_at = lax.broadcasted_iota(jnp.int32, (1, 128), 1)
    own_lanes = (lane_at >= x * NB) & (lane_at < x * NB + NB)
    wide = [
        jnp.where(own_lanes, jnp.concatenate([ref[...]] * (128 // NB), axis=1), 0)
        for ref in (nid_ref, ncnt_ref)
    ]
    idz[z] = jnp.concatenate(wide + [jnp.zeros((6, 128), jnp.int32)], axis=0)

    pl.semaphore_wait(barrier, len(peers))

    upper = lax.div(z, zh)
    own_chunk = y + upper * (ring + x - y)
    own_place = x + upper * (y - x)
    own_z = lax.rem(z, zh)
    nall[core, own_chunk, own_place, own_z] = own16
    s_nz = slots(nz)
    s_iz = slots(nz)
    own_slot = nall.at[core, own_chunk, own_place, own_z]
    for o in range(1, nz):
        send(own_slot, own_slot, s_nz + o, z_dev(z_to(o)))
        send(idz.at[z], idz.at[z], s_iz + o, z_dev(z_to(o)))
    s_tok = slots(3)
    send(tok_hbm, tok_all.at[h], s_tok, hist_dev(partner))
    send(tok_hbm, tok_all.at[h], s_tok + 1, hist_dev(sib))

    loads[3].wait()
    loads[4].wait()
    tokf = tok_ref[...].astype(F32)
    normed_f, inverse = layer_norm(tokf)
    nrmf[...] = normed_f
    normed = normed_f.astype(BF16)
    nrm_all[h] = normed
    for blk, ref in enumerate((gate, v_all.at[h], q_all.at[h], k_all.at[h])):
        cols = slice(blk * W, (blk + 1) * W)
        part = matmul(normed, win_ref[:, cols])
        proj[:, cols] = part
        ref[...] = silu(part).astype(BF16)

    for o in range(1, nz):
        src = z_from(o)
        src_upper = lax.div(src, zh)
        recv(
            nall.at[core, y + src_upper * (ring + x - y), x + src_upper * (y - x), lax.rem(src, zh)],
            s_nz + o,
        )
        recv(idz.at[src], s_iz + o)
    idx[x] = jnp.concatenate(
        [idz[k, 0:1] for k in range(nz)]
        + [jnp.zeros((8 - nz, 128), jnp.int32)] * (nz < 8)
        + [idz[k, 1:2] for k in range(nz)]
        + [jnp.zeros((8 - nz, 128), jnp.int32)] * (nz < 8),
        axis=0,
    )
    s_n2x = slots(ring)
    s_n2y = slots(ring)
    s_ix = slots(ring)
    for o in range(1, ring):
        low_half = nall.at[core, y, x]
        high_half = nall.at[core, ring + x, y]
        send(low_half, low_half, s_n2x + o, x_dev(x_to(o)))
        send(high_half, high_half, s_n2y + o, y_dev(y_to(o)))
        send(idx.at[x], idx.at[x], s_ix + o, x_dev(x_to(o)))

    def keys_values(b):
        normed_b = layer_norm(tok_all[b].astype(F32))[0].astype(BF16)
        nrm_all[b] = normed_b
        v_all[b] = silu(matmul(normed_b, win_ref[:, W : 2 * W])).astype(BF16)
        k_all[b] = silu(matmul(normed_b, win_ref[:, 3 * W :])).astype(BF16)

    recv(tok_all.at[partner], s_tok)
    send(tok_all.at[partner], tok_all.at[partner], s_tok + 2, hist_dev(sib))
    recv(tok_all.at[sib], s_tok + 1)
    keys_values(sib)
    keys_values(partner)

    for o in range(1, ring):
        recv(nall.at[core, y, x_from(o)], s_n2x + o)
        recv(nall.at[core, ring + x, y_from(o)], s_n2y + o)
        recv(idx.at[x_from(o)], s_ix + o)
    tile = idx[0]
    for k in range(1, ring):
        tile = tile + idx[k]
    idy[yh] = tile
    s_n3y = slots(ring)
    s_n3x = slots(ring)
    s_iy = slots(1)

    def third_leg(o):
        send(nall.at[core, y], nall.at[core, y], s_n3y + o, y_dev(y_to(o)))
        send(nall.at[core, ring + x], nall.at[core, ring + x], s_n3x + o, x_dev(x_to(o)))

    for o in (1, ring - 1)[: ring - 1]:
        third_leg(o)
    if nyh > 1:
        send(idy.at[yh], idy.at[yh], s_iy, y_dev(lax.rem(yh + 1, nyh) * 2 + yl))
    s_sib = slots(2 * ring)
    for k, own in enumerate((y, ring + x)):
        send(nall.at[core, own], nall.at[core, own], s_sib + k * ring, hist_dev(sib))

    recv(tok_all.at[cross], s_tok + 2)
    keys_values(cross)

    lane = lax.broadcasted_iota(jnp.int32, (1, 128), 1)
    low = lane < 64
    half_mask = [jnp.where(low, 1.0, 0.0).astype(BF16), jnp.where(low, 0.0, 1.0).astype(BF16)]
    causal = lax.broadcasted_iota(jnp.int32, (R, L), 1) <= h * R + lax.broadcasted_iota(
        jnp.int32, (R, L), 0
    )
    scale = 0.125

    def forward_pair(n, carry):
        cols = pl.ds(pl.multiple_of(n * 128, 128), 128)
        q = q_all[h, :, cols]
        k = k_all[:, :, cols].reshape(L, 128)
        v = v_all[:, :, cols].reshape(L, 128)
        halves = []
        for e in range(2):
            s = inner_product(q * half_mask[e], k) * scale
            sigma = sigmoid(s)
            w = jnp.where(causal, s * sigma * (1.0 / L), 0.0).astype(BF16)
            slope[2 * n + e] = jnp.where(
                causal, sigma * (1.0 + s * (1.0 - sigma)) * (scale / L), 0.0
            )
            halves.append(matmul(w, v))
        attn[:, cols] = jnp.where(low, halves[0], halves[1]).astype(BF16)
        return carry

    lax.fori_loop(0, 1, forward_pair, 0)
    for o in range(2, ring - 1):
        third_leg(o)
    lax.fori_loop(1, HEADS // 2, forward_pair, 0)

    for k in range(5, 9):
        loads[k].wait()
    attn_normed, attn_inv = layer_norm(attn[...].astype(F32))
    gate_f = gate[...].astype(F32)
    mixed = (attn_normed * gate_f).astype(BF16)
    my_own[:, :W] = mixed
    output = tok_ref[...].astype(F32) + matmul(mixed, wout_ref[...])
    y_hat, y_inv = unit_rows(output)
    y_hat_b = y_hat.astype(BF16)
    my_own[:, W:] = y_hat_b
    t_hat, t_inv = unit_rows(tgt_ref[...].astype(F32))
    pos_col = jnp.sum(y_hat * t_hat, -1, keepdims=True) / TEMP
    pos_row = jnp.broadcast_to(pos_col, (R, 128)).T[0:1, :]

    if nyh > 1:
        recv(idy.at[lax.rem(yh + 1, nyh)], s_iy)
    for a in range(nyh):
        ids = idy[a, :8].astype(F32)
        logs = jnp.log(jnp.maximum(idy[a, 8:].astype(F32), 1.0))
        turned = jnp.concatenate([ids, logs, jnp.zeros((112, 128), F32)], axis=0).T
        for b in range(nx):
            for c in range(2):
                rows = turned[b * NB + c * NH : b * NB + (c + 1) * NH]
                for k in range(nz):
                    if k < zh:
                        chunk, place = 2 * a + c, b
                    else:
                        chunk, place = ring + b, 2 * a + c
                    at = pl.ds((place * zh + k % zh) * NH, NH)
                    idb[chunk, at] = jnp.broadcast_to(rows[:, k : k + 1], (NH, 128))
                    lcb[chunk, at] = jnp.broadcast_to(rows[:, 8 + k : 9 + k], (NH, 128))

    span = ring * zh * NH
    tid_row = tid_ref[...].astype(F32)

    def hand_on(o):
        for k, (src, base) in enumerate(((y_from(o), s_n3y), (ring + x_from(o), s_n3x))):
            recv(nall.at[core, src], base + o)
            send(nall.at[core, src], nall.at[core, src], s_sib + k * ring + o, hist_dev(sib))

    def logits(o, acc):
        for k, c in enumerate((y_from(o), ring + x_from(o))):
            recv(nall.at[other, c], s_sib + k * ring + o)
            lg = inner_product(nall[0, c].reshape(span, 256), y_hat_b[:, :256]) + inner_product(
                nall[1, c].reshape(span, 256), y_hat_b[:, 256:]
            )
            lg = lg * (1.0 / TEMP) - lcb[c]
            value = jnp.where(idb[c] != tid_row, jnp.exp(lg), 0.0)
            ex[c] = value
            acc = acc + jnp.sum(value.reshape(span // 8, 8, 128), 0)
        return acc

    order = [0, 1, 3, 2] if ring == 4 else list(range(ring))
    acc = jnp.zeros((8, 128), F32)
    for k in range(1, ring):
        hand_on(order[k])
        acc = logits(order[k - 1], acc)
    s_my = slots(1)
    send(my_own, my_sib, s_my, hist_dev(sib))
    acc = logits(order[-1], acc)
    total = jnp.exp(pos_row) + jnp.sum(acc, 0, keepdims=True)
    position = h * R + lax.broadcasted_iota(jnp.int32, (1, 128), 1)
    valid = jnp.where(position < len_ref[0], 1.0, 0.0)
    pg_row = valid * (jnp.exp(pos_row) / total - 1.0) / TEMP
    pg = jnp.broadcast_to(pg_row, (128, 128)).T[:, 0:1]
    scale_row = valid / (total * TEMP)

    def grad_chunk(c, carry):
        g = ex[c] * scale_row
        ngo[c] = g.astype(BF16)
        g4 = g.reshape(span // NH, 2, NQ, 128)
        for q in range(2):
            ngs[q, c] = g4[:, q].reshape(span // 2, 128).astype(BF16)
        return carry

    lax.fori_loop(0, chunks, grad_chunk, 0)
    s_ng = slots(1)
    send(ngs.at[other], nga, s_ng, hist_dev(sib))
    ng = ngo[...].reshape(dp_size * NB, 128).T
    d_hat = pg * t_hat + jnp.concatenate(
        [matmul(ng, nall[c].reshape(dp_size * NB, 256)) for c in range(2)], axis=1
    )
    d_out = unit_back(d_hat, y_hat, y_inv)
    d_out_b = d_out.astype(BF16)
    d_mixed = inner_product(d_out_b, wout_ref[...])
    da_all[h] = norm_back(d_mixed * gate_f, attn_normed, attn_inv).astype(BF16)
    s_da = slots(3)
    send(da_all.at[h], da_all.at[h], s_da, hist_dev(partner))
    send(da_all.at[h], da_all.at[h], s_da + 1, hist_dev(sib))

    def leg1(group):
        src, arrived = group[0], group[1]
        base = slots(2 * ring)
        for o in range(1, ring):
            send(src.at[y_to(o)], arrived.at[0, o], base + o, y_dev(y_to(o)))
            send(src.at[ring + x_to(o)], arrived.at[1, o], base + ring + o, x_dev(x_to(o)))
        return base

    def leg2(group, base):
        src, arrived, mid, arrived2 = group[:4]
        out = slots(2 * ring)
        for part, own in enumerate((y, ring + x)):
            total = src[own].astype(F32)
            for o in range(1, ring):
                recv(arrived.at[part, o], base + part * ring + o)
                total = total + arrived[part, o].astype(F32)
            mid[part] = total.astype(BF16).reshape(mid.shape[1:])
            for o in range(1, ring):
                to, device = (x_to(o), x_dev(x_to(o))) if part == 0 else (y_to(o), y_dev(y_to(o)))
                send(mid.at[part, to], arrived2.at[part, o], out + part * ring + o, device)
        return out

    def leg3(group, base):
        mid, arrived2, zs, zr = group[2:6]
        for part, own in enumerate((x, y)):
            total = mid[part, own].astype(F32)
            for o in range(1, ring):
                recv(arrived2.at[part, o], base + part * ring + o)
                total = total + arrived2[part, o].astype(F32)
            total = total.reshape((zh, total.shape[0] // zh, total.shape[1]))
            if zs.dtype == BF16:
                half = total.shape[2] // 2
                total = jnp.concatenate([total[:, :, :half], total[:, :, half:]], axis=1).astype(BF16)
            zs[part * zh : (part + 1) * zh] = total
        out = slots(nz)
        for o in range(1, nz):
            send(zs.at[z_to(o)], zr.at[o], out + o, z_dev(z_to(o)))
        return out

    def leg4(group, base):
        zs, zr, eh = group[4:]
        total = zs[z].astype(F32)
        for o in range(1, nz):
            recv(zr.at[o], base + o)
            total = total + zr[o].astype(F32)
        if zs.dtype == BF16:
            rows = total.shape[0] // 2
            total = jnp.concatenate([total[:rows], total[rows:]], axis=1)
        eh[h] = total
        out = slots(HIST)
        for o in range(1, HIST):
            send(eh.at[h], eh.at[h], out + o, hist_dev(hist_to(o)))
        return out

    def arrive(group, base):
        for o in range(1, HIST):
            recv(group[6].at[hist_from(o)], base + o)

    def spread(result, k, group, c0):
        width = result.shape[1]
        for a in range(nyh):
            for b in range(nx):
                for half in range(2):
                    block = jnp.concatenate(
                        [
                            result[((half * zh + j) * npl + a * nx + b) * rw :][:rw]
                            for j in range(zh)
                        ],
                        axis=0,
                    ).astype(BF16)
                    chunk, place = (2 * a + k, b) if half == 0 else (ring + b, 2 * a + k)
                    group[0][chunk, place * zh * rw : (place + 1) * zh * rw, c0 : c0 + width] = block

    for o in range(1, HIST):
        b = hist_from(o)
        q_all[b] = silu(matmul(nrm_all[b], win_ref[:, 2 * W : 3 * W])).astype(BF16)

    recv(my_sib, s_my)
    recv(nga, s_ng)

    right = jnp.concatenate([my_own[:, W:], my_sib[:, W:]], axis=0)
    zsrc, zgot, amid, agot, bmid, bgot, ez = gz

    def neg_chunk(c, part, index):
        left = jnp.concatenate([ngs[core, c], nga[c]], axis=1)
        result = matmul(left, right)
        g1[0][c] = result[:, :256].astype(BF16)
        for j in range(zh):
            block = jnp.concatenate(
                [result[(k * zh + j) * NQ : (k * zh + j + 1) * NQ, 256:] for k in range(ring)], axis=0
            )
            zsrc[part * zh + j, index] = block.astype(BF16)

    t1 = slots(2 * ring)
    for o in order[1:] + [0]:
        for part, index in enumerate((y_to(o), x_to(o))):
            c = part * ring + index
            neg_chunk(c, part, index)
            if o:
                device = y_dev(index) if part == 0 else x_dev(index)
                send(g1[0].at[c], g1[1].at[part, o], t1 + part * ring + o, device)
    s_zz = slots(nz)
    for o in range(1, nz):
        send(zsrc.at[z_to(o)], zgot.at[o], s_zz + o, z_dev(z_to(o)))

    def turn(low_index, high_index):
        return low_index + upper * (high_index - low_index)

    def turn_dev(low_dev, high_dev):
        return {name: turn(low_dev[name], high_dev[name]) for name in ("dp", "hist")}

    def z_first_leg2():
        total = zsrc[z].astype(F32)
        for o in range(1, nz):
            recv(zgot.at[o], s_zz + o)
            total = total + zgot[o].astype(F32)
        amid[...] = total.astype(BF16)
        out = slots(ring)
        for o in range(1, ring):
            to = turn(y_to(o), x_to(o))
            send(amid.at[to], agot.at[o], out + o, turn_dev(y_dev(y_to(o)), x_dev(x_to(o))))
        return out

    def z_first_leg3(base):
        total = amid[turn(y, x)].astype(F32)
        for o in range(1, ring):
            recv(agot.at[o], base + o)
            total = total + agot[o].astype(F32)
        total = total.reshape(ring, NQ, 256)
        bmid[...] = jnp.concatenate([total[:, :, :128], total[:, :, 128:]], axis=1).astype(BF16)
        out = slots(ring)
        for o in range(1, ring):
            to = turn(x_to(o), y_to(o))
            send(bmid.at[to], bgot.at[o], out + o, turn_dev(x_dev(x_to(o)), y_dev(y_to(o))))
        return out

    def z_first_leg4(base):
        total = bmid[turn(x, y)].astype(F32)
        for o in range(1, ring):
            recv(bgot.at[o], base + o)
            total = total + bgot[o].astype(F32)
        ez[h] = jnp.concatenate([total[:NQ], total[NQ:]], axis=1)
        out = slots(HIST)
        for o in range(1, HIST):
            send(ez.at[h], ez.at[h], out + o, hist_dev(hist_to(o)))
        return out


    dout[...] = d_out
    dtgt_ref[...] = unit_back(pg * y_hat, t_hat, t_inv).astype(BF16)
    store(dtgt_ref, dtgt_hbm)
    d_gate = (d_mixed * attn_normed * silu_slope(proj[:, :W])).astype(BF16)
    dpo[:, :W] = d_gate
    for n in range(HIST):
        cols = slice(n * 128, (n + 1) * 128)
        dpq[n % 2, n // 2, :, 0:128] = d_out_b[:, cols]
        dpq[n % 2, n // 2, :, 128:256] = d_gate[:, cols]

    loss = jnp.sum(valid * (jnp.log(total) - pos_row), -1, keepdims=True)
    l1[x] = jnp.broadcast_to(loss, (8, 128))
    s_l1 = slots(ring)
    for o in range(1, ring):
        send(l1.at[x], l1.at[x], s_l1 + o, x_dev(x_to(o)))

    def query_pair(n, carry):
        cols = pl.ds(pl.multiple_of(n * 128, 128), 128)
        da = da_all[h, :, cols]
        k = k_all[:, :, cols].reshape(L, 128)
        v = v_all[:, :, cols].reshape(L, 128)
        halves = []
        for e in range(2):
            dw = inner_product(da * half_mask[e], v)
            halves.append(matmul((dw * slope[2 * n + e]).astype(BF16), k))
        dq = jnp.where(low, halves[0], halves[1]).astype(BF16).astype(F32)
        at = pl.ds(pl.multiple_of(2 * W + n * 128, 128), 128)
        piece = (dq * silu_slope(proj[:, at])).astype(BF16)
        dpo[:, at] = piece
        dpq[lax.rem(n, 2), lax.div(n, 2), :, 256:384] = piece
        return carry

    lax.fori_loop(0, HEADS // 2, query_pair, 0)
    s_dq = slots(1)
    send(dpq.at[other], dpq_r, s_dq, hist_dev(sib))

    mixed_t = jnp.concatenate([my_own[:, :W], my_sib[:, :W]], axis=0).T
    normed_t = jnp.concatenate([nrm_all[h], nrm_all[sib]], axis=0).T
    causal_t = lax.broadcasted_iota(jnp.int32, (R, L), 1) >= h * R + lax.broadcasted_iota(
        jnp.int32, (R, L), 0
    )

    def key_prepare(n, carry):
        cols = pl.ds(pl.multiple_of(n * 128, 128), 128)
        k = k_all[h, :, cols]
        q = q_all[:, :, cols].reshape(L, 128)
        for e in range(2):
            s = inner_product(k * half_mask[e], q) * scale
            sigma = sigmoid(s)
            weights_t[2 * n + e] = jnp.where(causal_t, s * sigma * (1.0 / L), 0.0).astype(BF16)
            slope_t[2 * n + e] = jnp.where(
                causal_t, sigma * (1.0 + s * (1.0 - sigma)) * (scale / L), 0.0
            )
        for first in (W, 3 * W):
            at = pl.ds(pl.multiple_of(first + n * 128, 128), 128)
            proj[:, at] = silu_slope(proj[:, at])
        return carry

    lax.fori_loop(0, HEADS // 2, key_prepare, 0)
    recv(da_all.at[partner], s_da)
    send(da_all.at[partner], da_all.at[partner], s_da + 2, hist_dev(sib))
    recv(dpq_r, s_dq)
    for k in range(2):
        right = jnp.concatenate([dpq[core, k], dpq_r[k]], axis=0)
        spread(matmul(mixed_t, right[:, :128]), k, g2, 0)
        spread(matmul(normed_t, right[:, 128:]), k, g2, 128)
    t2 = leg1(g2)


    for o in range(1, ring):
        recv(l1.at[x_from(o)], s_l1 + o)
    part = l1[0]
    for k in range(1, ring):
        part = part + l1[k]
    l2[y] = part
    s_l2 = slots(ring)
    for o in range(1, ring):
        send(l2.at[y], l2.at[y], s_l2 + o, y_dev(y_to(o)))

    recv(da_all.at[sib], s_da + 1)
    recv(da_all.at[cross], s_da + 2)
    def key_pair(n, carry):
        cols = pl.ds(pl.multiple_of(n * 128, 128), 128)
        v = v_all[h, :, cols]
        q = q_all[:, :, cols].reshape(L, 128)
        da = da_all[:, :, cols].reshape(L, 128)
        dks, dvs = [], []
        for e in range(2):
            dw = inner_product(v * half_mask[e], da)
            dks.append(matmul((dw * slope_t[2 * n + e]).astype(BF16), q))
            dvs.append(matmul(weights_t[2 * n + e], da))
        for at, parts, place in ((W, dvs, 0), (3 * W, dks, 128)):
            grad = jnp.where(low, parts[0], parts[1]).astype(BF16).astype(F32)
            at = pl.ds(pl.multiple_of(at + n * 128, 128), 128)
            piece = (grad * proj[:, at]).astype(BF16)
            dpo[:, at] = piece
            dpk[lax.rem(n, 2), lax.div(n, 2), :, place : place + 128] = piece
        return carry

    lax.fori_loop(0, HEADS // 2, key_pair, 0)
    s_dk = slots(1)
    send(dpk.at[other], dpk_r, s_dk, hist_dev(sib))

    recv(dpk_r, s_dk)
    for k in range(2):
        right = jnp.concatenate([dpk[core, k], dpk_r[k]], axis=0)
        spread(matmul(normed_t, right), k, g3, 0)
    t3 = leg1(g3)
    t1 = leg2(g1, t1)
    t2 = leg2(g2, t2)
    for o in range(1, ring):
        recv(l2.at[y_from(o)], s_l2 + o)
    part = l2[0]
    for k in range(1, ring):
        part = part + l2[k]
    l3[z] = part
    s_l3 = slots(nz)
    for o in range(1, nz):
        send(l3.at[z], l3.at[z], s_l3 + o, z_dev(z_to(o)))

    grad = inner_product(dpo[...], win_ref[...])
    dtok_ref[...] = (dout[...] + norm_back(grad, nrmf[...], inverse)).astype(BF16)
    store(dtok_ref, dtok_hbm)

    t3 = leg2(g3, t3)
    tz = z_first_leg2()
    t1 = leg3(g1, t1)
    t2 = leg3(g2, t2)
    t3 = leg3(g3, t3)
    tz = z_first_leg3(tz)
    for o in range(1, nz):
        recv(l3.at[z_from(o)], s_l3 + o)
    part = l3[0]
    for k in range(1, nz):
        part = part + l3[k]
    l4[core] = part
    s_l4 = slots(1)
    send(l4.at[core], l4.at[core], s_l4, hist_dev(sib))
    t1 = leg4(g1, t1)
    t2 = leg4(g2, t2)
    tz = z_first_leg4(tz)
    t3 = leg4(g3, t3)
    recv(l4.at[other], s_l4)
    loss_ref[...] = (l4[0] + l4[1])[0:1, 0:1] / total_events
    store(loss_ref, loss_hbm)
    arrive(g1, t1)
    for o in range(1, HIST):
        recv(ez.at[hist_from(o)], tz + o)
    d_nhat = jnp.concatenate([g1[6][...].reshape(NB, 256), ez[...].reshape(NB, 256)], axis=1)
    dneg_ref[...] = unit_back(d_nhat, n_hat, n_inv) / total_events
    store(dneg_ref, dneg_hbm)
    arrive(g2, t2)
    for k in range(HIST):
        cols = slice(k * 128, (k + 1) * 128)
        dwout_ref[:, cols] = g2[6][k, :, 0:128] / total_events
        dwin_ref[:, cols] = g2[6][k, :, 128:256] / total_events
        dwin_ref[:, 2 * W + k * 128 : 2 * W + (k + 1) * 128] = g2[6][k, :, 256:384] / total_events
    store(dwout_ref, dwout_hbm)
    arrive(g3, t3)
    for k in range(HIST):
        dwin_ref[:, W + k * 128 : W + (k + 1) * 128] = g3[6][k, :, 0:128] / total_events
        dwin_ref[:, 3 * W + k * 128 : 3 * W + (k + 1) * 128] = g3[6][k, :, 128:256] / total_events
    store(dwin_ref, dwin_hbm)
    for copy in sends:
        copy.wait_send()
    for copy in stores:
        copy.wait()


def hand_over(*refs):
    sources, results, staged, sems = refs[:6], refs[6:12], refs[12:18], refs[18]
    loads = [pltpu.make_async_copy(sources[k], staged[k], sems.at[k]) for k in range(6)]
    stores = [pltpu.make_async_copy(staged[k], results[k], sems.at[6 + k]) for k in range(6)]
    for copy in loads:
        copy.start()
    for load, copy in zip(loads, stores):
        load.wait()
        copy.start()
    for copy in stores:
        copy.wait()


def local(sizes, *args):
    tokens, targets, target_ids, lengths, negatives, negative_ids, counts, w_in, w_out = args
    nz, nyh, nx = sizes
    npl = nyh * nx
    dp_size = nz * npl
    rw = W // dp_size
    ring = nx
    assert ring == 2 * nyh
    zh = nz // 2
    chunks = 2 * ring
    span = ring * zh * NH
    vmem = pltpu.VMEM
    count = 256

    def group(rows, width, narrow):
        block = ring * zh * rows
        over_z = vmem((nz, 2 * rows, width // 2), BF16) if narrow else vmem((nz, rows, width), F32)
        return (
            vmem((chunks, block, width), BF16),
            vmem((2, ring, block, width), BF16),
            vmem((2, ring, zh * rows, width), BF16),
            vmem((2, ring, zh * rows, width), BF16),
            over_z,
            over_z,
            vmem((HIST, rows, width), F32),
        )

    scratch = [
        vmem((1, 1), F32),
        vmem((R, W), BF16),
        vmem((R, W), BF16),
        vmem((rw, 4 * W), F32),
        vmem((rw, W), F32),
        vmem((NB, W), F32),
        vmem((R, W), BF16),
        vmem((R, W), BF16),
        vmem((1, R), jnp.int32),
        pltpu.SMEM((1,), jnp.int32),
        vmem((NB, W), BF16),
        vmem((1, NB), jnp.int32),
        vmem((1, NB), jnp.int32),
        vmem((W, 4 * W), BF16),
        vmem((W, W), BF16),
        vmem((HIST, R, W), BF16),
        vmem((HIST, R, W), BF16),
        vmem((R, W), F32),
        vmem((R, 4 * W), F32),
        vmem((R, W), BF16),
        vmem((HIST, R, W), BF16),
        vmem((HIST, R, W), BF16),
        vmem((HIST, R, W), BF16),
        vmem((HEADS, R, L), F32),
        vmem((HEADS, R, L), F32),
        vmem((HEADS, R, L), BF16),
        vmem((R, W), BF16),
        vmem((2, chunks, ring, zh, NH, 256), BF16),
        vmem((nz, 8, 128), jnp.int32),
        vmem((ring, 16, 128), jnp.int32),
        vmem((nyh, 16, 128), jnp.int32),
        vmem((chunks, span, 128), F32),
        vmem((chunks, span, 128), F32),
        vmem((chunks, span, 128), F32),
        vmem((chunks, span, 128), BF16),
        vmem((2, chunks, span // 2, 128), BF16),
        vmem((chunks, span // 2, 128), BF16),
        vmem((R, 2 * W), BF16),
        vmem((R, 2 * W), BF16),
        vmem((HIST, R, W), BF16),
        vmem((2, 2, R, 384), BF16),
        vmem((2, R, 384), BF16),
        vmem((2, 2, R, 256), BF16),
        vmem((2, R, 256), BF16),
        vmem((R, 4 * W), BF16),
        vmem((R, W), F32),
        group(NQ, 256, True),
        (
            vmem((nz, ring, ring * NQ, 256), BF16),
            vmem((nz, ring, ring * NQ, 256), BF16),
            vmem((ring, ring * NQ, 256), BF16),
            vmem((ring, ring * NQ, 256), BF16),
            vmem((ring, 2 * NQ, 128), BF16),
            vmem((ring, 2 * NQ, 128), BF16),
            vmem((HIST, NQ, 256), F32),
        ),
        group(rw, 384, False),
        group(rw, 256, True),
        vmem((ring, 8, 128), F32),
        vmem((ring, 8, 128), F32),
        vmem((nz, 8, 128), F32),
        vmem((2, 8, 128), F32),
        pltpu.SemaphoreType.DMA((9,)),
        pltpu.SemaphoreType.DMA((6,)),
        pltpu.SemaphoreType.DMA((count,)),
        pltpu.SemaphoreType.DMA((count,)),
    ]
    shape = jax.ShapeDtypeStruct
    shapes = [
        shape((1, 1), F32),
        shape((R, W), BF16),
        shape((R, W), BF16),
        shape((rw, 4 * W), F32),
        shape((rw, W), F32),
        shape((NB, W), F32),
    ]
    outs = pl.pallas_call(
        functools.partial(kernel, sizes, count),
        out_shape=shapes,
        in_specs=[pl.BlockSpec(memory_space=pltpu.HBM)] * 9,
        out_specs=[pl.BlockSpec(memory_space=pltpu.HBM)] * 6,
        scratch_shapes=scratch,
        compiler_params=pltpu.CompilerParams(
            collective_id=0, has_side_effects=True, vmem_limit_bytes=VMEM_LIMIT
        ),
    )(
        tokens.reshape(R, W),
        targets.reshape(R, W),
        target_ids,
        lengths,
        negatives,
        negative_ids.reshape(1, NB),
        counts.reshape(1, NB),
        w_in,
        w_out,
    )
    outs = pl.pallas_call(
        hand_over,
        out_shape=shapes,
        in_specs=[pl.BlockSpec(memory_space=pl.ANY)] * 6,
        out_specs=[pl.BlockSpec(memory_space=pl.ANY)] * 6,
        scratch_shapes=[vmem(item.shape, item.dtype) for item in shapes]
        + [pltpu.SemaphoreType.DMA((12,))],
        compiler_params=pltpu.CompilerParams(vmem_limit_bytes=VMEM_LIMIT),
    )(*outs)
    return (
        outs[0].reshape(()),
        outs[1].reshape(1, R, W),
        outs[2].reshape(1, R, W),
        outs[3],
        outs[4],
        outs[5],
    )


def solution(mesh):
    in_specs = (
        P("dp", "hist", None),
        P("dp", "hist", None),
        P("dp", "hist"),
        P("dp"),
        P("dp", None),
        P("dp"),
        P("dp"),
        P(),
        P(),
    )
    out_specs = (
        P(),
        P("dp", "hist", None),
        P("dp", "hist", None),
        P("dp", None),
        P("dp", None),
        P("dp", None),
    )
    return jax.shard_map(
        functools.partial(local, plan(mesh)),
        mesh=mesh,
        in_specs=in_specs,
        out_specs=out_specs,
        check_vma=False,
    )
```

```python
import functools

import jax
import jax.numpy as jnp
from jax import lax
from jax.experimental import pallas as pl
from jax.experimental.pallas import tpu as pltpu
from jax.sharding import PartitionSpec as P

HEADS = 8
L = 512
W = 512
HIST = 4
R = 128
NB = 32
NQ = NB // HIST
NH = NB // 2
TEMP = 0.05
MESH = pl.DeviceIdType.MESH
VMEM_LIMIT = 64 * 1024 * 1024
F32 = jnp.float32
BF16 = jnp.bfloat16


def layer_norm(values):
    centered = values - jnp.mean(values, -1, keepdims=True)
    inverse = lax.rsqrt(jnp.mean(centered * centered, -1, keepdims=True) + 1e-06)
    return (centered * inverse, inverse)


def norm_back(grad, normed, inverse):
    return inverse * (
        grad
        - jnp.mean(grad, -1, keepdims=True)
        - normed * jnp.mean(grad * normed, -1, keepdims=True)
    )


def unit_rows(values):
    inverse = lax.rsqrt(jnp.sum(values * values, -1, keepdims=True) + 1e-06)
    return (values * inverse, inverse)


def unit_back(grad, unit, inverse):
    return inverse * (grad - unit * jnp.sum(unit * grad, -1, keepdims=True))


def sigmoid(values):
    return 0.5 * jnp.tanh(0.5 * values) + 0.5


def silu_slope(values):
    sigma = sigmoid(values)
    return sigma * (1.0 + values * (1.0 - sigma))


def silu(values):
    return values * sigmoid(values)


def inner_product(left, right):
    return lax.dot_general(left, right, (((1,), (1,)), ((), ())), preferred_element_type=F32)


def matmul(left, right):
    return jnp.dot(left, right, preferred_element_type=F32)


def plan(mesh):
    dp = mesh.shape["dp"]
    if dp == 64:
        return 8, 2, 4
    return dp // 2, 1, 2


def kernel(
    sizes,
    count,
    tok_hbm,
    tgt_hbm,
    tid_hbm,
    len_hbm,
    neg_hbm,
    nid_hbm,
    ncnt_hbm,
    win_hbm,
    wout_hbm,
    loss_hbm,
    dtok_hbm,
    dtgt_hbm,
    dwin_hbm,
    dwout_hbm,
    dneg_hbm,
    loss_ref,
    dtok_ref,
    dtgt_ref,
    dwin_ref,
    dwout_ref,
    dneg_ref,
    tok_ref,
    tgt_ref,
    tid_ref,
    len_ref,
    neg_ref,
    nid_ref,
    ncnt_ref,
    win_ref,
    wout_ref,
    tok_all,
    nrm_all,
    nrmf,
    proj,
    gate,
    k_all,
    v_all,
    q_all,
    slope,
    slope_t,
    weights_t,
    attn,
    nall,
    idz,
    idx,
    idy,
    idb,
    lcb,
    ex,
    ngo,
    ngs,
    nga,
    my_own,
    my_sib,
    da_all,
    dpq,
    dpq_r,
    dpk,
    dpk_r,
    dpo,
    dout,
    g1,
    gz,
    g2,
    g3,
    l1,
    l2,
    l3,
    l4,
    lsem,
    osem,
    ssem,
    rsem,
):
    nz, nyh, nx = sizes
    npl = nyh * nx
    ring = nx
    chunks = 2 * ring
    zh = nz // 2
    dp_size = nz * npl
    rw = W // dp_size
    total_events = float(dp_size * L)
    d = lax.axis_index("dp")
    h = lax.axis_index("hist")
    z = lax.div(d, npl)
    p = lax.rem(d, npl)
    yh = lax.div(p, nx)
    x = lax.rem(p, nx)
    yl = lax.div(h, 2)
    y = yh * 2 + yl
    core = lax.rem(h, 2)
    other = 1 - core
    sib = yl * 2 + other
    partner = (1 - yl) * 2 + core
    cross = (1 - yl) * 2 + other

    def hist_to(o):
        return lax.rem(h + o, HIST)

    def hist_from(o):
        return lax.rem(h + HIST - o, HIST)

    def z_to(o):
        return lax.rem(z + o, nz)

    def z_from(o):
        return lax.rem(z + nz - o, nz)

    def x_to(o):
        return lax.rem(x + o, ring)

    def x_from(o):
        return lax.rem(x + ring - o, ring)

    def y_to(o):
        return lax.rem(y + o, ring)

    def y_from(o):
        return lax.rem(y + ring - o, ring)

    def hist_dev(index):
        return {"dp": d, "hist": index}

    def z_dev(index):
        return {"dp": index * npl + p, "hist": h}

    def x_dev(index):
        return {"dp": z * npl + yh * nx + index, "hist": h}

    def y_dev(index):
        return {
            "dp": z * npl + lax.div(index, 2) * nx + x,
            "hist": lax.rem(index, 2) * 2 + core,
        }

    sends = []
    taken = [0]

    def slots(number):
        base = taken[0]
        taken[0] += number
        assert taken[0] <= count
        return base

    def send(src, dst, slot, device):
        copy = pltpu.make_async_remote_copy(
            src_ref=src,
            dst_ref=dst,
            send_sem=ssem.at[slot],
            recv_sem=rsem.at[slot],
            device_id=device,
            device_id_type=MESH,
        )
        copy.start()
        sends.append(copy)

    def recv(dst, slot):
        pltpu.make_async_remote_copy(
            src_ref=dst,
            dst_ref=dst,
            send_sem=ssem.at[slot],
            recv_sem=rsem.at[slot],
            device_id=hist_dev(sib),
            device_id_type=MESH,
        ).wait_recv()

    stores = []

    def store(src, dst):
        copy = pltpu.make_async_copy(src, dst, osem.at[len(stores)])
        copy.start()
        stores.append(copy)

    barrier = pltpu.get_barrier_semaphore()
    peers = (
        [hist_dev(hist_to(o)) for o in range(1, HIST)]
        + [x_dev(x_to(o)) for o in range(1, ring)]
        + [z_dev(z_to(o)) for o in range(1, nz)]
    )
    if nyh > 1:
        peers += [y_dev(lax.rem(yh + 1, nyh) * 2 + k) for k in range(2)]
    for device in peers:
        pl.semaphore_signal(barrier, inc=1, device_id=device, device_id_type=MESH)

    loads = []
    for k, (src, dst) in enumerate(
        (
            (neg_hbm, neg_ref),
            (nid_hbm, nid_ref),
            (ncnt_hbm, ncnt_ref),
            (tok_hbm, tok_ref),
            (win_hbm, win_ref),
            (wout_hbm, wout_ref),
            (tgt_hbm, tgt_ref),
            (tid_hbm, tid_ref),
            (len_hbm, len_ref),
        )
    ):
        copy = pltpu.make_async_copy(src, dst, lsem.at[k])
        copy.start()
        loads.append(copy)

    for k in range(3):
        loads[k].wait()
    n_hat, n_inv = unit_rows(neg_ref[...].astype(F32))
    rows16 = jnp.where(yl == 0, n_hat[:NH], n_hat[NH:])
    own16 = jnp.where(core == 0, rows16[:, :256], rows16[:, 256:]).astype(BF16)
    lane_at = lax.broadcasted_iota(jnp.int32, (1, 128), 1)
    own_lanes = (lane_at >= x * NB) & (lane_at < x * NB + NB)
    wide = [
        jnp.where(own_lanes, jnp.concatenate([ref[...]] * (128 // NB), axis=1), 0)
        for ref in (nid_ref, ncnt_ref)
    ]
    idz[z] = jnp.concatenate(wide + [jnp.zeros((6, 128), jnp.int32)], axis=0)

    pl.semaphore_wait(barrier, len(peers))

    upper = lax.div(z, zh)
    own_chunk = y + upper * (ring + x - y)
    own_place = x + upper * (y - x)
    own_z = lax.rem(z, zh)
    nall[core, own_chunk, own_place, own_z] = own16
    s_nz = slots(nz)
    s_iz = slots(nz)
    own_slot = nall.at[core, own_chunk, own_place, own_z]
    for o in sorted(range(1, nz), key=lambda o: -min(o, nz - o)):
        send(own_slot, own_slot, s_nz + o, z_dev(z_to(o)))
        send(idz.at[z], idz.at[z], s_iz + o, z_dev(z_to(o)))
    s_tok = slots(3)
    send(tok_hbm, tok_all.at[h], s_tok, hist_dev(partner))
    send(tok_hbm, tok_all.at[h], s_tok + 1, hist_dev(sib))

    loads[3].wait()
    loads[4].wait()
    tokf = tok_ref[...].astype(F32)
    normed_f, inverse = layer_norm(tokf)
    nrmf[...] = normed_f
    normed = normed_f.astype(BF16)
    nrm_all[h] = normed
    for blk, ref in enumerate((gate, v_all.at[h], q_all.at[h], k_all.at[h])):
        cols = slice(blk * W, (blk + 1) * W)
        part = matmul(normed, win_ref[:, cols])
        proj[:, cols] = part
        ref[...] = silu(part).astype(BF16)

    for o in range(1, nz):
        src = z_from(o)
        src_upper = lax.div(src, zh)
        recv(
            nall.at[core, y + src_upper * (ring + x - y), x + src_upper * (y - x), lax.rem(src, zh)],
            s_nz + o,
        )
        recv(idz.at[src], s_iz + o)
    idx[x] = jnp.concatenate(
        [idz[k, 0:1] for k in range(nz)]
        + [jnp.zeros((8 - nz, 128), jnp.int32)] * (nz < 8)
        + [idz[k, 1:2] for k in range(nz)]
        + [jnp.zeros((8 - nz, 128), jnp.int32)] * (nz < 8),
        axis=0,
    )
    s_n2x = slots(ring)
    s_n2y = slots(ring)
    s_ix = slots(ring)
    for o in range(1, ring):
        low_half = nall.at[core, y, x]
        high_half = nall.at[core, ring + x, y]
        send(low_half, low_half, s_n2x + o, x_dev(x_to(o)))
        send(high_half, high_half, s_n2y + o, y_dev(y_to(o)))
        send(idx.at[x], idx.at[x], s_ix + o, x_dev(x_to(o)))

    def keys_values(b):
        normed_b = layer_norm(tok_all[b].astype(F32))[0].astype(BF16)
        nrm_all[b] = normed_b
        v_all[b] = silu(matmul(normed_b, win_ref[:, W : 2 * W])).astype(BF16)
        k_all[b] = silu(matmul(normed_b, win_ref[:, 3 * W :])).astype(BF16)

    recv(tok_all.at[partner], s_tok)
    send(tok_all.at[partner], tok_all.at[partner], s_tok + 2, hist_dev(sib))
    recv(tok_all.at[sib], s_tok + 1)
    keys_values(sib)
    keys_values(partner)

    for o in range(1, ring):
        recv(nall.at[core, y, x_from(o)], s_n2x + o)
        recv(nall.at[core, ring + x, y_from(o)], s_n2y + o)
        recv(idx.at[x_from(o)], s_ix + o)
    tile = idx[0]
    for k in range(1, ring):
        tile = tile + idx[k]
    idy[yh] = tile
    s_n3y = slots(ring)
    s_n3x = slots(ring)
    s_iy = slots(1)

    def third_leg(o):
        send(nall.at[core, y], nall.at[core, y], s_n3y + o, y_dev(y_to(o)))
        send(nall.at[core, ring + x], nall.at[core, ring + x], s_n3x + o, x_dev(x_to(o)))

    for o in (1, ring - 1)[: ring - 1]:
        third_leg(o)
    if nyh > 1:
        send(idy.at[yh], idy.at[yh], s_iy, y_dev(lax.rem(yh + 1, nyh) * 2 + yl))
    s_sib = slots(2 * ring)
    for k, own in enumerate((y, ring + x)):
        send(nall.at[core, own], nall.at[core, own], s_sib + k * ring, hist_dev(sib))

    recv(tok_all.at[cross], s_tok + 2)
    keys_values(cross)

    lane = lax.broadcasted_iota(jnp.int32, (1, 128), 1)
    low = lane < 64
    half_mask = [jnp.where(low, 1.0, 0.0).astype(BF16), jnp.where(low, 0.0, 1.0).astype(BF16)]
    causal = lax.broadcasted_iota(jnp.int32, (R, L), 1) <= h * R + lax.broadcasted_iota(
        jnp.int32, (R, L), 0
    )
    scale = 0.125

    def forward_pair(n, carry):
        cols = pl.ds(pl.multiple_of(n * 128, 128), 128)
        q = q_all[h, :, cols]
        k = k_all[:, :, cols].reshape(L, 128)
        v = v_all[:, :, cols].reshape(L, 128)
        halves = []
        for e in range(2):
            s = inner_product(q * half_mask[e], k) * scale
            sigma = sigmoid(s)
            w = jnp.where(causal, s * sigma * (1.0 / L), 0.0).astype(BF16)
            slope[2 * n + e] = jnp.where(
                causal, sigma * (1.0 + s * (1.0 - sigma)) * (scale / L), 0.0
            )
            halves.append(matmul(w, v))
        attn[:, cols] = jnp.where(low, halves[0], halves[1]).astype(BF16)
        return carry

    lax.fori_loop(0, 1, forward_pair, 0)
    for o in range(2, ring - 1):
        third_leg(o)
    lax.fori_loop(1, HEADS // 2, forward_pair, 0)

    for k in range(5, 9):
        loads[k].wait()
    attn_normed, attn_inv = layer_norm(attn[...].astype(F32))
    gate_f = gate[...].astype(F32)
    mixed = (attn_normed * gate_f).astype(BF16)
    my_own[:, :W] = mixed
    output = tok_ref[...].astype(F32) + matmul(mixed, wout_ref[...])
    y_hat, y_inv = unit_rows(output)
    y_hat_b = y_hat.astype(BF16)
    my_own[:, W:] = y_hat_b
    t_hat, t_inv = unit_rows(tgt_ref[...].astype(F32))
    pos_col = jnp.sum(y_hat * t_hat, -1, keepdims=True) / TEMP
    pos_row = jnp.broadcast_to(pos_col, (R, 128)).T[0:1, :]

    if nyh > 1:
        recv(idy.at[lax.rem(yh + 1, nyh)], s_iy)
    for a in range(nyh):
        ids = idy[a, :8].astype(F32)
        logs = jnp.log(jnp.maximum(idy[a, 8:].astype(F32), 1.0))
        turned = jnp.concatenate([ids, logs, jnp.zeros((112, 128), F32)], axis=0).T
        for b in range(nx):
            for c in range(2):
                rows = turned[b * NB + c * NH : b * NB + (c + 1) * NH]
                for k in range(nz):
                    if k < zh:
                        chunk, place = 2 * a + c, b
                    else:
                        chunk, place = ring + b, 2 * a + c
                    at = pl.ds((place * zh + k % zh) * NH, NH)
                    idb[chunk, at] = jnp.broadcast_to(rows[:, k : k + 1], (NH, 128))
                    lcb[chunk, at] = jnp.broadcast_to(rows[:, 8 + k : 9 + k], (NH, 128))

    span = ring * zh * NH
    tid_row = tid_ref[...].astype(F32)

    def hand_on(o):
        for k, (src, base) in enumerate(((y_from(o), s_n3y), (ring + x_from(o), s_n3x))):
            recv(nall.at[core, src], base + o)
            send(nall.at[core, src], nall.at[core, src], s_sib + k * ring + o, hist_dev(sib))

    def logits(o, acc):
        for k, c in enumerate((y_from(o), ring + x_from(o))):
            recv(nall.at[other, c], s_sib + k * ring + o)
            lg = inner_product(nall[0, c].reshape(span, 256), y_hat_b[:, :256]) + inner_product(
                nall[1, c].reshape(span, 256), y_hat_b[:, 256:]
            )
            lg = lg * (1.0 / TEMP) - lcb[c]
            value = jnp.where(idb[c] != tid_row, jnp.exp(lg), 0.0)
            ex[c] = value
            acc = acc + jnp.sum(value.reshape(span // 8, 8, 128), 0)
        return acc

    order = [0, 1, 3, 2] if ring == 4 else list(range(ring))
    acc = jnp.zeros((8, 128), F32)
    for k in range(1, ring):
        hand_on(order[k])
        acc = logits(order[k - 1], acc)
    s_my = slots(1)
    send(my_own, my_sib, s_my, hist_dev(sib))
    acc = logits(order[-1], acc)
    total = jnp.exp(pos_row) + jnp.sum(acc, 0, keepdims=True)
    position = h * R + lax.broadcasted_iota(jnp.int32, (1, 128), 1)
    valid = jnp.where(position < len_ref[0], 1.0, 0.0)
    pg_row = valid * (jnp.exp(pos_row) / total - 1.0) / TEMP
    pg = jnp.broadcast_to(pg_row, (128, 128)).T[:, 0:1]
    scale_row = valid / (total * TEMP)

    def grad_chunk(c, carry):
        g = ex[c] * scale_row
        ngo[c] = g.astype(BF16)
        g4 = g.reshape(span // NH, 2, NQ, 128)
        for q in range(2):
            ngs[q, c] = g4[:, q].reshape(span // 2, 128).astype(BF16)
        return carry

    lax.fori_loop(0, chunks, grad_chunk, 0)
    s_ng = slots(1)
    send(ngs.at[other], nga, s_ng, hist_dev(sib))
    ng = ngo[...].reshape(dp_size * NB, 128).T
    d_hat = pg * t_hat + jnp.concatenate(
        [matmul(ng, nall[c].reshape(dp_size * NB, 256)) for c in range(2)], axis=1
    )
    d_out = unit_back(d_hat, y_hat, y_inv)
    d_out_b = d_out.astype(BF16)
    d_mixed = inner_product(d_out_b, wout_ref[...])
    da_all[h] = norm_back(d_mixed * gate_f, attn_normed, attn_inv).astype(BF16)
    s_da = slots(3)
    send(da_all.at[h], da_all.at[h], s_da, hist_dev(partner))
    send(da_all.at[h], da_all.at[h], s_da + 1, hist_dev(sib))

    def leg1(group):
        src, arrived = group[0], group[1]
        base = slots(2 * ring)
        for o in sorted(range(1, ring), key=lambda o: -min(o, ring - o)):
            send(src.at[y_to(o)], arrived.at[0, o], base + o, y_dev(y_to(o)))
            send(src.at[ring + x_to(o)], arrived.at[1, o], base + ring + o, x_dev(x_to(o)))
        return base

    def leg2(group, base):
        src, arrived, mid, arrived2 = group[:4]
        out = slots(2 * ring)
        for part, own in enumerate((y, ring + x)):
            total = src[own].astype(F32)
            for o in range(1, ring):
                recv(arrived.at[part, o], base + part * ring + o)
                total = total + arrived[part, o].astype(F32)
            mid[part] = total.astype(BF16).reshape(mid.shape[1:])
            for o in range(1, ring):
                to, device = (x_to(o), x_dev(x_to(o))) if part == 0 else (y_to(o), y_dev(y_to(o)))
                send(mid.at[part, to], arrived2.at[part, o], out + part * ring + o, device)
        return out

    def leg3(group, base):
        mid, arrived2, zs, zr = group[2:6]
        for part, own in enumerate((x, y)):
            total = mid[part, own].astype(F32)
            for o in range(1, ring):
                recv(arrived2.at[part, o], base + part * ring + o)
                total = total + arrived2[part, o].astype(F32)
            total = total.reshape((zh, total.shape[0] // zh, total.shape[1]))
            if zs.dtype == BF16:
                half = total.shape[2] // 2
                total = jnp.concatenate([total[:, :, :half], total[:, :, half:]], axis=1).astype(BF16)
            zs[part * zh : (part + 1) * zh] = total
        out = slots(nz)
        for o in sorted(range(1, nz), key=lambda o: -min(o, nz - o)):
            send(zs.at[z_to(o)], zr.at[o], out + o, z_dev(z_to(o)))
        return out

    def leg4(group, base):
        zs, zr, eh = group[4:]
        total = zs[z].astype(F32)
        for o in range(1, nz):
            recv(zr.at[o], base + o)
            total = total + zr[o].astype(F32)
        if zs.dtype == BF16:
            rows = total.shape[0] // 2
            total = jnp.concatenate([total[:rows], total[rows:]], axis=1)
        eh[h] = total
        out = slots(HIST)
        for o in range(1, HIST):
            send(eh.at[h], eh.at[h], out + o, hist_dev(hist_to(o)))
        return out

    def arrive(group, base):
        for o in range(1, HIST):
            recv(group[6].at[hist_from(o)], base + o)

    def spread(result, k, group, c0):
        width = result.shape[1]
        for a in range(nyh):
            for b in range(nx):
                for half in range(2):
                    block = jnp.concatenate(
                        [
                            result[((half * zh + j) * npl + a * nx + b) * rw :][:rw]
                            for j in range(zh)
                        ],
                        axis=0,
                    ).astype(BF16)
                    chunk, place = (2 * a + k, b) if half == 0 else (ring + b, 2 * a + k)
                    group[0][chunk, place * zh * rw : (place + 1) * zh * rw, c0 : c0 + width] = block

    for o in range(1, HIST):
        b = hist_from(o)
        q_all[b] = silu(matmul(nrm_all[b], win_ref[:, 2 * W : 3 * W])).astype(BF16)

    recv(my_sib, s_my)
    recv(nga, s_ng)

    right = jnp.concatenate([my_own[:, W:], my_sib[:, W:]], axis=0)
    zsrc, zgot, amid, agot, bmid, bgot, ez = gz

    def neg_chunk(c, part, index):
        left = jnp.concatenate([ngs[core, c], nga[c]], axis=1)
        result = matmul(left, right)
        g1[0][c] = result[:, :256].astype(BF16)
        for j in range(zh):
            block = jnp.concatenate(
                [result[(k * zh + j) * NQ : (k * zh + j + 1) * NQ, 256:] for k in range(ring)], axis=0
            )
            zsrc[part * zh + j, index] = block.astype(BF16)

    t1 = slots(2 * ring)
    for o in order[1:] + [0]:
        for part, index in enumerate((y_to(o), x_to(o))):
            c = part * ring + index
            neg_chunk(c, part, index)
            if o:
                device = y_dev(index) if part == 0 else x_dev(index)
                send(g1[0].at[c], g1[1].at[part, o], t1 + part * ring + o, device)
    s_zz = slots(nz)
    for o in sorted(range(1, nz), key=lambda o: -min(o, nz - o)):
        send(zsrc.at[z_to(o)], zgot.at[o], s_zz + o, z_dev(z_to(o)))

    def turn(low_index, high_index):
        return low_index + upper * (high_index - low_index)

    def turn_dev(low_dev, high_dev):
        return {name: turn(low_dev[name], high_dev[name]) for name in ("dp", "hist")}

    def z_first_leg2():
        total = zsrc[z].astype(F32)
        for o in range(1, nz):
            recv(zgot.at[o], s_zz + o)
            total = total + zgot[o].astype(F32)
        amid[...] = total.astype(BF16)
        out = slots(ring)
        for o in range(1, ring):
            to = turn(y_to(o), x_to(o))
            send(amid.at[to], agot.at[o], out + o, turn_dev(y_dev(y_to(o)), x_dev(x_to(o))))
        return out

    def z_first_leg3(base):
        total = amid[turn(y, x)].astype(F32)
        for o in range(1, ring):
            recv(agot.at[o], base + o)
            total = total + agot[o].astype(F32)
        total = total.reshape(ring, NQ, 256)
        bmid[...] = jnp.concatenate([total[:, :, :128], total[:, :, 128:]], axis=1).astype(BF16)
        out = slots(ring)
        for o in range(1, ring):
            to = turn(x_to(o), y_to(o))
            send(bmid.at[to], bgot.at[o], out + o, turn_dev(x_dev(x_to(o)), y_dev(y_to(o))))
        return out

    def z_first_leg4(base):
        total = bmid[turn(x, y)].astype(F32)
        for o in range(1, ring):
            recv(bgot.at[o], base + o)
            total = total + bgot[o].astype(F32)
        ez[h] = jnp.concatenate([total[:NQ], total[NQ:]], axis=1)
        out = slots(HIST)
        for o in range(1, HIST):
            send(ez.at[h], ez.at[h], out + o, hist_dev(hist_to(o)))
        return out


    dout[...] = d_out
    dtgt_ref[...] = unit_back(pg * y_hat, t_hat, t_inv).astype(BF16)
    store(dtgt_ref, dtgt_hbm)
    d_gate = (d_mixed * attn_normed * silu_slope(proj[:, :W])).astype(BF16)
    dpo[:, :W] = d_gate
    for n in range(HIST):
        cols = slice(n * 128, (n + 1) * 128)
        dpq[n % 2, n // 2, :, 0:128] = d_out_b[:, cols]
        dpq[n % 2, n // 2, :, 128:256] = d_gate[:, cols]

    loss = jnp.sum(valid * (jnp.log(total) - pos_row), -1, keepdims=True)
    l1[x] = jnp.broadcast_to(loss, (8, 128))
    s_l1 = slots(ring)
    for o in range(1, ring):
        send(l1.at[x], l1.at[x], s_l1 + o, x_dev(x_to(o)))

    def query_pair(n, carry):
        cols = pl.ds(pl.multiple_of(n * 128, 128), 128)
        da = da_all[h, :, cols]
        k = k_all[:, :, cols].reshape(L, 128)
        v = v_all[:, :, cols].reshape(L, 128)
        halves = []
        for e in range(2):
            dw = inner_product(da * half_mask[e], v)
            halves.append(matmul((dw * slope[2 * n + e]).astype(BF16), k))
        dq = jnp.where(low, halves[0], halves[1]).astype(BF16).astype(F32)
        at = pl.ds(pl.multiple_of(2 * W + n * 128, 128), 128)
        piece = (dq * silu_slope(proj[:, at])).astype(BF16)
        dpo[:, at] = piece
        dpq[lax.rem(n, 2), lax.div(n, 2), :, 256:384] = piece
        return carry

    lax.fori_loop(0, HEADS // 2, query_pair, 0)
    s_dq = slots(1)
    send(dpq.at[other], dpq_r, s_dq, hist_dev(sib))

    mixed_t = jnp.concatenate([my_own[:, :W], my_sib[:, :W]], axis=0).T
    normed_t = jnp.concatenate([nrm_all[h], nrm_all[sib]], axis=0).T
    causal_t = lax.broadcasted_iota(jnp.int32, (R, L), 1) >= h * R + lax.broadcasted_iota(
        jnp.int32, (R, L), 0
    )

    def key_prepare(n, carry):
        cols = pl.ds(pl.multiple_of(n * 128, 128), 128)
        k = k_all[h, :, cols]
        q = q_all[:, :, cols].reshape(L, 128)
        for e in range(2):
            s = inner_product(k * half_mask[e], q) * scale
            sigma = sigmoid(s)
            weights_t[2 * n + e] = jnp.where(causal_t, s * sigma * (1.0 / L), 0.0).astype(BF16)
            slope_t[2 * n + e] = jnp.where(
                causal_t, sigma * (1.0 + s * (1.0 - sigma)) * (scale / L), 0.0
            )
        for first in (W, 3 * W):
            at = pl.ds(pl.multiple_of(first + n * 128, 128), 128)
            proj[:, at] = silu_slope(proj[:, at])
        return carry

    lax.fori_loop(0, HEADS // 2, key_prepare, 0)
    recv(da_all.at[partner], s_da)
    send(da_all.at[partner], da_all.at[partner], s_da + 2, hist_dev(sib))
    recv(dpq_r, s_dq)
    for k in range(2):
        right = jnp.concatenate([dpq[core, k], dpq_r[k]], axis=0)
        spread(matmul(mixed_t, right[:, :128]), k, g2, 0)
        spread(matmul(normed_t, right[:, 128:]), k, g2, 128)
    t2 = leg1(g2)


    for o in range(1, ring):
        recv(l1.at[x_from(o)], s_l1 + o)
    part = l1[0]
    for k in range(1, ring):
        part = part + l1[k]
    l2[y] = part
    s_l2 = slots(ring)
    for o in range(1, ring):
        send(l2.at[y], l2.at[y], s_l2 + o, y_dev(y_to(o)))

    recv(da_all.at[sib], s_da + 1)
    recv(da_all.at[cross], s_da + 2)
    def key_pair(n, carry):
        cols = pl.ds(pl.multiple_of(n * 128, 128), 128)
        v = v_all[h, :, cols]
        q = q_all[:, :, cols].reshape(L, 128)
        da = da_all[:, :, cols].reshape(L, 128)
        dks, dvs = [], []
        for e in range(2):
            dw = inner_product(v * half_mask[e], da)
            dks.append(matmul((dw * slope_t[2 * n + e]).astype(BF16), q))
            dvs.append(matmul(weights_t[2 * n + e], da))
        for at, parts, place in ((W, dvs, 0), (3 * W, dks, 128)):
            grad = jnp.where(low, parts[0], parts[1]).astype(BF16).astype(F32)
            at = pl.ds(pl.multiple_of(at + n * 128, 128), 128)
            piece = (grad * proj[:, at]).astype(BF16)
            dpo[:, at] = piece
            dpk[lax.rem(n, 2), lax.div(n, 2), :, place : place + 128] = piece
        return carry

    lax.fori_loop(0, HEADS // 2, key_pair, 0)
    s_dk = slots(1)
    send(dpk.at[other], dpk_r, s_dk, hist_dev(sib))

    recv(dpk_r, s_dk)
    for k in range(2):
        right = jnp.concatenate([dpk[core, k], dpk_r[k]], axis=0)
        spread(matmul(normed_t, right), k, g3, 0)
    t3 = leg1(g3)
    t1 = leg2(g1, t1)
    t2 = leg2(g2, t2)
    for o in range(1, ring):
        recv(l2.at[y_from(o)], s_l2 + o)
    part = l2[0]
    for k in range(1, ring):
        part = part + l2[k]
    l3[z] = part
    s_l3 = slots(nz)
    for o in range(1, nz):
        send(l3.at[z], l3.at[z], s_l3 + o, z_dev(z_to(o)))

    t3 = leg2(g3, t3)
    tz = z_first_leg2()
    t1 = leg3(g1, t1)
    t2 = leg3(g2, t2)
    grad = inner_product(dpo[...], win_ref[...])
    dtok_ref[...] = (dout[...] + norm_back(grad, nrmf[...], inverse)).astype(BF16)
    store(dtok_ref, dtok_hbm)
    t3 = leg3(g3, t3)
    tz = z_first_leg3(tz)
    for o in range(1, nz):
        recv(l3.at[z_from(o)], s_l3 + o)
    part = l3[0]
    for k in range(1, nz):
        part = part + l3[k]
    l4[core] = part
    s_l4 = slots(1)
    send(l4.at[core], l4.at[core], s_l4, hist_dev(sib))
    t1 = leg4(g1, t1)
    t2 = leg4(g2, t2)
    tz = z_first_leg4(tz)
    t3 = leg4(g3, t3)
    recv(l4.at[other], s_l4)
    loss_ref[...] = (l4[0] + l4[1])[0:1, 0:1] / total_events
    store(loss_ref, loss_hbm)
    arrive(g1, t1)
    for o in range(1, HIST):
        recv(ez.at[hist_from(o)], tz + o)
    d_nhat = jnp.concatenate([g1[6][...].reshape(NB, 256), ez[...].reshape(NB, 256)], axis=1)
    dneg_ref[...] = unit_back(d_nhat, n_hat, n_inv) / total_events
    store(dneg_ref, dneg_hbm)
    arrive(g2, t2)
    for k in range(HIST):
        cols = slice(k * 128, (k + 1) * 128)
        dwout_ref[:, cols] = g2[6][k, :, 0:128] / total_events
        dwin_ref[:, cols] = g2[6][k, :, 128:256] / total_events
        dwin_ref[:, 2 * W + k * 128 : 2 * W + (k + 1) * 128] = g2[6][k, :, 256:384] / total_events
    store(dwout_ref, dwout_hbm)
    for copy in sends:
        copy.wait_send()
    sends.clear()
    arrive(g3, t3)
    for k in range(HIST):
        dwin_ref[:, W + k * 128 : W + (k + 1) * 128] = g3[6][k, :, 0:128] / total_events
        dwin_ref[:, 3 * W + k * 128 : 3 * W + (k + 1) * 128] = g3[6][k, :, 128:256] / total_events
    store(dwin_ref, dwin_hbm)
    for copy in sends:
        copy.wait_send()
    for copy in stores:
        copy.wait()


def hand_over(*refs):
    sources, results, staged, sems = refs[:6], refs[6:12], refs[12:18], refs[18]
    loads = [pltpu.make_async_copy(sources[k], staged[k], sems.at[k]) for k in range(6)]
    stores = [pltpu.make_async_copy(staged[k], results[k], sems.at[6 + k]) for k in range(6)]
    for copy in loads:
        copy.start()
    for load, copy in zip(loads, stores):
        load.wait()
        copy.start()
    for copy in stores:
        copy.wait()


def local(sizes, *args):
    tokens, targets, target_ids, lengths, negatives, negative_ids, counts, w_in, w_out = args
    nz, nyh, nx = sizes
    npl = nyh * nx
    dp_size = nz * npl
    rw = W // dp_size
    ring = nx
    assert ring == 2 * nyh
    zh = nz // 2
    chunks = 2 * ring
    span = ring * zh * NH
    vmem = pltpu.VMEM
    count = 256

    def group(rows, width, narrow):
        block = ring * zh * rows
        over_z = vmem((nz, 2 * rows, width // 2), BF16) if narrow else vmem((nz, rows, width), F32)
        return (
            vmem((chunks, block, width), BF16),
            vmem((2, ring, block, width), BF16),
            vmem((2, ring, zh * rows, width), BF16),
            vmem((2, ring, zh * rows, width), BF16),
            over_z,
            over_z,
            vmem((HIST, rows, width), F32),
        )

    scratch = [
        vmem((1, 1), F32),
        vmem((R, W), BF16),
        vmem((R, W), BF16),
        vmem((rw, 4 * W), F32),
        vmem((rw, W), F32),
        vmem((NB, W), F32),
        vmem((R, W), BF16),
        vmem((R, W), BF16),
        vmem((1, R), jnp.int32),
        pltpu.SMEM((1,), jnp.int32),
        vmem((NB, W), BF16),
        vmem((1, NB), jnp.int32),
        vmem((1, NB), jnp.int32),
        vmem((W, 4 * W), BF16),
        vmem((W, W), BF16),
        vmem((HIST, R, W), BF16),
        vmem((HIST, R, W), BF16),
        vmem((R, W), F32),
        vmem((R, 4 * W), F32),
        vmem((R, W), BF16),
        vmem((HIST, R, W), BF16),
        vmem((HIST, R, W), BF16),
        vmem((HIST, R, W), BF16),
        vmem((HEADS, R, L), F32),
        vmem((HEADS, R, L), F32),
        vmem((HEADS, R, L), BF16),
        vmem((R, W), BF16),
        vmem((2, chunks, ring, zh, NH, 256), BF16),
        vmem((nz, 8, 128), jnp.int32),
        vmem((ring, 16, 128), jnp.int32),
        vmem((nyh, 16, 128), jnp.int32),
        vmem((chunks, span, 128), F32),
        vmem((chunks, span, 128), F32),
        vmem((chunks, span, 128), F32),
        vmem((chunks, span, 128), BF16),
        vmem((2, chunks, span // 2, 128), BF16),
        vmem((chunks, span // 2, 128), BF16),
        vmem((R, 2 * W), BF16),
        vmem((R, 2 * W), BF16),
        vmem((HIST, R, W), BF16),
        vmem((2, 2, R, 384), BF16),
        vmem((2, R, 384), BF16),
        vmem((2, 2, R, 256), BF16),
        vmem((2, R, 256), BF16),
        vmem((R, 4 * W), BF16),
        vmem((R, W), F32),
        group(NQ, 256, True),
        (
            vmem((nz, ring, ring * NQ, 256), BF16),
            vmem((nz, ring, ring * NQ, 256), BF16),
            vmem((ring, ring * NQ, 256), BF16),
            vmem((ring, ring * NQ, 256), BF16),
            vmem((ring, 2 * NQ, 128), BF16),
            vmem((ring, 2 * NQ, 128), BF16),
            vmem((HIST, NQ, 256), F32),
        ),
        group(rw, 384, False),
        group(rw, 256, True),
        vmem((ring, 8, 128), F32),
        vmem((ring, 8, 128), F32),
        vmem((nz, 8, 128), F32),
        vmem((2, 8, 128), F32),
        pltpu.SemaphoreType.DMA((9,)),
        pltpu.SemaphoreType.DMA((6,)),
        pltpu.SemaphoreType.DMA((count,)),
        pltpu.SemaphoreType.DMA((count,)),
    ]
    shape = jax.ShapeDtypeStruct
    shapes = [
        shape((1, 1), F32),
        shape((R, W), BF16),
        shape((R, W), BF16),
        shape((rw, 4 * W), F32),
        shape((rw, W), F32),
        shape((NB, W), F32),
    ]
    outs = pl.pallas_call(
        functools.partial(kernel, sizes, count),
        out_shape=shapes,
        in_specs=[pl.BlockSpec(memory_space=pltpu.HBM)] * 9,
        out_specs=[pl.BlockSpec(memory_space=pltpu.HBM)] * 6,
        scratch_shapes=scratch,
        compiler_params=pltpu.CompilerParams(
            collective_id=0, has_side_effects=True, vmem_limit_bytes=VMEM_LIMIT
        ),
    )(
        tokens.reshape(R, W),
        targets.reshape(R, W),
        target_ids,
        lengths,
        negatives,
        negative_ids.reshape(1, NB),
        counts.reshape(1, NB),
        w_in,
        w_out,
    )
    outs = pl.pallas_call(
        hand_over,
        out_shape=shapes,
        in_specs=[pl.BlockSpec(memory_space=pl.ANY)] * 6,
        out_specs=[pl.BlockSpec(memory_space=pl.ANY)] * 6,
        scratch_shapes=[vmem(item.shape, item.dtype) for item in shapes]
        + [pltpu.SemaphoreType.DMA((12,))],
        compiler_params=pltpu.CompilerParams(vmem_limit_bytes=VMEM_LIMIT),
    )(*outs)
    return (
        outs[0].reshape(()),
        outs[1].reshape(1, R, W),
        outs[2].reshape(1, R, W),
        outs[3],
        outs[4],
        outs[5],
    )


def solution(mesh):
    in_specs = (
        P("dp", "hist", None),
        P("dp", "hist", None),
        P("dp", "hist"),
        P("dp"),
        P("dp", None),
        P("dp"),
        P("dp"),
        P(),
        P(),
    )
    out_specs = (
        P(),
        P("dp", "hist", None),
        P("dp", "hist", None),
        P("dp", None),
        P("dp", None),
        P("dp", None),
    )
    return jax.shard_map(
        functools.partial(local, plan(mesh)),
        mesh=mesh,
        in_specs=in_specs,
        out_specs=out_specs,
        check_vma=False,
    )
```
